32 devices in a mesh: section: 4 (over y, x), expert: 8 (over z, core).
Axes of the slice: x: 2, y: 2, z: 4, core: 2. Of those that a mesh axis runs over, the one named last changes fastest.
Arguments:
- saved_input: bfloat16 [4, 1024, 2048], P('section', 'expert'), may hold values from -6 to 6
- upstream: bfloat16 [4, 1024, 2048], P('section', 'expert'), may hold values from -6 to 6
- norm_gain: float32 [4, 2048], P('section'), may hold values from 0.1 to 1.9
- gate_weight: bfloat16 [4, 8, 2048, 768], P('section', 'expert'), may hold values from -0.125 to 0.125
- up_weight: bfloat16 [4, 8, 2048, 768], P('section', 'expert'), may hold values from -0.125 to 0.125
- down_weight: bfloat16 [4, 8, 768, 2048], P('section', 'expert'), may hold values from -0.21875 to 0.21875
- expert_ids: int32 [4, 1024, 4], P('section', 'expert'), may hold values from 0 to 7, all different within a row; in each aligned block of 128 rows (0 to 127, 128 to 255, ..., all dimensions but the last counted through in order) at most 96 rows name the same one
- gate_share: float32 [4, 1024, 4], P('section', 'expert'), may hold values from 0.05 to 1
Outputs:
- passed_grad: bfloat16 [4, 1024, 2048], P('section', 'expert')
The draws below stay inside these ranges and needn't reach their ends.
Inputs may be any that keep to these rules, and one draw needn't show every extreme that they name: `expert_ids`: among the 128 tokens of one index of expert in one layer, every expert is named by at most 96 of the pairs (token, k), a bound that some block reaches; a token names 4 different experts.
All inputs are finite; a program needn't handle non-finite values.
Results may differ from the reference program's by a relative error of at most 0.0063.
Values may be sent and summed in bfloat16 or wider, within the bound.
No kernel may reach another device: no remote copies, remote signals or barrier semaphores. Data moves between devices by JAX's collectives and lax.ppermute only.
A program may use at most 128 MiB of HBM per device.

```python
import math
import jax
import jax.numpy as jnp
import numpy as np
from jax import lax

D = 2048
FF = 768
TOPK = 4
TOK_DEV = 128
EXPERTS = 8
CAP = 96
TOKENS = 1024
N_SECTION = 4
N_EXPERT = 8


def steps_of(key, shape, pieces, least, high):
    def one(dim, blocks):
        draws = jax.random.uniform(jax.random.fold_in(jax.random.fold_in(key, 6), dim), (blocks,), jnp.float32, least / len(pieces), high / len(pieces))
        return jnp.repeat(jnp.exp(draws), shape[dim] // blocks).reshape((-1,) + (1,) * (len(shape) - dim - 1))

    factor_of = one(*pieces[0])
    for cut in pieces[1:]:
        factor_of = factor_of * one(*cut)
    return factor_of


def deal_out(key, own, number, rows, number_of, top, bound, slope):
    order = jax.random.permutation(key, number_of)
    crowded, ordinary = load_shares(number_of, rows * top, bound, slope, True), load_shares(number_of, rows * top, bound, slope, False)
    places = jnp.arange(number_of)

    def named(tallies, rotation):
        used = int((tallies > 0).sum())
        fixed = max(1, used // 4)
        shifted = fixed + (places - fixed + rotation * (used - fixed)) % max(1, number_of - fixed)
        return jnp.zeros((number_of,), jnp.int32).at[order[jnp.where(places < fixed, places, shifted)]].set(jnp.asarray(tallies, jnp.int32))

    tallies = jnp.where(number % 4 == 0, named(crowded, number // 4), named(ordinary, number - number // 4 - 1))
    mixed = jax.random.permutation(jax.random.fold_in(own, 3), number_of)
    source_of, taker = mixed[0:number_of // 2 * 2:2], mixed[1:number_of // 2 * 2:2]
    margin = jnp.minimum(tallies[source_of] - 1, bound - tallies[taker]) // 2
    margin = jnp.where((source_of == order[0]) | (taker == order[0]) | (tallies[taker] == 0), 0, jnp.maximum(margin, 0))
    shifted = jax.random.randint(jax.random.fold_in(own, 4), (number_of // 2,), 0, 1 << 20) % (margin + 1)
    tallies = tallies.at[source_of].add(-shifted).at[taker].add(shifted)
    labels = jnp.searchsorted(jnp.cumsum(tallies), jnp.arange(rows * top), side="right").astype(jnp.int32)
    grid = labels.reshape(top, rows).T
    grid = grid[jax.random.permutation(jax.random.fold_in(own, 1), rows)]
    rotation = jax.random.randint(jax.random.fold_in(own, 2), (rows, 1), 0, top)
    return jnp.take_along_axis(grid, (jnp.arange(top)[None, :] + rotation) % top, axis=1)


def load_shares(count, total, most, slope, full):
    weights = [(1 << 20) // math.isqrt(rank ** slope) + 1 for rank in range(1, count + 1)]
    largest = most if full else min(most, max(-(-total // count), total * weights[0] // sum(weights)))
    least = 1 if total - largest >= count - 1 else 0
    holding, spare = [largest] + [least] * (count - 1), total - largest - least * (count - 1)
    while spare > 0:
        candidates = [i for i in range(1, count) if holding[i] < largest] or [i for i in range(1, count) if holding[i] < most]
        whole, remaining = sum([weights[i] for i in candidates]), spare
        for i in candidates:
            more = min(most - holding[i], max(1, remaining * weights[i] // whole), spare)
            holding[i] = holding[i] + more
            spare = spare - more
    return np.array(holding)


def bell_draw(stream_key, shape, scale, limit, pieces=(), kind=jnp.bfloat16):
    factor_of = steps_of(stream_key, shape, pieces, -0.22, 0.18) if pieces else 1.0
    result = jax.random.normal(stream_key, shape, jnp.float32) * scale * factor_of
    return jnp.minimum(jnp.maximum(result, -limit), limit).astype(kind)


def setup_inputs(seed: int = 0) -> dict:
    splits = jax.random.split(jax.random.key(seed), 9)
    saved_input = bell_draw(splits[0], (N_SECTION, TOKENS, D), 1.0, 6.0, ((0, 4), (1, 8)))
    upstream = bell_draw(splits[1], (N_SECTION, TOKENS, D), 1.0, 6.0, ((0, 4), (1, 8)))
    norm_gain = jnp.clip(1.0 + 0.18 * jax.random.normal(splits[2], (N_SECTION, D), jnp.float32), 0.1, 1.9)
    gate_weight = bell_draw(splits[3], (N_SECTION, EXPERTS, D, FF), D ** -0.5, 0.125, ((0, 4), (1, 8)))
    up_weight = bell_draw(splits[4], (N_SECTION, EXPERTS, D, FF), D ** -0.5, 0.125, ((0, 4), (1, 8)))
    down_weight = bell_draw(splits[5], (N_SECTION, EXPERTS, FF, D), FF ** -0.5, 0.21875, ((0, 4), (1, 8)))
    expert_ids_keys = jax.random.split(jax.random.fold_in(splits[6], 1), N_SECTION * TOKENS // TOK_DEV)
    expert_ids_turns = jax.random.permutation(jax.random.fold_in(splits[6], 3), N_SECTION * TOKENS // TOK_DEV)
    expert_ids = jax.vmap(lambda own, number: deal_out(jax.random.fold_in(splits[6], 2), own, number, TOK_DEV, EXPERTS, TOPK, CAP, 2))(expert_ids_keys, expert_ids_turns).reshape((N_SECTION, TOKENS, TOPK))
    gate_share = jnp.clip(jnp.exp(math.log(1.0) - 2.9957323 * jax.random.uniform(splits[7], (N_SECTION, TOKENS, TOPK), jnp.float32) ** steps_of(splits[7], (N_SECTION, TOKENS, TOPK), ((0, 4), (1, 8)), -0.2, 0.2)), 0.05, 1.0)
    return {"saved_input": saved_input, "upstream": upstream, "norm_gain": norm_gain, "gate_weight": gate_weight, "up_weight": up_weight, "down_weight": down_weight, "expert_ids": expert_ids, "gate_share": gate_share}


epsilon = 1e-06

def slot_ranks(routed, experts):
    onehot = (routed[..., None] == jnp.arange(experts, dtype=jnp.int32)).astype(jnp.int32)
    before = jnp.cumsum(onehot, axis=-2) - onehot
    return lax.optimization_barrier(jnp.sum(before * onehot, axis=-1)).astype(jnp.int32)

def expert_backward(inputs, grads, gate_w, up_w, down_w):
    pre_gate = jnp.dot(inputs, gate_w, preferred_element_type=jnp.float32)
    pre_up = jnp.dot(inputs, up_w, preferred_element_type=jnp.float32)
    sigmoid_gate = jax.nn.sigmoid(pre_gate)
    hidden_grad = lax.dot_general(grads, down_w, (((1,), (1,)), ((), ())), preferred_element_type=jnp.float32)
    d_gate = (hidden_grad * pre_up * sigmoid_gate * (1.0 + pre_gate * (1.0 - sigmoid_gate))).astype(jnp.bfloat16)
    d_up = (hidden_grad * pre_gate * sigmoid_gate).astype(jnp.bfloat16)
    summed = lax.dot_general(d_gate, gate_w, (((1,), (1,)), ((), ())), preferred_element_type=jnp.float32)
    summed = summed + lax.dot_general(d_up, up_w, (((1,), (1,)), ((), ())), preferred_element_type=jnp.float32)
    return summed.astype(jnp.bfloat16)

def section_grad(saved_rows, upstream_rows, gain_row, gate_w, up_w, down_w, routed, shares):
    inputs_f = saved_rows.astype(jnp.float32)
    inv_root = lax.rsqrt(lax.optimization_barrier(jnp.mean(inputs_f * inputs_f, axis=1, keepdims=True)) + epsilon)
    unit_rows = inputs_f * inv_root
    normed = (unit_rows * gain_row[None, :]).astype(jnp.bfloat16)
    out_grad = (shares[:, :, None] * upstream_rows.astype(jnp.float32)[:, None, :]).astype(jnp.bfloat16)
    blocks = routed.reshape(N_EXPERT, TOK_DEV * TOPK)
    slot_rank = slot_ranks(blocks, EXPERTS)
    source_row = jnp.arange(N_EXPERT, dtype=jnp.int32)[:, None] * CAP + slot_rank
    flat_ids = routed.reshape(-1).astype(jnp.int32)
    flat_rows = source_row.reshape(-1).astype(jnp.int32)
    buffer_x = jnp.zeros((EXPERTS, N_EXPERT * CAP, D), jnp.bfloat16).at[flat_ids, flat_rows].set(jnp.repeat(normed, TOPK, axis=0))
    buffer_d = jnp.zeros((EXPERTS, N_EXPERT * CAP, D), jnp.bfloat16).at[flat_ids, flat_rows].set(out_grad.reshape(-1, D))
    back_rows = lax.map(lambda items: expert_backward(items[0], items[1], items[2], items[3], items[4]), (buffer_x, buffer_d, gate_w, up_w, down_w))
    gathered = back_rows[flat_ids, flat_rows].astype(jnp.float32).reshape(TOKENS, TOPK, D)
    normed_grad = lax.optimization_barrier(jnp.sum(gathered, axis=1))
    scaled = normed_grad * gain_row[None, :]
    layer_grad = upstream_rows.astype(jnp.float32) + inv_root * (scaled - unit_rows * lax.optimization_barrier(jnp.mean(scaled * unit_rows, axis=1, keepdims=True)))
    return layer_grad.astype(jnp.bfloat16)

def reference(saved_input, upstream, norm_gain, gate_weight, up_weight, down_weight, expert_ids, gate_share):
    layers = []
    for section_index in range(N_SECTION):
        layers.append(section_grad(saved_input[section_index], upstream[section_index], norm_gain[section_index], gate_weight[section_index], up_weight[section_index], down_weight[section_index], expert_ids[section_index], gate_share[section_index]))
    stacked = jnp.stack(layers, axis=0)
    return jnp.roll(stacked, -1, axis=0)
```

```python
import jax
import jax.numpy as jnp
from jax import lax
from jax.sharding import PartitionSpec as P

epsilon = 1e-06
dense_most = 16


def shifted(value, axis, by):
    length = lax.axis_size(axis)
    return lax.ppermute(value, axis, [(i, (i + by) % length) for i in range(length)])


def slot_ranks(flat_ids, experts):
    pairs = flat_ids.shape[0]
    onehot = (flat_ids[:, None] == jnp.arange(experts, dtype=jnp.int32)[None, :]).astype(
        jnp.bfloat16
    )
    row_index = jnp.arange(pairs, dtype=jnp.int32)
    lower = (row_index[None, :] < row_index[:, None]).astype(jnp.bfloat16)
    before = jnp.dot(lower, onehot, preferred_element_type=jnp.float32)
    ranks = jnp.sum(before * onehot.astype(jnp.float32), axis=1)
    return ranks.astype(jnp.int32)


def expert_backward(inputs, grads, gate_w, up_w, down_w):
    pre_gate = jnp.dot(inputs, gate_w, preferred_element_type=jnp.float32)
    pre_up = jnp.dot(inputs, up_w, preferred_element_type=jnp.float32)
    sigmoid_gate = jax.nn.sigmoid(pre_gate)
    hidden_grad = lax.dot_general(
        grads, down_w, (((1,), (1,)), ((), ())), preferred_element_type=jnp.float32
    )
    d_gate = (hidden_grad * pre_up * sigmoid_gate * (1.0 + pre_gate * (1.0 - sigmoid_gate))).astype(
        jnp.bfloat16
    )
    d_up = (hidden_grad * pre_gate * sigmoid_gate).astype(jnp.bfloat16)
    summed = lax.dot_general(
        d_gate, gate_w, (((1,), (1,)), ((), ())), preferred_element_type=jnp.float32
    )
    summed = summed + lax.dot_general(
        d_up, up_w, (((1,), (1,)), ((), ())), preferred_element_type=jnp.float32
    )
    return summed.astype(jnp.bfloat16)


def routed_device(
    saved_input, upstream, norm_gain, gate_weight, up_weight, down_weight, expert_ids, gate_share
):
    saved_rows = saved_input[0]
    upstream_rows = upstream[0]
    gain_row = norm_gain[0]
    gate_w = gate_weight[0, 0]
    up_w = up_weight[0, 0]
    down_w = down_weight[0, 0]
    routed = expert_ids[0]
    shares = gate_share[0]
    tok_rows, top_count = routed.shape
    model_width = saved_rows.shape[1]
    experts = lax.axis_size("expert")
    capacity = max(2, 3 * tok_rows * top_count // (2 * experts))
    inputs_f = saved_rows.astype(jnp.float32)
    inv_root = lax.rsqrt(jnp.mean(inputs_f * inputs_f, axis=1, keepdims=True) + epsilon)
    unit_rows = inputs_f * inv_root
    normed = (unit_rows * gain_row[None, :]).astype(jnp.bfloat16)
    flat_ids = routed.reshape(-1)
    slot_rank = slot_ranks(flat_ids, experts)
    slot_number = (flat_ids * capacity + slot_rank).reshape(tok_rows, top_count)
    slot_index = jnp.arange(experts * capacity, dtype=jnp.int32)
    matches = slot_number[None, :, :] == slot_index[:, None, None]
    select = jnp.any(matches, axis=2).astype(jnp.bfloat16)
    slot_share = jnp.sum(jnp.where(matches, shares[None, :, :], 0.0), axis=(1, 2))
    send_inputs = jnp.dot(select, normed, preferred_element_type=jnp.float32).astype(jnp.bfloat16)
    send_inputs = send_inputs.reshape(experts, capacity, model_width)
    copied_grads = jnp.dot(select, upstream_rows, preferred_element_type=jnp.float32)
    send_grads = (
        (copied_grads * slot_share[:, None])
        .astype(jnp.bfloat16)
        .reshape(experts, capacity, model_width)
    )
    got_inputs, got_grads = (
        lax.all_to_all(send_inputs, "expert", split_axis=0, concat_axis=0, tiled=True),
        lax.all_to_all(send_grads, "expert", split_axis=0, concat_axis=0, tiled=True),
    )
    slot_count = got_inputs.shape[1]
    result_rows = expert_backward(
        got_inputs.reshape(-1, model_width),
        got_grads.reshape(-1, model_width),
        gate_w,
        up_w,
        down_w,
    )
    returned = lax.all_to_all(
        result_rows.reshape(experts, slot_count, model_width),
        "expert",
        split_axis=0,
        concat_axis=0,
        tiled=True,
    )
    normed_grad = lax.dot_general(
        select,
        returned.reshape(experts * capacity, model_width),
        (((0,), (0,)), ((), ())),
        preferred_element_type=jnp.float32,
    )
    scaled = normed_grad * gain_row[None, :]
    layer_grad = upstream_rows.astype(jnp.float32) + inv_root * (
        scaled - unit_rows * jnp.mean(scaled * unit_rows, axis=1, keepdims=True)
    )
    layer_grad = layer_grad.astype(jnp.bfloat16)
    passed = shifted(layer_grad, "section", -1)
    return passed[None]


def dense_share(routed, shares, experts):
    named = routed[:, :, None] == jnp.arange(experts, dtype=jnp.int32)[None, None, :]
    return jnp.sum(jnp.where(named, shares[:, :, None], 0.0), axis=1)


def dense_device(
    saved_input, upstream, norm_gain, gate_weight, up_weight, down_weight, expert_ids, gate_share
):
    saved_rows = saved_input[0]
    upstream_rows = upstream[0]
    gain_row = norm_gain[0]
    gate_w = gate_weight[0, 0]
    up_w = up_weight[0, 0]
    down_w = down_weight[0, 0]
    experts = lax.axis_size("expert")
    me = lax.axis_index("expert")
    inputs_f = saved_rows.astype(jnp.float32)
    inv_root = lax.rsqrt(jnp.mean(inputs_f * inputs_f, axis=1, keepdims=True) + epsilon)
    unit_rows = inputs_f * inv_root
    normed = (unit_rows * gain_row[None, :]).astype(jnp.bfloat16)
    shares = dense_share(expert_ids[0], gate_share[0], experts)
    all_normed = lax.all_gather(normed, "expert", axis=0, tiled=True)
    all_upstream = lax.all_gather(upstream_rows, "expert", axis=0, tiled=True)
    all_shares = lax.all_gather(shares, "expert", axis=0, tiled=True)
    mine = (jnp.arange(experts) == me).astype(jnp.float32)
    share = jnp.sum(all_shares * mine[None, :], axis=1, keepdims=True)
    pre_gate = jnp.dot(all_normed, gate_w, preferred_element_type=jnp.float32)
    pre_up = jnp.dot(all_normed, up_w, preferred_element_type=jnp.float32)
    sigmoid_gate = jax.nn.sigmoid(pre_gate)
    hidden_grad = share * lax.dot_general(
        all_upstream, down_w, (((1,), (1,)), ((), ())), preferred_element_type=jnp.float32
    )
    d_gate = (hidden_grad * pre_up * sigmoid_gate * (1.0 + pre_gate * (1.0 - sigmoid_gate))).astype(
        jnp.bfloat16
    )
    d_up = (hidden_grad * pre_gate * sigmoid_gate).astype(jnp.bfloat16)
    summed = lax.dot_general(
        d_gate, gate_w, (((1,), (1,)), ((), ())), preferred_element_type=jnp.float32
    )
    summed = summed + lax.dot_general(
        d_up, up_w, (((1,), (1,)), ((), ())), preferred_element_type=jnp.float32
    )
    pieces = summed.astype(jnp.bfloat16)
    normed_grad = lax.psum_scatter(pieces, "expert", scatter_dimension=0, tiled=True)
    scaled = normed_grad.astype(jnp.float32) * gain_row[None, :]
    layer_grad = upstream_rows.astype(jnp.float32) + inv_root * (
        scaled - unit_rows * jnp.mean(scaled * unit_rows, axis=1, keepdims=True)
    )
    passed = shifted(layer_grad.astype(jnp.bfloat16), "section", -1)
    return passed[None]


def solution(mesh):
    placed = (
        P("section", "expert", None),
        P("section", "expert", None),
        P("section", None),
        P("section", "expert", None, None),
        P("section", "expert", None, None),
        P("section", "expert", None, None),
        P("section", "expert", None),
        P("section", "expert", None),
    )
    plan = dense_device if mesh.shape["expert"] <= dense_most else routed_device
    return jax.shard_map(
        plan,
        mesh=mesh,
        in_specs=placed,
        out_specs=P("section", "expert", None),
        check_vma=False,
    )
```

```python
import functools
import jax
import jax.numpy as jnp
from jax import lax
from jax.experimental import pallas as pl
from jax.experimental.pallas import tpu as pltpu
from jax.sharding import PartitionSpec as P

epsilon = 1e-06
chunks = 1


def shifted(value, axis, by):
    length = lax.axis_size(axis)
    return lax.ppermute(value, axis, [(i, (i + by) % length) for i in range(length)])


def slot_ranks(flat_ids, experts):
    pairs = flat_ids.shape[0]
    onehot = (flat_ids[:, None] == jnp.arange(experts, dtype=jnp.int32)[None, :]).astype(
        jnp.bfloat16
    )
    row_index = jnp.arange(pairs, dtype=jnp.int32)
    lower = (row_index[None, :] < row_index[:, None]).astype(jnp.bfloat16)
    before = jnp.dot(lower, onehot, preferred_element_type=jnp.float32)
    ranks = jnp.sum(before * onehot.astype(jnp.float32), axis=1)
    return ranks.astype(jnp.int32)


def expert_backward(inputs, grads, gate_w, up_w, down_w):
    pre_gate = jnp.dot(inputs, gate_w, preferred_element_type=jnp.float32)
    pre_up = jnp.dot(inputs, up_w, preferred_element_type=jnp.float32)
    sigmoid_gate = jax.nn.sigmoid(pre_gate)
    hidden_grad = lax.dot_general(
        grads, down_w, (((1,), (1,)), ((), ())), preferred_element_type=jnp.float32
    )
    d_gate = (hidden_grad * pre_up * sigmoid_gate * (1.0 + pre_gate * (1.0 - sigmoid_gate))).astype(
        jnp.bfloat16
    )
    d_up = (hidden_grad * pre_gate * sigmoid_gate).astype(jnp.bfloat16)
    summed = lax.dot_general(
        d_gate, gate_w, (((1,), (1,)), ((), ())), preferred_element_type=jnp.float32
    )
    summed = summed + lax.dot_general(
        d_up, up_w, (((1,), (1,)), ((), ())), preferred_element_type=jnp.float32
    )
    return summed.astype(jnp.bfloat16)


def routed_device(
    saved_input, upstream, norm_gain, gate_weight, up_weight, down_weight, expert_ids, gate_share
):
    saved_rows = saved_input[0]
    upstream_rows = upstream[0]
    gain_row = norm_gain[0]
    gate_w = gate_weight[0, 0]
    up_w = up_weight[0, 0]
    down_w = down_weight[0, 0]
    routed = expert_ids[0]
    shares = gate_share[0]
    tok_rows, top_count = routed.shape
    model_width = saved_rows.shape[1]
    experts = lax.axis_size("expert")
    capacity = max(2, 3 * tok_rows * top_count // (2 * experts))
    inputs_f = saved_rows.astype(jnp.float32)
    inv_root = lax.rsqrt(jnp.mean(inputs_f * inputs_f, axis=1, keepdims=True) + epsilon)
    unit_rows = inputs_f * inv_root
    normed = (unit_rows * gain_row[None, :]).astype(jnp.bfloat16)
    flat_ids = routed.reshape(-1)
    slot_rank = slot_ranks(flat_ids, experts)
    slot_number = (flat_ids * capacity + slot_rank).reshape(tok_rows, top_count)
    slot_index = jnp.arange(experts * capacity, dtype=jnp.int32)
    matches = slot_number[None, :, :] == slot_index[:, None, None]
    select = jnp.any(matches, axis=2).astype(jnp.bfloat16)
    slot_share = jnp.sum(jnp.where(matches, shares[None, :, :], 0.0), axis=(1, 2))
    send_inputs = jnp.dot(select, normed, preferred_element_type=jnp.float32).astype(jnp.bfloat16)
    send_inputs = send_inputs.reshape(experts, capacity, model_width)
    copied_grads = jnp.dot(select, upstream_rows, preferred_element_type=jnp.float32)
    send_grads = (
        (copied_grads * slot_share[:, None])
        .astype(jnp.bfloat16)
        .reshape(experts, capacity, model_width)
    )
    got_inputs, got_grads = (
        lax.all_to_all(send_inputs, "expert", split_axis=0, concat_axis=0, tiled=True),
        lax.all_to_all(send_grads, "expert", split_axis=0, concat_axis=0, tiled=True),
    )
    slot_count = got_inputs.shape[1]
    result_rows = expert_backward(
        got_inputs.reshape(-1, model_width),
        got_grads.reshape(-1, model_width),
        gate_w,
        up_w,
        down_w,
    )
    returned = lax.all_to_all(
        result_rows.reshape(experts, slot_count, model_width),
        "expert",
        split_axis=0,
        concat_axis=0,
        tiled=True,
    )
    normed_grad = lax.dot_general(
        select,
        returned.reshape(experts * capacity, model_width),
        (((0,), (0,)), ((), ())),
        preferred_element_type=jnp.float32,
    )
    scaled = normed_grad * gain_row[None, :]
    layer_grad = upstream_rows.astype(jnp.float32) + inv_root * (
        scaled - unit_rows * jnp.mean(scaled * unit_rows, axis=1, keepdims=True)
    )
    layer_grad = layer_grad.astype(jnp.bfloat16)
    passed = shifted(layer_grad, "section", -1)
    return passed[None]


def share_parts(routed, shares, experts, lanes):
    named = routed[:, :, None] == jnp.arange(experts, dtype=jnp.int32)[None, None, :]
    dense = jnp.sum(jnp.where(named, shares[:, :, None], 0.0), axis=1)
    high = lax.reduce_precision(dense, 8, 7)
    middle = lax.reduce_precision(dense - high, 8, 7)
    low = dense - high - middle
    parts = jnp.concatenate([high, middle, low], axis=1)
    parts = jnp.pad(parts, ((0, 0), (0, lanes - 3 * experts)))
    return parts.astype(jnp.bfloat16)


def slot_kernel(
    steps, experts, named_ref, rows_ref, gate_a, up_a, down_a, gate_b, up_b, down_b, out_ref
):
    step = pl.program_id(0)
    width = out_ref.shape[1]

    @pl.when(step == 0)
    def _():
        out_ref[...] = jnp.zeros_like(out_ref)

    def add(named, gate_ref, up_ref, down_ref):
        parts = rows_ref[:, 2 * width :].astype(jnp.float32)
        lane = lax.broadcasted_iota(jnp.int32, parts.shape, 1)
        wanted = (lax.rem(lane, experts) == named) & (lane < 3 * experts)
        share = jnp.sum(jnp.where(wanted, parts, 0.0), axis=1, keepdims=True)
        inputs = rows_ref[:, :width]
        grads = rows_ref[:, width : 2 * width]
        gate_w, up_w = gate_ref[...], up_ref[...]
        last = (((1,), (1,)), ((), ()))
        pre_gate = jnp.dot(inputs, gate_w, preferred_element_type=jnp.float32)
        pre_up = jnp.dot(inputs, up_w, preferred_element_type=jnp.float32)
        hidden = lax.dot_general(grads, down_ref[...], last, preferred_element_type=jnp.float32)
        hidden = hidden * share
        sigmoid_gate = jax.nn.sigmoid(pre_gate)
        d_gate = hidden * pre_up * sigmoid_gate * (1.0 + pre_gate * (1.0 - sigmoid_gate))
        d_up = hidden * pre_gate * sigmoid_gate
        out_ref[...] += lax.dot_general(
            d_gate.astype(jnp.bfloat16), gate_w, last, preferred_element_type=jnp.float32
        ) + lax.dot_general(
            d_up.astype(jnp.bfloat16), up_w, last, preferred_element_type=jnp.float32
        )

    @pl.when(step < steps)
    def _():
        add(named_ref[0], gate_a, up_a, down_a)

    @pl.when(step >= steps)
    def _():
        add(named_ref[1], gate_b, up_b, down_b)


def slot_pieces(named, rows, own, other, experts, width):
    count, hidden = rows.shape[0], own[0].shape[1]
    tile = 256
    steps = hidden // tile

    def first(i, n):
        return jnp.minimum(i, steps - 1)

    def second(i, n):
        return jnp.maximum(i - steps, 0)

    def specs(pick):
        return [
            pl.BlockSpec((width, tile), lambda i, n: (0, pick(i, n))),
            pl.BlockSpec((width, tile), lambda i, n: (0, pick(i, n))),
            pl.BlockSpec((tile, width), lambda i, n: (pick(i, n), 0)),
        ]

    return pl.pallas_call(
        functools.partial(slot_kernel, steps, experts),
        grid_spec=pltpu.PrefetchScalarGridSpec(
            num_scalar_prefetch=1,
            grid=(2 * steps,),
            in_specs=[pl.BlockSpec(rows.shape, lambda i, n: (0, 0))] + specs(first) + specs(second),
            out_specs=pl.BlockSpec((count, width), lambda i, n: (0, 0)),
        ),
        out_shape=jax.ShapeDtypeStruct((count, width), jnp.float32),
        cost_estimate=pl.CostEstimate(
            flops=20 * count * width * hidden,
            bytes_accessed=12 * width * hidden + 8 * count * width,
            transcendentals=2 * count * hidden,
        ),
        compiler_params=pltpu.CompilerParams(vmem_limit_bytes=40 << 20),
    )(named, rows, *own, *other)


def line_device(
    saved_input, upstream, norm_gain, gate_weight, up_weight, down_weight, expert_ids, gate_share
):
    own = (gate_weight[0, 0], up_weight[0, 0], down_weight[0, 0])
    upstream_rows = upstream[0]
    gain_row = norm_gain[0]
    tok_rows, width = upstream_rows.shape
    experts = lax.axis_size("expert")
    me = lax.axis_index("expert")
    is_end = (me // 2 == 0) | (me // 2 == experts // 2 - 1)
    named = jnp.stack([me, me ^ 1]).astype(jnp.int32)

    def along(pairs):
        cores = [(2 * a + h, 2 * b + h) for a, b in pairs for h in range(2)]
        return lambda value: lax.ppermute(value, "expert", cores)

    pair_hop = along([(0, 1), (1, 0), (2, 3), (3, 2)])
    middle_hop = along([(1, 2), (2, 1)])
    outward_hop = along([(1, 0), (2, 3)])
    inward_hop = along([(0, 1), (3, 2)])

    inputs_f = saved_input[0].astype(jnp.float32)
    inv_root = lax.rsqrt(jnp.mean(inputs_f * inputs_f, axis=1, keepdims=True) + epsilon)
    unit_rows = inputs_f * inv_root
    normed = (unit_rows * gain_row[None, :]).astype(jnp.bfloat16)
    parts = share_parts(expert_ids[0], gate_share[0], experts, 128)
    rows = jnp.concatenate([normed, upstream_rows, parts], axis=1)
    swap = [(i, i ^ 1) for i in range(experts)]

    size = tok_rows // chunks
    cuts = [slice(c * size, (c + 1) * size) for c in range(chunks)]
    slots = []
    other = None
    for cut in cuts:
        mine = rows[cut]
        near = pair_hop(mine)
        across = middle_hop(mine)
        if other is None:
            other = tuple(lax.ppermute(w, "expert", swap) for w in own)
        second = outward_hop(across)
        far = middle_hop(near)
        third = outward_hop(far)
        slots.append(
            (mine, near, jnp.where(is_end, second, across), jnp.where(is_end, third, far))
        )
    passed = []
    for cut, (mine, near, second, third) in zip(cuts, slots):
        pieces = lambda block: slot_pieces(named, block, own, other, experts, width)
        here, at_near, at_second, at_third = pieces(mine), pieces(near), pieces(second), pieces(third)
        narrow = lambda value: value.astype(jnp.bfloat16)
        wide = lambda value: value.astype(jnp.float32)
        in_third = inward_hop(narrow(at_third))
        in_second = inward_hop(narrow(at_second))
        over_third = middle_hop(narrow(at_third + wide(in_third)))
        over_second = middle_hop(narrow(at_second + wide(in_second)))
        last = pair_hop(narrow(at_near + wide(over_third)))
        normed_grad = here + wide(over_second) + wide(last)
        scaled = normed_grad * gain_row[None, :]
        unit = unit_rows[cut]
        layer_grad = wide(upstream_rows[cut]) + inv_root[cut] * (
            scaled - unit * jnp.mean(scaled * unit, axis=1, keepdims=True)
        )
        passed.append(shifted(narrow(layer_grad), "section", -1))
    return jnp.concatenate(passed, axis=0)[None]


def solution(mesh):
    placed = (
        P("section", "expert", None),
        P("section", "expert", None),
        P("section", None),
        P("section", "expert", None, None),
        P("section", "expert", None, None),
        P("section", "expert", None, None),
        P("section", "expert", None),
        P("section", "expert", None),
    )
    plan = line_device if mesh.shape["expert"] == 8 else routed_device
    return jax.shard_map(
        plan,
        mesh=mesh,
        in_specs=placed,
        out_specs=P("section", "expert", None),
        check_vma=False,
    )
```

```python
import functools
import jax
import jax.numpy as jnp
from jax import lax
from jax.experimental import pallas as pl
from jax.experimental.pallas import tpu as pltpu
from jax.sharding import PartitionSpec as P

epsilon = 1e-06
chunks = 2


def shifted(value, axis, by):
    length = lax.axis_size(axis)
    return lax.ppermute(value, axis, [(i, (i + by) % length) for i in range(length)])


def slot_ranks(flat_ids, experts):
    pairs = flat_ids.shape[0]
    onehot = (flat_ids[:, None] == jnp.arange(experts, dtype=jnp.int32)[None, :]).astype(
        jnp.bfloat16
    )
    row_index = jnp.arange(pairs, dtype=jnp.int32)
    lower = (row_index[None, :] < row_index[:, None]).astype(jnp.bfloat16)
    before = jnp.dot(lower, onehot, preferred_element_type=jnp.float32)
    ranks = jnp.sum(before * onehot.astype(jnp.float32), axis=1)
    return ranks.astype(jnp.int32)


def expert_backward(inputs, grads, gate_w, up_w, down_w):
    pre_gate = jnp.dot(inputs, gate_w, preferred_element_type=jnp.float32)
    pre_up = jnp.dot(inputs, up_w, preferred_element_type=jnp.float32)
    sigmoid_gate = jax.nn.sigmoid(pre_gate)
    hidden_grad = lax.dot_general(
        grads, down_w, (((1,), (1,)), ((), ())), preferred_element_type=jnp.float32
    )
    d_gate = (hidden_grad * pre_up * sigmoid_gate * (1.0 + pre_gate * (1.0 - sigmoid_gate))).astype(
        jnp.bfloat16
    )
    d_up = (hidden_grad * pre_gate * sigmoid_gate).astype(jnp.bfloat16)
    summed = lax.dot_general(
        d_gate, gate_w, (((1,), (1,)), ((), ())), preferred_element_type=jnp.float32
    )
    summed = summed + lax.dot_general(
        d_up, up_w, (((1,), (1,)), ((), ())), preferred_element_type=jnp.float32
    )
    return summed.astype(jnp.bfloat16)


def routed_device(
    saved_input, upstream, norm_gain, gate_weight, up_weight, down_weight, expert_ids, gate_share
):
    saved_rows = saved_input[0]
    upstream_rows = upstream[0]
    gain_row = norm_gain[0]
    gate_w = gate_weight[0, 0]
    up_w = up_weight[0, 0]
    down_w = down_weight[0, 0]
    routed = expert_ids[0]
    shares = gate_share[0]
    tok_rows, top_count = routed.shape
    model_width = saved_rows.shape[1]
    experts = lax.axis_size("expert")
    capacity = max(2, 3 * tok_rows * top_count // (2 * experts))
    inputs_f = saved_rows.astype(jnp.float32)
    inv_root = lax.rsqrt(jnp.mean(inputs_f * inputs_f, axis=1, keepdims=True) + epsilon)
    unit_rows = inputs_f * inv_root
    normed = (unit_rows * gain_row[None, :]).astype(jnp.bfloat16)
    flat_ids = routed.reshape(-1)
    slot_rank = slot_ranks(flat_ids, experts)
    slot_number = (flat_ids * capacity + slot_rank).reshape(tok_rows, top_count)
    slot_index = jnp.arange(experts * capacity, dtype=jnp.int32)
    matches = slot_number[None, :, :] == slot_index[:, None, None]
    select = jnp.any(matches, axis=2).astype(jnp.bfloat16)
    slot_share = jnp.sum(jnp.where(matches, shares[None, :, :], 0.0), axis=(1, 2))
    send_inputs = jnp.dot(select, normed, preferred_element_type=jnp.float32).astype(jnp.bfloat16)
    send_inputs = send_inputs.reshape(experts, capacity, model_width)
    copied_grads = jnp.dot(select, upstream_rows, preferred_element_type=jnp.float32)
    send_grads = (
        (copied_grads * slot_share[:, None])
        .astype(jnp.bfloat16)
        .reshape(experts, capacity, model_width)
    )
    got_inputs, got_grads = (
        lax.all_to_all(send_inputs, "expert", split_axis=0, concat_axis=0, tiled=True),
        lax.all_to_all(send_grads, "expert", split_axis=0, concat_axis=0, tiled=True),
    )
    slot_count = got_inputs.shape[1]
    result_rows = expert_backward(
        got_inputs.reshape(-1, model_width),
        got_grads.reshape(-1, model_width),
        gate_w,
        up_w,
        down_w,
    )
    returned = lax.all_to_all(
        result_rows.reshape(experts, slot_count, model_width),
        "expert",
        split_axis=0,
        concat_axis=0,
        tiled=True,
    )
    normed_grad = lax.dot_general(
        select,
        returned.reshape(experts * capacity, model_width),
        (((0,), (0,)), ((), ())),
        preferred_element_type=jnp.float32,
    )
    scaled = normed_grad * gain_row[None, :]
    layer_grad = upstream_rows.astype(jnp.float32) + inv_root * (
        scaled - unit_rows * jnp.mean(scaled * unit_rows, axis=1, keepdims=True)
    )
    layer_grad = layer_grad.astype(jnp.bfloat16)
    passed = shifted(layer_grad, "section", -1)
    return passed[None]


in_vmem = pl.BlockSpec(memory_space=pltpu.VMEM)
in_smem = pl.BlockSpec(memory_space=pltpu.SMEM)
anywhere = pl.BlockSpec(memory_space=pl.ANY)


def prep_kernel(experts, saved_ref, upstream_ref, gain_ref, ids_ref, share_ref, *out_refs):
    root_ref, row_refs = out_refs[0], out_refs[1:]
    size, width = row_refs[0].shape[0], saved_ref.shape[1]
    lanes = row_refs[0].shape[1] - 2 * width
    for c, ref in enumerate(row_refs):
        cut = pl.ds(c * size, size)
        value = saved_ref[cut, :].astype(jnp.float32)
        mean = jnp.mean(value * value, axis=1, keepdims=True)
        inv_root = lax.rsqrt(mean + epsilon)
        root_ref[cut, :] = inv_root
        ref[:, :width] = (value * inv_root * gain_ref[...]).astype(jnp.bfloat16)
        ref[:, width : 2 * width] = upstream_ref[cut, :]
        lane = lax.broadcasted_iota(jnp.int32, (size, lanes), 1)
        dense = jnp.zeros((size, lanes), jnp.float32)
        for k in range(ids_ref.shape[1]):
            hit = lax.rem(lane, experts) == ids_ref[cut, k : k + 1]
            dense = dense + jnp.where(hit, share_ref[cut, k : k + 1], 0.0)
        high = dense.astype(jnp.bfloat16).astype(jnp.float32)
        middle = (dense - high).astype(jnp.bfloat16).astype(jnp.float32)
        low = dense - high - middle
        parts = jnp.where(lane < experts, high, jnp.where(lane < 2 * experts, middle, low))
        ref[:, 2 * width :] = jnp.where(lane < 3 * experts, parts, 0.0).astype(jnp.bfloat16)


def prep(saved_rows, upstream_rows, gain_row, routed, shares, experts):
    count, width = saved_rows.shape
    lanes = 128
    block = jax.ShapeDtypeStruct((count // chunks, 2 * width + lanes), jnp.bfloat16)
    return pl.pallas_call(
        functools.partial(prep_kernel, experts),
        in_specs=[in_vmem] * 5,
        out_specs=[in_vmem] * (1 + chunks),
        out_shape=[jax.ShapeDtypeStruct((count, 1), jnp.float32)] + [block] * chunks,
        compiler_params=pltpu.CompilerParams(vmem_limit_bytes=24 << 20),
    )(saved_rows, upstream_rows, gain_row, routed, shares)


def slot_kernel(experts, picked, named_ref, *refs):
    count = 4 if picked else 2
    block_refs, weight_refs = refs[:count], refs[count : count + 6]
    out_refs = refs[-6:-4]
    rows_ref, gate_grads, up_grads, share_ref = refs[-4:]
    size = block_refs[0].shape[0]
    width = out_refs[0].shape[1]
    hidden = weight_refs[0].shape[1]
    tile = 256
    last = (((1,), (1,)), ((), ()))
    if picked:

        @pl.when(named_ref[2] == 1)
        def _():
            rows_ref[:size, :] = block_refs[0][...]
            rows_ref[size:, :] = block_refs[2][...]

        @pl.when(named_ref[2] == 0)
        def _():
            rows_ref[:size, :] = block_refs[1][...]
            rows_ref[size:, :] = block_refs[3][...]
    else:
        rows_ref[:size, :] = block_refs[0][...]
        rows_ref[size:, :] = block_refs[1][...]
    parts = rows_ref[:, 2 * width :].astype(jnp.float32)
    lane = lax.broadcasted_iota(jnp.int32, parts.shape, 1)
    for w in range(2):
        wanted = (lax.rem(lane, experts) == named_ref[w]) & (lane < 3 * experts)
        share_ref[w] = jnp.sum(jnp.where(wanted, parts, 0.0), axis=1, keepdims=True)
    for w in range(2):
        gate_ref, up_ref, down_ref = weight_refs[3 * w : 3 * w + 3]

        def grads_of(step, carry):
            cut = pl.ds(pl.multiple_of(step * tile, tile), tile)
            inputs = rows_ref[:, :width]
            pre_gate = jnp.dot(inputs, gate_ref[:, cut], preferred_element_type=jnp.float32)
            pre_up = jnp.dot(inputs, up_ref[:, cut], preferred_element_type=jnp.float32)
            grad = lax.dot_general(
                rows_ref[:, width : 2 * width],
                down_ref[cut, :],
                last,
                preferred_element_type=jnp.float32,
            )
            grad = grad * share_ref[w]
            sigmoid_gate = jax.nn.sigmoid(pre_gate)
            scaled = grad * sigmoid_gate
            d_gate = scaled * pre_up * (1.0 + pre_gate * (1.0 - sigmoid_gate))
            gate_grads[w, :, cut] = d_gate.astype(jnp.bfloat16)
            up_grads[w, :, cut] = (scaled * pre_gate).astype(jnp.bfloat16)
            return carry

        lax.fori_loop(0, hidden // tile, grads_of, 0)

    def pieces_of(step, carry):
        cut = pl.ds(pl.multiple_of(step * tile, tile), tile)
        total = None
        for w in range(2):
            for held, weight_ref in ((gate_grads, weight_refs[3 * w]), (up_grads, weight_refs[3 * w + 1])):
                part = lax.dot_general(
                    held[w], weight_ref[cut, :], last, preferred_element_type=jnp.float32
                )
                total = part if total is None else total + part
        out_refs[0][:, cut] = total[:size].astype(out_refs[0].dtype)
        out_refs[1][:, cut] = total[size:].astype(out_refs[1].dtype)
        return carry

    lax.fori_loop(0, width // tile, pieces_of, 0)


def slot_pieces(named, blocks, own, other, after, experts, width, kinds):
    size = blocks[0].shape[0]
    hidden = own[0].shape[1]
    rows = 2 * size
    return pl.pallas_call(
        functools.partial(slot_kernel, experts, len(blocks) == 4),
        in_specs=[in_smem] + [in_vmem] * (len(blocks) + 6) + [anywhere] * len(after),
        out_specs=[in_vmem] * 2,
        out_shape=[jax.ShapeDtypeStruct((size, width), kind) for kind in kinds],
        scratch_shapes=[
            pltpu.VMEM((rows, blocks[0].shape[1]), jnp.bfloat16),
            pltpu.VMEM((2, rows, hidden), jnp.bfloat16),
            pltpu.VMEM((2, rows, hidden), jnp.bfloat16),
            pltpu.VMEM((2, rows, 1), jnp.float32),
        ],
        cost_estimate=pl.CostEstimate(
            flops=20 * rows * width * hidden,
            bytes_accessed=12 * width * hidden + 8 * rows * width,
            transcendentals=2 * rows * hidden,
        ),
        compiler_params=pltpu.CompilerParams(vmem_limit_bytes=48 << 20),
    )(named, *blocks, *own, *other, *after)


def final_kernel(first, saved_ref, upstream_ref, gain_ref, root_ref, here_ref, second_ref, last_ref, out_ref):
    cut = pl.ds(first, out_ref.shape[0])
    inv_root = root_ref[cut, :]
    normed_grad = here_ref[...] + second_ref[...].astype(jnp.float32)
    normed_grad = normed_grad + last_ref[...].astype(jnp.float32)
    scaled = normed_grad * gain_ref[...]
    unit = saved_ref[cut, :].astype(jnp.float32) * inv_root
    mean = jnp.mean(scaled * unit, axis=1, keepdims=True)
    layer_grad = upstream_ref[cut, :].astype(jnp.float32) + inv_root * (scaled - unit * mean)
    out_ref[...] = layer_grad.astype(jnp.bfloat16)


def finish(first, saved_rows, upstream_rows, gain_row, inv_root, here, second, last):
    return pl.pallas_call(
        functools.partial(final_kernel, first),
        in_specs=[in_vmem] * 7,
        out_specs=in_vmem,
        out_shape=jax.ShapeDtypeStruct(here.shape, jnp.bfloat16),
        compiler_params=pltpu.CompilerParams(vmem_limit_bytes=24 << 20),
    )(saved_rows, upstream_rows, gain_row, inv_root, here, second, last)


def line_device(
    saved_input, upstream, norm_gain, gate_weight, up_weight, down_weight, expert_ids, gate_share
):
    own = (gate_weight[0, 0], up_weight[0, 0], down_weight[0, 0])
    saved_rows, upstream_rows = saved_input[0], upstream[0]
    tok_rows, width = upstream_rows.shape
    experts = lax.axis_size("expert")
    me = lax.axis_index("expert")
    is_end = (me // 2 == 0) | (me // 2 == experts // 2 - 1)
    named = jnp.stack([me, me ^ 1, is_end.astype(jnp.int32)]).astype(jnp.int32)

    def along(pairs):
        cores = [(2 * a + h, 2 * b + h) for a, b in pairs for h in range(2)]
        return lambda value: lax.ppermute(value, "expert", cores)

    pair_hop = along([(0, 1), (1, 0), (2, 3), (3, 2)])
    middle_hop = along([(1, 2), (2, 1)])
    outward_hop = along([(1, 0), (2, 3)])
    inward_hop = along([(0, 1), (3, 2)])
    narrow = lambda value: value.astype(jnp.bfloat16)
    wide = lambda value: value.astype(jnp.float32)

    inv_root, *blocks = prep(
        saved_rows, upstream_rows, norm_gain, expert_ids[0], gate_share[0], experts
    )
    swap = [(i, i ^ 1) for i in range(experts)]
    size = tok_rows // chunks
    moved = []
    other = None
    for mine in blocks:
        near = pair_hop(mine)
        across = middle_hop(mine)
        if other is None:
            other = tuple(lax.ppermute(w, "expert", swap) for w in own)
        second = outward_hop(across)
        far = middle_hop(near)
        third = outward_hop(far)
        moved.append((mine, near, second, across, third, far))
    after = []
    made = []
    for mine, near, *_ in moved:
        pair = slot_pieces(
            named, (mine, near), own, other, after, experts, width, (jnp.float32, jnp.bfloat16)
        )
        after = [pair[0]]
        made.append(pair)
    passed = []
    for c, (_, _, second, across, third, far) in enumerate(moved):
        here, at_near = made[c]
        at_second, at_third = slot_pieces(
            named,
            (second, across, third, far),
            own,
            other,
            after,
            experts,
            width,
            (jnp.bfloat16, jnp.bfloat16),
        )
        after = [at_third]
        in_third = inward_hop(at_third)
        in_second = inward_hop(at_second)
        over_third = middle_hop(narrow(wide(at_third) + wide(in_third)))
        over_second = middle_hop(narrow(wide(at_second) + wide(in_second)))
        final = pair_hop(narrow(wide(at_near) + wide(over_third)))
        layer_grad = finish(
            c * size, saved_rows, upstream_rows, norm_gain, inv_root, here, over_second, final
        )
        passed.append(shifted(layer_grad, "section", -1))
    return jnp.concatenate(passed, axis=0)[None]


def solution(mesh):
    placed = (
        P("section", "expert", None),
        P("section", "expert", None),
        P("section", None),
        P("section", "expert", None, None),
        P("section", "expert", None, None),
        P("section", "expert", None, None),
        P("section", "expert", None),
        P("section", "expert", None),
    )
    plan = line_device if mesh.shape["expert"] == 8 else routed_device
    return jax.shard_map(
        plan,
        mesh=mesh,
        in_specs=placed,
        out_specs=P("section", "expert", None),
        check_vma=False,
    )
```

```python
import functools
import jax
import jax.numpy as jnp
from jax import lax
from jax.experimental import pallas as pl
from jax.experimental.pallas import tpu as pltpu
from jax.sharding import PartitionSpec as P

epsilon = 1e-06


def shifted(value, axis, by):
    length = lax.axis_size(axis)
    return lax.ppermute(value, axis, [(i, (i + by) % length) for i in range(length)])


def slot_ranks(flat_ids, experts):
    pairs = flat_ids.shape[0]
    onehot = (flat_ids[:, None] == jnp.arange(experts, dtype=jnp.int32)[None, :]).astype(
        jnp.bfloat16
    )
    row_index = jnp.arange(pairs, dtype=jnp.int32)
    lower = (row_index[None, :] < row_index[:, None]).astype(jnp.bfloat16)
    before = jnp.dot(lower, onehot, preferred_element_type=jnp.float32)
    ranks = jnp.sum(before * onehot.astype(jnp.float32), axis=1)
    return ranks.astype(jnp.int32)


def expert_backward(inputs, grads, gate_w, up_w, down_w):
    pre_gate = jnp.dot(inputs, gate_w, preferred_element_type=jnp.float32)
    pre_up = jnp.dot(inputs, up_w, preferred_element_type=jnp.float32)
    sigmoid_gate = jax.nn.sigmoid(pre_gate)
    hidden_grad = lax.dot_general(
        grads, down_w, (((1,), (1,)), ((), ())), preferred_element_type=jnp.float32
    )
    d_gate = (hidden_grad * pre_up * sigmoid_gate * (1.0 + pre_gate * (1.0 - sigmoid_gate))).astype(
        jnp.bfloat16
    )
    d_up = (hidden_grad * pre_gate * sigmoid_gate).astype(jnp.bfloat16)
    summed = lax.dot_general(
        d_gate, gate_w, (((1,), (1,)), ((), ())), preferred_element_type=jnp.float32
    )
    summed = summed + lax.dot_general(
        d_up, up_w, (((1,), (1,)), ((), ())), preferred_element_type=jnp.float32
    )
    return summed.astype(jnp.bfloat16)


def routed_device(
    saved_input, upstream, norm_gain, gate_weight, up_weight, down_weight, expert_ids, gate_share
):
    saved_rows = saved_input[0]
    upstream_rows = upstream[0]
    gain_row = norm_gain[0]
    gate_w = gate_weight[0, 0]
    up_w = up_weight[0, 0]
    down_w = down_weight[0, 0]
    routed = expert_ids[0]
    shares = gate_share[0]
    tok_rows, top_count = routed.shape
    model_width = saved_rows.shape[1]
    experts = lax.axis_size("expert")
    capacity = max(2, 3 * tok_rows * top_count // (2 * experts))
    inputs_f = saved_rows.astype(jnp.float32)
    inv_root = lax.rsqrt(jnp.mean(inputs_f * inputs_f, axis=1, keepdims=True) + epsilon)
    unit_rows = inputs_f * inv_root
    normed = (unit_rows * gain_row[None, :]).astype(jnp.bfloat16)
    flat_ids = routed.reshape(-1)
    slot_rank = slot_ranks(flat_ids, experts)
    slot_number = (flat_ids * capacity + slot_rank).reshape(tok_rows, top_count)
    slot_index = jnp.arange(experts * capacity, dtype=jnp.int32)
    matches = slot_number[None, :, :] == slot_index[:, None, None]
    select = jnp.any(matches, axis=2).astype(jnp.bfloat16)
    slot_share = jnp.sum(jnp.where(matches, shares[None, :, :], 0.0), axis=(1, 2))
    send_inputs = jnp.dot(select, normed, preferred_element_type=jnp.float32).astype(jnp.bfloat16)
    send_inputs = send_inputs.reshape(experts, capacity, model_width)
    copied_grads = jnp.dot(select, upstream_rows, preferred_element_type=jnp.float32)
    send_grads = (
        (copied_grads * slot_share[:, None])
        .astype(jnp.bfloat16)
        .reshape(experts, capacity, model_width)
    )
    got_inputs, got_grads = (
        lax.all_to_all(send_inputs, "expert", split_axis=0, concat_axis=0, tiled=True),
        lax.all_to_all(send_grads, "expert", split_axis=0, concat_axis=0, tiled=True),
    )
    slot_count = got_inputs.shape[1]
    result_rows = expert_backward(
        got_inputs.reshape(-1, model_width),
        got_grads.reshape(-1, model_width),
        gate_w,
        up_w,
        down_w,
    )
    returned = lax.all_to_all(
        result_rows.reshape(experts, slot_count, model_width),
        "expert",
        split_axis=0,
        concat_axis=0,
        tiled=True,
    )
    normed_grad = lax.dot_general(
        select,
        returned.reshape(experts * capacity, model_width),
        (((0,), (0,)), ((), ())),
        preferred_element_type=jnp.float32,
    )
    scaled = normed_grad * gain_row[None, :]
    layer_grad = upstream_rows.astype(jnp.float32) + inv_root * (
        scaled - unit_rows * jnp.mean(scaled * unit_rows, axis=1, keepdims=True)
    )
    layer_grad = layer_grad.astype(jnp.bfloat16)
    passed = shifted(layer_grad, "section", -1)
    return passed[None]


tile = 256
last_dims = (((1,), (1,)), ((), ()))
in_vmem = pl.BlockSpec(memory_space=pltpu.VMEM)
in_smem = pl.BlockSpec(memory_space=pltpu.SMEM)
anywhere = pl.BlockSpec(memory_space=pl.ANY)


def tile_cut(step):
    return pl.ds(pl.multiple_of(step * tile, tile), tile)


def shared_kernel(experts, upstream_ref, ids_ref, share_ref, out_ref):
    size, width = upstream_ref.shape
    lanes = out_ref.shape[1] - width
    out_ref[:, :width] = upstream_ref[...]
    lane = lax.broadcasted_iota(jnp.int32, (size, lanes), 1)
    dense = jnp.zeros((size, lanes), jnp.float32)
    for k in range(ids_ref.shape[1]):
        hit = lax.rem(lane, experts) == ids_ref[:, k : k + 1]
        dense = dense + jnp.where(hit, share_ref[:, k : k + 1], 0.0)
    high = dense.astype(jnp.bfloat16).astype(jnp.float32)
    middle = (dense - high).astype(jnp.bfloat16).astype(jnp.float32)
    low = dense - high - middle
    parts = jnp.where(lane < experts, high, jnp.where(lane < 2 * experts, middle, low))
    out_ref[:, width:] = jnp.where(lane < 3 * experts, parts, 0.0).astype(jnp.bfloat16)


def shared_rows(upstream_rows, routed, shares, experts):
    count, width = upstream_rows.shape
    return pl.pallas_call(
        functools.partial(shared_kernel, experts),
        in_specs=[in_vmem] * 3,
        out_specs=in_vmem,
        out_shape=jax.ShapeDtypeStruct((count, width + 128), jnp.bfloat16),
        compiler_params=pltpu.CompilerParams(vmem_limit_bytes=16 << 20),
    )(upstream_rows, routed, shares)


def factors_kernel(pairs, saved_ref, gain_ref, *refs):
    weight_refs = refs[: 2 * pairs]
    gate_ref, up_ref, rows_ref = refs[-3:]
    value = saved_ref[...].astype(jnp.float32)
    inv_root = lax.rsqrt(jnp.mean(value * value, axis=1, keepdims=True) + epsilon)
    rows_ref[...] = (value * inv_root * gain_ref[...]).astype(jnp.bfloat16)

    def body(step, carry):
        cut = tile_cut(step)
        for w in range(pairs):
            inputs = rows_ref[...]
            pre_gate = jnp.dot(
                inputs, weight_refs[2 * w][:, cut], preferred_element_type=jnp.float32
            )
            pre_up = jnp.dot(
                inputs, weight_refs[2 * w + 1][:, cut], preferred_element_type=jnp.float32
            )
            sigmoid_gate = jax.nn.sigmoid(pre_gate)
            gate_ref[w, :, cut] = pre_up * sigmoid_gate * (1.0 + pre_gate * (1.0 - sigmoid_gate))
            up_ref[w, :, cut] = pre_gate * sigmoid_gate
        return carry

    lax.fori_loop(0, gate_ref.shape[2] // tile, body, 0)


def slot_factors(rows, gain_row, weights, after):
    pairs = len(weights)
    count, width = rows.shape
    hidden = weights[0][0].shape[1]
    flat = [w for gate_w, up_w, _ in weights for w in (gate_w, up_w)]
    shape = jax.ShapeDtypeStruct((pairs, count, hidden), jnp.float32)
    return pl.pallas_call(
        functools.partial(factors_kernel, pairs),
        in_specs=[in_vmem] * (2 + len(flat)) + [anywhere] * len(after),
        out_specs=[in_vmem] * 2,
        out_shape=[shape] * 2,
        scratch_shapes=[pltpu.VMEM((count, width), jnp.bfloat16)],
        cost_estimate=pl.CostEstimate(
            flops=8 * pairs * count * width * hidden,
            bytes_accessed=4 * pairs * width * hidden,
            transcendentals=pairs * count * hidden,
        ),
        compiler_params=pltpu.CompilerParams(vmem_limit_bytes=40 << 20),
    )(rows, gain_row, *flat, *after)


def pieces_kernel(experts, pairs, start, named_ref, rows_ref, gain_ref, gate_ref, up_ref, *refs):
    weight_refs, refs = refs[: 3 * pairs], refs[3 * pairs :]
    base_ref = refs[0] if start else None
    out_ref, gate_grads, up_grads = refs[-3:]
    width = out_ref.shape[1]
    hidden = gate_ref.shape[2]
    parts = rows_ref[:, width:].astype(jnp.float32)
    lane = lax.broadcasted_iota(jnp.int32, parts.shape, 1)
    shares = []
    for w in range(pairs):
        wanted = (lax.rem(lane, experts) == named_ref[w]) & (lane < 3 * experts)
        shares.append(jnp.sum(jnp.where(wanted, parts, 0.0), axis=1, keepdims=True))

    def grads_of(step, carry):
        cut = tile_cut(step)
        for w in range(pairs):
            grad = lax.dot_general(
                rows_ref[:, :width],
                weight_refs[3 * w + 2][cut, :],
                last_dims,
                preferred_element_type=jnp.float32,
            )
            grad = grad * shares[w]
            gate_grads[w, :, cut] = (grad * gate_ref[w, :, cut]).astype(jnp.bfloat16)
            up_grads[w, :, cut] = (grad * up_ref[w, :, cut]).astype(jnp.bfloat16)
        return carry

    lax.fori_loop(0, hidden // tile, grads_of, 0)

    def pieces_of(step, carry):
        cut = tile_cut(step)
        total = None
        for w in range(pairs):
            for held, weight_ref in ((gate_grads, weight_refs[3 * w]), (up_grads, weight_refs[3 * w + 1])):
                part = lax.dot_general(
                    held[w], weight_ref[cut, :], last_dims, preferred_element_type=jnp.float32
                )
                total = part if total is None else total + part
        total = total * gain_ref[:, cut]
        if start:
            total = total + base_ref[:, cut]
        out_ref[:, cut] = total.astype(out_ref.dtype)
        return carry

    lax.fori_loop(0, width // tile, pieces_of, 0)


def slot_pieces(named, rows, gain_row, factors, weights, experts, kind, base, after):
    pairs, count, hidden = factors[0].shape
    width = weights[0][0].shape[0]
    flat = [w for group in weights for w in group]
    start = [] if base is None else [base]
    return pl.pallas_call(
        functools.partial(pieces_kernel, experts, pairs, len(start)),
        in_specs=[in_smem]
        + [in_vmem] * (4 + len(flat) + len(start))
        + [anywhere] * len(after),
        out_specs=in_vmem,
        out_shape=jax.ShapeDtypeStruct((count, width), kind),
        scratch_shapes=[pltpu.VMEM((pairs, count, hidden), jnp.bfloat16)] * 2,
        cost_estimate=pl.CostEstimate(
            flops=12 * pairs * count * width * hidden,
            bytes_accessed=6 * pairs * width * hidden,
            transcendentals=0,
        ),
        compiler_params=pltpu.CompilerParams(vmem_limit_bytes=40 << 20),
    )(named, rows, gain_row, *factors, *flat, *start, *after)


def final_kernel(saved_ref, upstream_ref, *refs):
    out_ref = refs[-1]
    value = saved_ref[...].astype(jnp.float32)
    inv_root = lax.rsqrt(jnp.mean(value * value, axis=1, keepdims=True) + epsilon)
    scaled = refs[0][...].astype(jnp.float32)
    for ref in refs[1:-1]:
        scaled = scaled + ref[...].astype(jnp.float32)
    unit = value * inv_root
    mean = jnp.mean(scaled * unit, axis=1, keepdims=True)
    layer_grad = upstream_ref[...].astype(jnp.float32) + inv_root * (scaled - unit * mean)
    out_ref[...] = layer_grad.astype(jnp.bfloat16)


def finish(saved_rows, upstream_rows, pieces):
    return pl.pallas_call(
        final_kernel,
        in_specs=[in_vmem] * (2 + len(pieces)),
        out_specs=in_vmem,
        out_shape=jax.ShapeDtypeStruct(saved_rows.shape, jnp.bfloat16),
        compiler_params=pltpu.CompilerParams(vmem_limit_bytes=24 << 20),
    )(saved_rows, upstream_rows, *pieces)


def line_device(
    saved_input, upstream, norm_gain, gate_weight, up_weight, down_weight, expert_ids, gate_share
):
    own = (gate_weight[0, 0], up_weight[0, 0], down_weight[0, 0])
    saved_rows, upstream_rows = saved_input[0], upstream[0]
    experts = lax.axis_size("expert")
    sections = lax.axis_size("section")
    me = lax.axis_index("expert")
    named = jnp.stack([me, me ^ 1]).astype(jnp.int32)
    swapped = jnp.stack([me ^ 1, me]).astype(jnp.int32)

    def hop(by):
        return lambda value: lax.ppermute(value, "expert", [(i, i ^ by) for i in range(experts)])

    def handed(by):
        pairs = [
            (s * experts + i, (s - 1) % sections * experts + (i ^ by))
            for s in range(sections)
            for i in range(experts)
        ]
        return lambda value: lax.ppermute(value, ("section", "expert"), pairs)

    other = tuple(hop(1)(w) for w in own)
    x_two, x_one = hop(4)(saved_rows), hop(2)(saved_rows)
    shared = shared_rows(upstream_rows, expert_ids[0], gate_share[0], experts)
    u_two, u_one = hop(4)(shared), hop(2)(shared)
    x_three = hop(2)(x_two)
    u_three = hop(2)(u_two)
    next_saved, next_upstream = handed(0)(saved_rows), handed(0)(upstream_rows)

    both = (own, other)
    narrow = jnp.bfloat16
    gain = norm_gain

    def pieces_of(names, rows, factors, weights, kind=narrow, base=None, after=()):
        return slot_pieces(names, rows, gain, factors, weights, experts, kind, base, after)

    factors = slot_factors(saved_rows, gain, (own,), [])
    here = pieces_of(named, shared, factors, (own,), jnp.float32)
    factors = slot_factors(saved_rows, gain, (other,), [here])
    here = pieces_of(swapped, shared, factors, (other,), narrow, here)
    two_factors = slot_factors(x_two, gain, both, [here])
    one_factors = slot_factors(x_one, gain, both, [two_factors[0]])
    two = pieces_of(named, u_two, two_factors, both, after=[one_factors[0]])
    one = pieces_of(named, u_one, one_factors, both, after=[two, next_saved])
    here_next = handed(0)(here)
    one_next = handed(2)(one)
    two_next = handed(4)(two)
    three_factors = slot_factors(x_three, gain, both, [one, next_upstream, here_next])
    three = pieces_of(named, u_three, three_factors, both)
    pieces = [here_next, one_next, two_next, handed(6)(three)]
    return finish(next_saved, next_upstream, pieces)[None]


def solution(mesh):
    placed = (
        P("section", "expert", None),
        P("section", "expert", None),
        P("section", None),
        P("section", "expert", None, None),
        P("section", "expert", None, None),
        P("section", "expert", None, None),
        P("section", "expert", None),
        P("section", "expert", None),
    )
    plan = line_device if mesh.shape["expert"] == 8 else routed_device
    return jax.shard_map(
        plan,
        mesh=mesh,
        in_specs=placed,
        out_specs=P("section", "expert", None),
        check_vma=False,
    )
```

```python
import functools
import jax
import jax.numpy as jnp
from jax import lax
from jax.experimental import pallas as pl
from jax.experimental.pallas import tpu as pltpu
from jax.sharding import PartitionSpec as P

epsilon = 1e-06


def shifted(value, axis, by):
    length = lax.axis_size(axis)
    return lax.ppermute(value, axis, [(i, (i + by) % length) for i in range(length)])


def slot_ranks(flat_ids, experts):
    pairs = flat_ids.shape[0]
    onehot = (flat_ids[:, None] == jnp.arange(experts, dtype=jnp.int32)[None, :]).astype(
        jnp.bfloat16
    )
    row_index = jnp.arange(pairs, dtype=jnp.int32)
    lower = (row_index[None, :] < row_index[:, None]).astype(jnp.bfloat16)
    before = jnp.dot(lower, onehot, preferred_element_type=jnp.float32)
    ranks = jnp.sum(before * onehot.astype(jnp.float32), axis=1)
    return ranks.astype(jnp.int32)


def expert_backward(inputs, grads, gate_w, up_w, down_w):
    pre_gate = jnp.dot(inputs, gate_w, preferred_element_type=jnp.float32)
    pre_up = jnp.dot(inputs, up_w, preferred_element_type=jnp.float32)
    sigmoid_gate = jax.nn.sigmoid(pre_gate)
    hidden_grad = lax.dot_general(
        grads, down_w, (((1,), (1,)), ((), ())), preferred_element_type=jnp.float32
    )
    d_gate = (hidden_grad * pre_up * sigmoid_gate * (1.0 + pre_gate * (1.0 - sigmoid_gate))).astype(
        jnp.bfloat16
    )
    d_up = (hidden_grad * pre_gate * sigmoid_gate).astype(jnp.bfloat16)
    summed = lax.dot_general(
        d_gate, gate_w, (((1,), (1,)), ((), ())), preferred_element_type=jnp.float32
    )
    summed = summed + lax.dot_general(
        d_up, up_w, (((1,), (1,)), ((), ())), preferred_element_type=jnp.float32
    )
    return summed.astype(jnp.bfloat16)


def routed_device(
    saved_input, upstream, norm_gain, gate_weight, up_weight, down_weight, expert_ids, gate_share
):
    saved_rows = saved_input[0]
    upstream_rows = upstream[0]
    gain_row = norm_gain[0]
    gate_w = gate_weight[0, 0]
    up_w = up_weight[0, 0]
    down_w = down_weight[0, 0]
    routed = expert_ids[0]
    shares = gate_share[0]
    tok_rows, top_count = routed.shape
    model_width = saved_rows.shape[1]
    experts = lax.axis_size("expert")
    capacity = max(2, 3 * tok_rows * top_count // (2 * experts))
    inputs_f = saved_rows.astype(jnp.float32)
    inv_root = lax.rsqrt(jnp.mean(inputs_f * inputs_f, axis=1, keepdims=True) + epsilon)
    unit_rows = inputs_f * inv_root
    normed = (unit_rows * gain_row[None, :]).astype(jnp.bfloat16)
    flat_ids = routed.reshape(-1)
    slot_rank = slot_ranks(flat_ids, experts)
    slot_number = (flat_ids * capacity + slot_rank).reshape(tok_rows, top_count)
    slot_index = jnp.arange(experts * capacity, dtype=jnp.int32)
    matches = slot_number[None, :, :] == slot_index[:, None, None]
    select = jnp.any(matches, axis=2).astype(jnp.bfloat16)
    slot_share = jnp.sum(jnp.where(matches, shares[None, :, :], 0.0), axis=(1, 2))
    send_inputs = jnp.dot(select, normed, preferred_element_type=jnp.float32).astype(jnp.bfloat16)
    send_inputs = send_inputs.reshape(experts, capacity, model_width)
    copied_grads = jnp.dot(select, upstream_rows, preferred_element_type=jnp.float32)
    send_grads = (
        (copied_grads * slot_share[:, None])
        .astype(jnp.bfloat16)
        .reshape(experts, capacity, model_width)
    )
    got_inputs, got_grads = (
        lax.all_to_all(send_inputs, "expert", split_axis=0, concat_axis=0, tiled=True),
        lax.all_to_all(send_grads, "expert", split_axis=0, concat_axis=0, tiled=True),
    )
    slot_count = got_inputs.shape[1]
    result_rows = expert_backward(
        got_inputs.reshape(-1, model_width),
        got_grads.reshape(-1, model_width),
        gate_w,
        up_w,
        down_w,
    )
    returned = lax.all_to_all(
        result_rows.reshape(experts, slot_count, model_width),
        "expert",
        split_axis=0,
        concat_axis=0,
        tiled=True,
    )
    normed_grad = lax.dot_general(
        select,
        returned.reshape(experts * capacity, model_width),
        (((0,), (0,)), ((), ())),
        preferred_element_type=jnp.float32,
    )
    scaled = normed_grad * gain_row[None, :]
    layer_grad = upstream_rows.astype(jnp.float32) + inv_root * (
        scaled - unit_rows * jnp.mean(scaled * unit_rows, axis=1, keepdims=True)
    )
    layer_grad = layer_grad.astype(jnp.bfloat16)
    passed = shifted(layer_grad, "section", -1)
    return passed[None]


tile = 256
in_vmem = pl.BlockSpec(memory_space=pltpu.VMEM)
in_smem = pl.BlockSpec(memory_space=pltpu.SMEM)
anywhere = pl.BlockSpec(memory_space=pl.ANY)


def tile_cut(step):
    return pl.ds(pl.multiple_of(step * tile, tile), tile)


def shared_kernel(experts, upstream_ref, ids_ref, share_ref, out_ref):
    size, width = upstream_ref.shape
    lanes = out_ref.shape[1] - width
    out_ref[:, :width] = upstream_ref[...]
    lane = lax.broadcasted_iota(jnp.int32, (size, lanes), 1)
    dense = jnp.zeros((size, lanes), jnp.float32)
    for k in range(ids_ref.shape[1]):
        hit = lax.rem(lane, experts) == ids_ref[:, k : k + 1]
        dense = dense + jnp.where(hit, share_ref[:, k : k + 1], 0.0)
    high = dense.astype(jnp.bfloat16).astype(jnp.float32)
    middle = (dense - high).astype(jnp.bfloat16).astype(jnp.float32)
    low = dense - high - middle
    parts = jnp.where(lane < experts, high, jnp.where(lane < 2 * experts, middle, low))
    out_ref[:, width:] = jnp.where(lane < 3 * experts, parts, 0.0).astype(jnp.bfloat16)


def shared_rows(upstream_rows, routed, shares, experts):
    count, width = upstream_rows.shape
    return pl.pallas_call(
        functools.partial(shared_kernel, experts),
        in_specs=[in_vmem] * 3,
        out_specs=in_vmem,
        out_shape=jax.ShapeDtypeStruct((count, width + 128), jnp.bfloat16),
        compiler_params=pltpu.CompilerParams(vmem_limit_bytes=8 << 20),
    )(upstream_rows, routed, shares)


def factors_kernel(pairs, saved_ref, gain_ref, *refs):
    weight_refs = refs[: 2 * pairs]
    gate_ref, up_ref, rows_ref = refs[-3:]
    value = saved_ref[...].astype(jnp.float32)
    inv_root = lax.rsqrt(jnp.mean(value * value, axis=1, keepdims=True) + epsilon)
    rows_ref[...] = (value * inv_root * gain_ref[...]).astype(jnp.bfloat16)

    def body(step, carry):
        cut = tile_cut(step)
        for w in range(pairs):
            inputs = rows_ref[...]
            pre_gate = jnp.dot(
                inputs, weight_refs[2 * w][:, cut], preferred_element_type=jnp.float32
            )
            pre_up = jnp.dot(
                inputs, weight_refs[2 * w + 1][:, cut], preferred_element_type=jnp.float32
            )
            sigmoid_gate = jax.nn.sigmoid(pre_gate)
            gate_ref[w, :, cut] = pre_up * sigmoid_gate * (1.0 + pre_gate * (1.0 - sigmoid_gate))
            up_ref[w, :, cut] = pre_gate * sigmoid_gate
        return carry

    lax.fori_loop(0, gate_ref.shape[2] // tile, body, 0)


def slot_factors(rows, gain_row, weights, after):
    pairs = len(weights)
    count, width = rows.shape
    hidden = weights[0][0].shape[1]
    flat = [w for gate_w, up_w, _ in weights for w in (gate_w, up_w)]
    shape = jax.ShapeDtypeStruct((pairs, count, hidden), jnp.float32)
    return pl.pallas_call(
        functools.partial(factors_kernel, pairs),
        in_specs=[in_vmem] * (2 + len(flat)) + [anywhere] * len(after),
        out_specs=[in_vmem] * 2,
        out_shape=[shape] * 2,
        scratch_shapes=[pltpu.VMEM((count, width), jnp.bfloat16)],
        cost_estimate=pl.CostEstimate(
            flops=8 * pairs * count * width * hidden,
            bytes_accessed=4 * pairs * width * hidden,
            transcendentals=pairs * count * hidden,
        ),
        compiler_params=pltpu.CompilerParams(vmem_limit_bytes=8 << 20),
    )(rows, gain_row, *flat, *after)


def share_of(rows_ref, width, experts, named):
    parts = rows_ref[:, width:].astype(jnp.float32)
    lane = lax.broadcasted_iota(jnp.int32, parts.shape, 1)
    wanted = (lax.rem(lane, experts) == named) & (lane < 3 * experts)
    return jnp.sum(jnp.where(wanted, parts, 0.0), axis=1, keepdims=True)


def turning_kernel(experts, start, named_ref, rows_ref, gain_ref, gate_ref, up_ref, *refs):
    weight_refs, refs = refs[:3], refs[3:]
    base_ref = refs[0] if start else None
    out_ref, gate_turned, up_turned, down_turned, gate_grads, up_grads = refs[-6:]
    width = out_ref.shape[1]
    hidden = gate_ref.shape[2]
    share = share_of(rows_ref, width, experts, named_ref[0])

    def grads_of(step, carry):
        cut = tile_cut(step)
        turned = weight_refs[2][cut, :].T
        down_turned[:, cut] = turned
        grad = jnp.dot(rows_ref[:, :width], turned, preferred_element_type=jnp.float32)
        grad = grad * share
        gate_grads[:, cut] = (grad * gate_ref[0, :, cut]).astype(jnp.bfloat16)
        up_grads[:, cut] = (grad * up_ref[0, :, cut]).astype(jnp.bfloat16)
        return carry

    lax.fori_loop(0, hidden // tile, grads_of, 0)

    def pieces_of(step, carry):
        cut = tile_cut(step)
        gate_tile = weight_refs[0][cut, :].T
        up_tile = weight_refs[1][cut, :].T
        gate_turned[:, cut] = gate_tile
        up_turned[:, cut] = up_tile
        total = jnp.dot(gate_grads[...], gate_tile, preferred_element_type=jnp.float32)
        total = total + jnp.dot(up_grads[...], up_tile, preferred_element_type=jnp.float32)
        total = total * gain_ref[:, cut]
        if start:
            total = total + base_ref[:, cut]
        out_ref[:, cut] = total.astype(out_ref.dtype)
        return carry

    lax.fori_loop(0, width // tile, pieces_of, 0)


def turning_pieces(named, rows, gain_row, factors, weights, experts, kind, base):
    _, count, hidden = factors[0].shape
    width = weights[0].shape[0]
    start = [] if base is None else [base]
    turned = jax.ShapeDtypeStruct((hidden, width), jnp.bfloat16)
    down_turned = jax.ShapeDtypeStruct((width, hidden), jnp.bfloat16)
    return pl.pallas_call(
        functools.partial(turning_kernel, experts, len(start)),
        in_specs=[in_smem] + [in_vmem] * (7 + len(start)),
        out_specs=[in_vmem] * 4,
        out_shape=[jax.ShapeDtypeStruct((count, width), kind), turned, turned, down_turned],
        scratch_shapes=[pltpu.VMEM((count, hidden), jnp.bfloat16)] * 2,
        cost_estimate=pl.CostEstimate(
            flops=12 * count * width * hidden,
            bytes_accessed=6 * width * hidden,
            transcendentals=0,
        ),
        compiler_params=pltpu.CompilerParams(vmem_limit_bytes=12 << 20),
    )(named, rows, gain_row, *factors, *weights, *start)


def pieces_kernel(experts, pairs, named_ref, rows_ref, gain_ref, gate_ref, up_ref, *refs):
    weight_refs = refs[: 3 * pairs]
    out_ref, gate_grads, up_grads = refs[-3:]
    width = out_ref.shape[1]
    hidden = gate_ref.shape[2]
    shares = [share_of(rows_ref, width, experts, named_ref[w]) for w in range(pairs)]

    def grads_of(step, carry):
        cut = tile_cut(step)
        for w in range(pairs):
            grad = jnp.dot(
                rows_ref[:, :width],
                weight_refs[3 * w + 2][:, cut],
                preferred_element_type=jnp.float32,
            )
            grad = grad * shares[w]
            gate_grads[w, :, cut] = (grad * gate_ref[w, :, cut]).astype(jnp.bfloat16)
            up_grads[w, :, cut] = (grad * up_ref[w, :, cut]).astype(jnp.bfloat16)
        return carry

    lax.fori_loop(0, hidden // tile, grads_of, 0)

    def pieces_of(step, carry):
        cut = tile_cut(step)
        total = None
        for w in range(pairs):
            for held, weight_ref in ((gate_grads, weight_refs[3 * w]), (up_grads, weight_refs[3 * w + 1])):
                part = jnp.dot(held[w], weight_ref[:, cut], preferred_element_type=jnp.float32)
                total = part if total is None else total + part
        out_ref[:, cut] = (total * gain_ref[:, cut]).astype(out_ref.dtype)
        return carry

    lax.fori_loop(0, width // tile, pieces_of, 0)


def slot_pieces(named, rows, gain_row, factors, weights, experts, after):
    pairs, count, hidden = factors[0].shape
    width = weights[0][0].shape[1]
    flat = [w for group in weights for w in group]
    return pl.pallas_call(
        functools.partial(pieces_kernel, experts, pairs),
        in_specs=[in_smem] + [in_vmem] * (4 + len(flat)) + [anywhere] * len(after),
        out_specs=in_vmem,
        out_shape=jax.ShapeDtypeStruct((count, width), jnp.bfloat16),
        scratch_shapes=[pltpu.VMEM((pairs, count, hidden), jnp.bfloat16)] * 2,
        cost_estimate=pl.CostEstimate(
            flops=12 * pairs * count * width * hidden,
            bytes_accessed=6 * pairs * width * hidden,
            transcendentals=0,
        ),
        compiler_params=pltpu.CompilerParams(vmem_limit_bytes=8 << 20),
    )(named, rows, gain_row, *factors, *flat, *after)


def final_kernel(saved_ref, upstream_ref, *refs):
    out_ref = refs[-1]
    value = saved_ref[...].astype(jnp.float32)
    inv_root = lax.rsqrt(jnp.mean(value * value, axis=1, keepdims=True) + epsilon)
    scaled = refs[0][...].astype(jnp.float32)
    for ref in refs[1:-1]:
        scaled = scaled + ref[...].astype(jnp.float32)
    unit = value * inv_root
    mean = jnp.mean(scaled * unit, axis=1, keepdims=True)
    layer_grad = upstream_ref[...].astype(jnp.float32) + inv_root * (scaled - unit * mean)
    out_ref[...] = layer_grad.astype(jnp.bfloat16)


def finish(saved_rows, upstream_rows, pieces):
    return pl.pallas_call(
        final_kernel,
        in_specs=[in_vmem] * (2 + len(pieces)),
        out_specs=in_vmem,
        out_shape=jax.ShapeDtypeStruct(saved_rows.shape, jnp.bfloat16),
        compiler_params=pltpu.CompilerParams(vmem_limit_bytes=8 << 20),
    )(saved_rows, upstream_rows, *pieces)


def joined_kernel(at_ends, is_end_ref, some_ref, *refs):
    out_ref = refs[-1]
    total = jnp.where(is_end_ref[0] == at_ends, some_ref[...].astype(jnp.float32), 0.0)
    for ref in refs[:-1]:
        total = total + ref[...].astype(jnp.float32)
    out_ref[...] = total.astype(out_ref.dtype)


def joined(is_end, at_ends, some, pieces, kind):
    return pl.pallas_call(
        functools.partial(joined_kernel, at_ends),
        in_specs=[in_smem] + [in_vmem] * (1 + len(pieces)),
        out_specs=in_vmem,
        out_shape=jax.ShapeDtypeStruct(some.shape, kind),
        compiler_params=pltpu.CompilerParams(vmem_limit_bytes=8 << 20),
    )(is_end, some, *pieces)


def line_device(
    saved_input, upstream, norm_gain, gate_weight, up_weight, down_weight, expert_ids, gate_share
):
    own = (gate_weight[0, 0], up_weight[0, 0], down_weight[0, 0])
    saved_rows, upstream_rows = saved_input[0], upstream[0]
    experts = lax.axis_size("expert")
    sections = lax.axis_size("section")
    me = lax.axis_index("expert")
    named = jnp.stack([me, me ^ 1]).astype(jnp.int32)
    swapped = jnp.stack([me ^ 1, me]).astype(jnp.int32)

    def hop(by):
        return lambda value: lax.ppermute(value, "expert", [(i, i ^ by) for i in range(experts)])

    def handed(by):
        pairs = [
            (s * experts + i, (s - 1) % sections * experts + (i ^ by))
            for s in range(sections)
            for i in range(experts)
        ]
        return lambda value: lax.ppermute(value, ("section", "expert"), pairs)

    other = tuple(hop(1)(w) for w in own)
    x_two, x_one = hop(4)(saved_rows), hop(2)(saved_rows)
    shared = shared_rows(upstream_rows, expert_ids[0], gate_share[0], experts)
    u_two, u_one = hop(4)(shared), hop(2)(shared)
    x_three = hop(2)(x_two)

    both = (own, other)
    gain = norm_gain
    ends = (0, 1, experts - 2, experts - 1)
    is_end = ((me < 2) | (me >= experts - 2)).astype(jnp.int32).reshape(1)

    def second_hop(value):
        pairs = []
        for s in range(sections):
            for i in range(experts):
                target = (s, i ^ 2) if i in ends else ((s - 1) % sections, i ^ 4)
                pairs.append((s * experts + i, target[0] * experts + target[1]))
        return lax.ppermute(value, ("section", "expert"), pairs)

    factors = slot_factors(saved_rows, gain, (own,), [])
    later_saved, later_upstream, _ = lax.optimization_barrier(
        (saved_rows, upstream_rows, factors[0])
    )
    next_saved, next_upstream = handed(0)(later_saved), handed(0)(later_upstream)
    here, *own_turned = turning_pieces(named, shared, gain, factors, own, experts, jnp.float32, None)
    factors = slot_factors(saved_rows, gain, (other,), [here])
    here, *other_turned = turning_pieces(
        swapped, shared, gain, factors, other, experts, jnp.bfloat16, here
    )
    turned = (own_turned, other_turned)
    two_factors = slot_factors(x_two, gain, both, [here])
    one_factors = slot_factors(x_one, gain, both, [two_factors[0], next_saved])
    u_two, one_gate = lax.optimization_barrier((u_two, one_factors[0]))
    one_factors = (one_gate, one_factors[1])
    u_three = hop(2)(u_two)
    two = slot_pieces(named, u_two, gain, two_factors, turned, experts, [one_factors[0], next_upstream])
    two_next = second_hop(two)
    here_next = handed(0)(here)
    three_factors = slot_factors(x_three, gain, both, [two])
    three = slot_pieces(named, u_three, gain, three_factors, turned, experts, [here_next])
    three = joined(is_end, 0, two_next, [three], jnp.bfloat16)
    three_next = handed(6)(three)
    one = slot_pieces(named, u_one, gain, one_factors, turned, experts, [three])
    one_next = handed(2)(one)
    summed = joined(is_end, 1, two_next, [here_next, three_next], jnp.float32)
    return finish(next_saved, next_upstream, [summed, one_next])[None]


def solution(mesh):
    placed = (
        P("section", "expert", None),
        P("section", "expert", None),
        P("section", None),
        P("section", "expert", None, None),
        P("section", "expert", None, None),
        P("section", "expert", None, None),
        P("section", "expert", None),
        P("section", "expert", None),
    )
    plan = line_device if mesh.shape["expert"] == 8 else routed_device
    return jax.shard_map(
        plan,
        mesh=mesh,
        in_specs=placed,
        out_specs=P("section", "expert", None),
        check_vma=False,
    )
```

```python
import functools
import jax
import jax.numpy as jnp
from jax import lax
from jax.experimental import pallas as pl
from jax.experimental.pallas import tpu as pltpu
from jax.sharding import PartitionSpec as P

epsilon = 1e-06


def shifted(value, axis, by):
    length = lax.axis_size(axis)
    return lax.ppermute(value, axis, [(i, (i + by) % length) for i in range(length)])


def slot_ranks(flat_ids, experts):
    pairs = flat_ids.shape[0]
    onehot = (flat_ids[:, None] == jnp.arange(experts, dtype=jnp.int32)[None, :]).astype(
        jnp.bfloat16
    )
    row_index = jnp.arange(pairs, dtype=jnp.int32)
    lower = (row_index[None, :] < row_index[:, None]).astype(jnp.bfloat16)
    before = jnp.dot(lower, onehot, preferred_element_type=jnp.float32)
    ranks = jnp.sum(before * onehot.astype(jnp.float32), axis=1)
    return ranks.astype(jnp.int32)


def expert_backward(inputs, grads, gate_w, up_w, down_w):
    pre_gate = jnp.dot(inputs, gate_w, preferred_element_type=jnp.float32)
    pre_up = jnp.dot(inputs, up_w, preferred_element_type=jnp.float32)
    sigmoid_gate = jax.nn.sigmoid(pre_gate)
    hidden_grad = lax.dot_general(
        grads, down_w, (((1,), (1,)), ((), ())), preferred_element_type=jnp.float32
    )
    d_gate = (hidden_grad * pre_up * sigmoid_gate * (1.0 + pre_gate * (1.0 - sigmoid_gate))).astype(
        jnp.bfloat16
    )
    d_up = (hidden_grad * pre_gate * sigmoid_gate).astype(jnp.bfloat16)
    summed = lax.dot_general(
        d_gate, gate_w, (((1,), (1,)), ((), ())), preferred_element_type=jnp.float32
    )
    summed = summed + lax.dot_general(
        d_up, up_w, (((1,), (1,)), ((), ())), preferred_element_type=jnp.float32
    )
    return summed.astype(jnp.bfloat16)


def routed_device(
    saved_input, upstream, norm_gain, gate_weight, up_weight, down_weight, expert_ids, gate_share
):
    saved_rows = saved_input[0]
    upstream_rows = upstream[0]
    gain_row = norm_gain[0]
    gate_w = gate_weight[0, 0]
    up_w = up_weight[0, 0]
    down_w = down_weight[0, 0]
    routed = expert_ids[0]
    shares = gate_share[0]
    tok_rows, top_count = routed.shape
    model_width = saved_rows.shape[1]
    experts = lax.axis_size("expert")
    capacity = max(2, 3 * tok_rows * top_count // (2 * experts))
    inputs_f = saved_rows.astype(jnp.float32)
    inv_root = lax.rsqrt(jnp.mean(inputs_f * inputs_f, axis=1, keepdims=True) + epsilon)
    unit_rows = inputs_f * inv_root
    normed = (unit_rows * gain_row[None, :]).astype(jnp.bfloat16)
    flat_ids = routed.reshape(-1)
    slot_rank = slot_ranks(flat_ids, experts)
    slot_number = (flat_ids * capacity + slot_rank).reshape(tok_rows, top_count)
    slot_index = jnp.arange(experts * capacity, dtype=jnp.int32)
    matches = slot_number[None, :, :] == slot_index[:, None, None]
    select = jnp.any(matches, axis=2).astype(jnp.bfloat16)
    slot_share = jnp.sum(jnp.where(matches, shares[None, :, :], 0.0), axis=(1, 2))
    send_inputs = jnp.dot(select, normed, preferred_element_type=jnp.float32).astype(jnp.bfloat16)
    send_inputs = send_inputs.reshape(experts, capacity, model_width)
    copied_grads = jnp.dot(select, upstream_rows, preferred_element_type=jnp.float32)
    send_grads = (
        (copied_grads * slot_share[:, None])
        .astype(jnp.bfloat16)
        .reshape(experts, capacity, model_width)
    )
    got_inputs, got_grads = (
        lax.all_to_all(send_inputs, "expert", split_axis=0, concat_axis=0, tiled=True),
        lax.all_to_all(send_grads, "expert", split_axis=0, concat_axis=0, tiled=True),
    )
    slot_count = got_inputs.shape[1]
    result_rows = expert_backward(
        got_inputs.reshape(-1, model_width),
        got_grads.reshape(-1, model_width),
        gate_w,
        up_w,
        down_w,
    )
    returned = lax.all_to_all(
        result_rows.reshape(experts, slot_count, model_width),
        "expert",
        split_axis=0,
        concat_axis=0,
        tiled=True,
    )
    normed_grad = lax.dot_general(
        select,
        returned.reshape(experts * capacity, model_width),
        (((0,), (0,)), ((), ())),
        preferred_element_type=jnp.float32,
    )
    scaled = normed_grad * gain_row[None, :]
    layer_grad = upstream_rows.astype(jnp.float32) + inv_root * (
        scaled - unit_rows * jnp.mean(scaled * unit_rows, axis=1, keepdims=True)
    )
    layer_grad = layer_grad.astype(jnp.bfloat16)
    passed = shifted(layer_grad, "section", -1)
    return passed[None]


tile = 256
in_vmem = pl.BlockSpec(memory_space=pltpu.VMEM)
in_smem = pl.BlockSpec(memory_space=pltpu.SMEM)
anywhere = pl.BlockSpec(memory_space=pl.ANY)


def tile_cut(step):
    return pl.ds(pl.multiple_of(step * tile, tile), tile)


def shared_kernel(experts, upstream_ref, ids_ref, share_ref, out_ref):
    size, width = upstream_ref.shape
    lanes = out_ref.shape[1] - width
    out_ref[:, :width] = upstream_ref[...]
    lane = lax.broadcasted_iota(jnp.int32, (size, lanes), 1)
    dense = jnp.zeros((size, lanes), jnp.float32)
    for k in range(ids_ref.shape[1]):
        hit = lax.rem(lane, experts) == ids_ref[:, k : k + 1]
        dense = dense + jnp.where(hit, share_ref[:, k : k + 1], 0.0)
    high = dense.astype(jnp.bfloat16).astype(jnp.float32)
    middle = (dense - high).astype(jnp.bfloat16).astype(jnp.float32)
    low = dense - high - middle
    parts = jnp.where(lane < experts, high, jnp.where(lane < 2 * experts, middle, low))
    out_ref[:, width:] = jnp.where(lane < 3 * experts, parts, 0.0).astype(jnp.bfloat16)


def shared_rows(upstream_rows, routed, shares, experts):
    count, width = upstream_rows.shape
    return pl.pallas_call(
        functools.partial(shared_kernel, experts),
        in_specs=[in_vmem] * 3,
        out_specs=in_vmem,
        out_shape=jax.ShapeDtypeStruct((count, width + 128), jnp.bfloat16),
        compiler_params=pltpu.CompilerParams(vmem_limit_bytes=8 << 20),
    )(upstream_rows, routed, shares)


def factors_kernel(pairs, saved_ref, gain_ref, *refs):
    weight_refs = refs[: 2 * pairs]
    gate_ref, up_ref, rows_ref = refs[-3:]
    value = saved_ref[...].astype(jnp.float32)
    inv_root = lax.rsqrt(jnp.mean(value * value, axis=1, keepdims=True) + epsilon)
    rows_ref[...] = (value * inv_root * gain_ref[...]).astype(jnp.bfloat16)

    def body(step, carry):
        cut = tile_cut(step)
        for w in range(pairs):
            inputs = rows_ref[...]
            pre_gate = jnp.dot(
                inputs, weight_refs[2 * w][:, cut], preferred_element_type=jnp.float32
            )
            pre_up = jnp.dot(
                inputs, weight_refs[2 * w + 1][:, cut], preferred_element_type=jnp.float32
            )
            sigmoid_gate = jax.nn.sigmoid(pre_gate)
            gate_ref[w, :, cut] = pre_up * sigmoid_gate * (1.0 + pre_gate * (1.0 - sigmoid_gate))
            up_ref[w, :, cut] = pre_gate * sigmoid_gate
        return carry

    lax.fori_loop(0, gate_ref.shape[2] // tile, body, 0)


def slot_factors(rows, gain_row, weights, after):
    pairs = len(weights)
    count, width = rows.shape
    hidden = weights[0][0].shape[1]
    flat = [w for gate_w, up_w, _ in weights for w in (gate_w, up_w)]
    shape = jax.ShapeDtypeStruct((pairs, count, hidden), jnp.float32)
    return pl.pallas_call(
        functools.partial(factors_kernel, pairs),
        in_specs=[in_vmem] * (2 + len(flat)) + [anywhere] * len(after),
        out_specs=[in_vmem] * 2,
        out_shape=[shape] * 2,
        scratch_shapes=[pltpu.VMEM((count, width), jnp.bfloat16)],
        cost_estimate=pl.CostEstimate(
            flops=8 * pairs * count * width * hidden,
            bytes_accessed=4 * pairs * width * hidden,
            transcendentals=pairs * count * hidden,
        ),
        compiler_params=pltpu.CompilerParams(vmem_limit_bytes=8 << 20),
    )(rows, gain_row, *flat, *after)


def share_of(rows_ref, width, experts, named):
    parts = rows_ref[:, width:].astype(jnp.float32)
    lane = lax.broadcasted_iota(jnp.int32, parts.shape, 1)
    wanted = (lax.rem(lane, experts) == named) & (lane < 3 * experts)
    return jnp.sum(jnp.where(wanted, parts, 0.0), axis=1, keepdims=True)


def turning_kernel(experts, start, named_ref, rows_ref, gain_ref, gate_ref, up_ref, *refs):
    weight_refs, refs = refs[:3], refs[3:]
    base_ref = refs[0] if start else None
    out_ref, gate_turned, up_turned, down_turned, gate_grads, up_grads = refs[-6:]
    width = out_ref.shape[1]
    hidden = gate_ref.shape[2]
    share = share_of(rows_ref, width, experts, named_ref[0])

    def grads_of(step, carry):
        cut = tile_cut(step)
        turned = weight_refs[2][cut, :].T
        down_turned[:, cut] = turned
        grad = jnp.dot(rows_ref[:, :width], turned, preferred_element_type=jnp.float32)
        grad = grad * share
        gate_grads[:, cut] = (grad * gate_ref[0, :, cut]).astype(jnp.bfloat16)
        up_grads[:, cut] = (grad * up_ref[0, :, cut]).astype(jnp.bfloat16)
        return carry

    lax.fori_loop(0, hidden // tile, grads_of, 0)

    def pieces_of(step, carry):
        cut = tile_cut(step)
        gate_tile = weight_refs[0][cut, :].T
        up_tile = weight_refs[1][cut, :].T
        gate_turned[:, cut] = gate_tile
        up_turned[:, cut] = up_tile
        total = jnp.dot(gate_grads[...], gate_tile, preferred_element_type=jnp.float32)
        total = total + jnp.dot(up_grads[...], up_tile, preferred_element_type=jnp.float32)
        total = total * gain_ref[:, cut]
        if start:
            total = total + base_ref[:, cut]
        out_ref[:, cut] = total.astype(out_ref.dtype)
        return carry

    lax.fori_loop(0, width // tile, pieces_of, 0)


def turning_pieces(named, rows, gain_row, factors, weights, experts, kind, base):
    _, count, hidden = factors[0].shape
    width = weights[0].shape[0]
    start = [] if base is None else [base]
    turned = jax.ShapeDtypeStruct((hidden, width), jnp.bfloat16)
    down_turned = jax.ShapeDtypeStruct((width, hidden), jnp.bfloat16)
    return pl.pallas_call(
        functools.partial(turning_kernel, experts, len(start)),
        in_specs=[in_smem] + [in_vmem] * (7 + len(start)),
        out_specs=[in_vmem] * 4,
        out_shape=[jax.ShapeDtypeStruct((count, width), kind), turned, turned, down_turned],
        scratch_shapes=[pltpu.VMEM((count, hidden), jnp.bfloat16)] * 2,
        cost_estimate=pl.CostEstimate(
            flops=12 * count * width * hidden,
            bytes_accessed=6 * width * hidden,
            transcendentals=0,
        ),
        compiler_params=pltpu.CompilerParams(vmem_limit_bytes=12 << 20),
    )(named, rows, gain_row, *factors, *weights, *start)


def pieces_kernel(experts, pairs, named_ref, rows_ref, gain_ref, gate_ref, up_ref, *refs):
    weight_refs = refs[: 3 * pairs]
    out_ref, gate_grads, up_grads = refs[-3:]
    width = out_ref.shape[1]
    hidden = gate_ref.shape[2]
    shares = [share_of(rows_ref, width, experts, named_ref[w]) for w in range(pairs)]

    def grads_of(step, carry):
        cut = tile_cut(step)
        for w in range(pairs):
            grad = jnp.dot(
                rows_ref[:, :width],
                weight_refs[3 * w + 2][:, cut],
                preferred_element_type=jnp.float32,
            )
            grad = grad * shares[w]
            gate_grads[w, :, cut] = (grad * gate_ref[w, :, cut]).astype(jnp.bfloat16)
            up_grads[w, :, cut] = (grad * up_ref[w, :, cut]).astype(jnp.bfloat16)
        return carry

    lax.fori_loop(0, hidden // tile, grads_of, 0)

    def pieces_of(step, carry):
        cut = tile_cut(step)
        total = None
        for w in range(pairs):
            for held, weight_ref in ((gate_grads, weight_refs[3 * w]), (up_grads, weight_refs[3 * w + 1])):
                part = jnp.dot(held[w], weight_ref[:, cut], preferred_element_type=jnp.float32)
                total = part if total is None else total + part
        out_ref[:, cut] = (total * gain_ref[:, cut]).astype(out_ref.dtype)
        return carry

    lax.fori_loop(0, width // tile, pieces_of, 0)


def slot_pieces(named, rows, gain_row, factors, weights, experts, after):
    pairs, count, hidden = factors[0].shape
    width = weights[0][0].shape[1]
    flat = [w for group in weights for w in group]
    return pl.pallas_call(
        functools.partial(pieces_kernel, experts, pairs),
        in_specs=[in_smem] + [in_vmem] * (4 + len(flat)) + [anywhere] * len(after),
        out_specs=in_vmem,
        out_shape=jax.ShapeDtypeStruct((count, width), jnp.bfloat16),
        scratch_shapes=[pltpu.VMEM((pairs, count, hidden), jnp.bfloat16)] * 2,
        cost_estimate=pl.CostEstimate(
            flops=12 * pairs * count * width * hidden,
            bytes_accessed=6 * pairs * width * hidden,
            transcendentals=0,
        ),
        compiler_params=pltpu.CompilerParams(vmem_limit_bytes=8 << 20),
    )(named, rows, gain_row, *factors, *flat, *after)


def final_kernel(saved_ref, upstream_ref, *refs):
    out_ref = refs[-1]
    value = saved_ref[...].astype(jnp.float32)
    inv_root = lax.rsqrt(jnp.mean(value * value, axis=1, keepdims=True) + epsilon)
    scaled = refs[0][...].astype(jnp.float32)
    for ref in refs[1:-1]:
        scaled = scaled + ref[...].astype(jnp.float32)
    unit = value * inv_root
    mean = jnp.mean(scaled * unit, axis=1, keepdims=True)
    layer_grad = upstream_ref[...].astype(jnp.float32) + inv_root * (scaled - unit * mean)
    out_ref[...] = layer_grad.astype(jnp.bfloat16)


def finish(saved_rows, upstream_rows, pieces):
    return pl.pallas_call(
        final_kernel,
        in_specs=[in_vmem] * (2 + len(pieces)),
        out_specs=in_vmem,
        out_shape=jax.ShapeDtypeStruct(saved_rows.shape, jnp.bfloat16),
        compiler_params=pltpu.CompilerParams(vmem_limit_bytes=8 << 20),
    )(saved_rows, upstream_rows, *pieces)


def joined_kernel(at_ends, is_end_ref, some_ref, *refs):
    out_ref = refs[-1]
    total = jnp.where(is_end_ref[0] == at_ends, some_ref[...].astype(jnp.float32), 0.0)
    for ref in refs[:-1]:
        total = total + ref[...].astype(jnp.float32)
    out_ref[...] = total.astype(out_ref.dtype)


def joined(is_end, at_ends, some, pieces, kind):
    return pl.pallas_call(
        functools.partial(joined_kernel, at_ends),
        in_specs=[in_smem] + [in_vmem] * (1 + len(pieces)),
        out_specs=in_vmem,
        out_shape=jax.ShapeDtypeStruct(some.shape, kind),
        compiler_params=pltpu.CompilerParams(vmem_limit_bytes=8 << 20),
    )(is_end, some, *pieces)


def line_device(
    saved_input, upstream, norm_gain, gate_weight, up_weight, down_weight, expert_ids, gate_share
):
    own = (gate_weight[0, 0], up_weight[0, 0], down_weight[0, 0])
    saved_rows, upstream_rows = saved_input[0], upstream[0]
    experts = lax.axis_size("expert")
    sections = lax.axis_size("section")
    me = lax.axis_index("expert")
    named = jnp.stack([me, me ^ 1]).astype(jnp.int32)
    swapped = jnp.stack([me ^ 1, me]).astype(jnp.int32)

    def hop(by):
        return lambda value: lax.ppermute(value, "expert", [(i, i ^ by) for i in range(experts)])

    def handed(by):
        pairs = [
            (s * experts + i, (s - 1) % sections * experts + (i ^ by))
            for s in range(sections)
            for i in range(experts)
        ]
        return lambda value: lax.ppermute(value, ("section", "expert"), pairs)

    shared = shared_rows(upstream_rows, expert_ids[0], gate_share[0], experts)
    x_two, x_one = hop(4)(saved_rows), hop(2)(saved_rows)
    gate_other, up_other = hop(1)(own[0]), hop(1)(own[1])
    u_two = hop(4)(shared)
    gain = norm_gain
    ends = (0, 1, experts - 2, experts - 1)
    is_end = ((me < 2) | (me >= experts - 2)).astype(jnp.int32).reshape(1)

    def second_hop(value):
        pairs = []
        for s in range(sections):
            for i in range(experts):
                target = (s, i ^ 2) if i in ends else ((s - 1) % sections, i ^ 4)
                pairs.append((s * experts + i, target[0] * experts + target[1]))
        return lax.ppermute(value, ("section", "expert"), pairs)

    own_factors = slot_factors(saved_rows, gain, (own,), [])
    later, gate = lax.optimization_barrier((shared, own_factors[0]))
    own_factors = (gate, own_factors[1])
    other = (gate_other, up_other, hop(1)(own[2]))
    u_one = hop(2)(later)
    other_factors = slot_factors(saved_rows, gain, (other,), [gate])
    both = (own, other)
    here, *own_turned = turning_pieces(
        named, shared, gain, own_factors, own, experts, jnp.float32, None
    )
    here, *other_turned = turning_pieces(
        swapped, shared, gain, other_factors, other, experts, jnp.bfloat16, here
    )
    turned = (own_turned, other_turned)
    x_three = hop(2)(x_two)
    two_factors = slot_factors(x_two, gain, both, [here])
    one_factors = slot_factors(x_one, gain, both, [two_factors[0]])
    three_factors = slot_factors(x_three, gain, both, [one_factors[0]])
    u_two, saved_later, three_gate = lax.optimization_barrier(
        (u_two, saved_rows, three_factors[0])
    )
    three_factors = (three_gate, three_factors[1])
    next_saved = handed(0)(saved_later)
    here_next = handed(0)(here)
    u_three = hop(2)(u_two)
    two = slot_pieces(named, u_two, gain, two_factors, turned, experts, [here_next])
    two_next = second_hop(two)
    upstream_later, two = lax.optimization_barrier((upstream_rows, two))
    next_upstream = handed(0)(upstream_later)
    one = slot_pieces(named, u_one, gain, one_factors, turned, experts, [two, next_saved])
    one_next = handed(2)(one)
    three = slot_pieces(named, u_three, gain, three_factors, turned, experts, [one, next_upstream])
    three = joined(is_end, 0, two_next, [three], jnp.bfloat16)
    summed = joined(is_end, 1, two_next, [here_next, one_next], jnp.float32)
    three_next = handed(6)(three)
    return finish(next_saved, next_upstream, [summed, three_next])[None]


def solution(mesh):
    placed = (
        P("section", "expert", None),
        P("section", "expert", None),
        P("section", None),
        P("section", "expert", None, None),
        P("section", "expert", None, None),
        P("section", "expert", None, None),
        P("section", "expert", None),
        P("section", "expert", None),
    )
    plan = line_device if mesh.shape["expert"] == 8 else routed_device
    return jax.shard_map(
        plan,
        mesh=mesh,
        in_specs=placed,
        out_specs=P("section", "expert", None),
        check_vma=False,
    )
```

```python
import functools
import jax
import jax.numpy as jnp
from jax import lax
from jax.experimental import pallas as pl
from jax.experimental.pallas import tpu as pltpu
from jax.sharding import PartitionSpec as P

epsilon = 1e-06


def shifted(value, axis, by):
    length = lax.axis_size(axis)
    return lax.ppermute(value, axis, [(i, (i + by) % length) for i in range(length)])


def slot_ranks(flat_ids, experts):
    pairs = flat_ids.shape[0]
    onehot = (flat_ids[:, None] == jnp.arange(experts, dtype=jnp.int32)[None, :]).astype(
        jnp.bfloat16
    )
    row_index = jnp.arange(pairs, dtype=jnp.int32)
    lower = (row_index[None, :] < row_index[:, None]).astype(jnp.bfloat16)
    before = jnp.dot(lower, onehot, preferred_element_type=jnp.float32)
    ranks = jnp.sum(before * onehot.astype(jnp.float32), axis=1)
    return ranks.astype(jnp.int32)


def expert_backward(inputs, grads, gate_w, up_w, down_w):
    pre_gate = jnp.dot(inputs, gate_w, preferred_element_type=jnp.float32)
    pre_up = jnp.dot(inputs, up_w, preferred_element_type=jnp.float32)
    sigmoid_gate = jax.nn.sigmoid(pre_gate)
    hidden_grad = lax.dot_general(
        grads, down_w, (((1,), (1,)), ((), ())), preferred_element_type=jnp.float32
    )
    d_gate = (hidden_grad * pre_up * sigmoid_gate * (1.0 + pre_gate * (1.0 - sigmoid_gate))).astype(
        jnp.bfloat16
    )
    d_up = (hidden_grad * pre_gate * sigmoid_gate).astype(jnp.bfloat16)
    summed = lax.dot_general(
        d_gate, gate_w, (((1,), (1,)), ((), ())), preferred_element_type=jnp.float32
    )
    summed = summed + lax.dot_general(
        d_up, up_w, (((1,), (1,)), ((), ())), preferred_element_type=jnp.float32
    )
    return summed.astype(jnp.bfloat16)


def routed_device(
    saved_input, upstream, norm_gain, gate_weight, up_weight, down_weight, expert_ids, gate_share
):
    saved_rows = saved_input[0]
    upstream_rows = upstream[0]
    gain_row = norm_gain[0]
    gate_w = gate_weight[0, 0]
    up_w = up_weight[0, 0]
    down_w = down_weight[0, 0]
    routed = expert_ids[0]
    shares = gate_share[0]
    tok_rows, top_count = routed.shape
    model_width = saved_rows.shape[1]
    experts = lax.axis_size("expert")
    capacity = max(2, 3 * tok_rows * top_count // (2 * experts))
    inputs_f = saved_rows.astype(jnp.float32)
    inv_root = lax.rsqrt(jnp.mean(inputs_f * inputs_f, axis=1, keepdims=True) + epsilon)
    unit_rows = inputs_f * inv_root
    normed = (unit_rows * gain_row[None, :]).astype(jnp.bfloat16)
    flat_ids = routed.reshape(-1)
    slot_rank = slot_ranks(flat_ids, experts)
    slot_number = (flat_ids * capacity + slot_rank).reshape(tok_rows, top_count)
    slot_index = jnp.arange(experts * capacity, dtype=jnp.int32)
    matches = slot_number[None, :, :] == slot_index[:, None, None]
    select = jnp.any(matches, axis=2).astype(jnp.bfloat16)
    slot_share = jnp.sum(jnp.where(matches, shares[None, :, :], 0.0), axis=(1, 2))
    send_inputs = jnp.dot(select, normed, preferred_element_type=jnp.float32).astype(jnp.bfloat16)
    send_inputs = send_inputs.reshape(experts, capacity, model_width)
    copied_grads = jnp.dot(select, upstream_rows, preferred_element_type=jnp.float32)
    send_grads = (
        (copied_grads * slot_share[:, None])
        .astype(jnp.bfloat16)
        .reshape(experts, capacity, model_width)
    )
    got_inputs, got_grads = (
        lax.all_to_all(send_inputs, "expert", split_axis=0, concat_axis=0, tiled=True),
        lax.all_to_all(send_grads, "expert", split_axis=0, concat_axis=0, tiled=True),
    )
    slot_count = got_inputs.shape[1]
    result_rows = expert_backward(
        got_inputs.reshape(-1, model_width),
        got_grads.reshape(-1, model_width),
        gate_w,
        up_w,
        down_w,
    )
    returned = lax.all_to_all(
        result_rows.reshape(experts, slot_count, model_width),
        "expert",
        split_axis=0,
        concat_axis=0,
        tiled=True,
    )
    normed_grad = lax.dot_general(
        select,
        returned.reshape(experts * capacity, model_width),
        (((0,), (0,)), ((), ())),
        preferred_element_type=jnp.float32,
    )
    scaled = normed_grad * gain_row[None, :]
    layer_grad = upstream_rows.astype(jnp.float32) + inv_root * (
        scaled - unit_rows * jnp.mean(scaled * unit_rows, axis=1, keepdims=True)
    )
    layer_grad = layer_grad.astype(jnp.bfloat16)
    passed = shifted(layer_grad, "section", -1)
    return passed[None]


tile = 256
in_vmem = pl.BlockSpec(memory_space=pltpu.VMEM)
anywhere = pl.BlockSpec(memory_space=pl.ANY)


def tile_cut(step):
    return pl.ds(pl.multiple_of(step * tile, tile), tile)


def shared_kernel(experts, upstream_ref, ids_ref, share_ref, out_ref):
    size, width = upstream_ref.shape
    lanes = out_ref.shape[1] - width
    top = ids_ref.shape[0]
    out_ref[:, :width] = upstream_ref[...]
    both = jnp.concatenate([ids_ref[...].astype(jnp.float32), share_ref[...]], axis=0).T
    lane = lax.broadcasted_iota(jnp.int32, (size, lanes), 1)
    expert = lax.rem(lane, experts).astype(jnp.float32)
    dense = jnp.zeros((size, lanes), jnp.float32)
    for k in range(top):
        hit = expert == both[:, k : k + 1]
        dense = dense + jnp.where(hit, both[:, top + k : top + k + 1], 0.0)
    high = dense.astype(jnp.bfloat16).astype(jnp.float32)
    middle = (dense - high).astype(jnp.bfloat16).astype(jnp.float32)
    low = dense - high - middle
    parts = jnp.where(lane < experts, high, jnp.where(lane < 2 * experts, middle, low))
    out_ref[:, width:] = jnp.where(lane < 3 * experts, parts, 0.0).astype(jnp.bfloat16)


def shared_rows(upstream_rows, routed, shares, experts):
    count, width = upstream_rows.shape
    return pl.pallas_call(
        functools.partial(shared_kernel, experts),
        in_specs=[in_vmem] * 3,
        out_specs=in_vmem,
        out_shape=jax.ShapeDtypeStruct((count, width + 128), jnp.bfloat16),
        compiler_params=pltpu.CompilerParams(vmem_limit_bytes=8 << 20),
    )(upstream_rows, routed, shares)


def factors_kernel(pairs, saved_ref, gain_ref, *refs):
    weight_refs = refs[: 2 * pairs]
    gate_ref, up_ref, rows_ref = refs[-3:]
    value = saved_ref[...].astype(jnp.float32)
    inv_root = lax.rsqrt(jnp.mean(value * value, axis=1, keepdims=True) + epsilon)
    rows_ref[...] = (value * inv_root * gain_ref[...]).astype(jnp.bfloat16)

    def body(step, carry):
        cut = tile_cut(step)
        for w in range(pairs):
            inputs = rows_ref[...]
            pre_gate = jnp.dot(
                inputs, weight_refs[2 * w][:, cut], preferred_element_type=jnp.float32
            )
            pre_up = jnp.dot(
                inputs, weight_refs[2 * w + 1][:, cut], preferred_element_type=jnp.float32
            )
            sigmoid_gate = jax.nn.sigmoid(pre_gate)
            gate_ref[w, :, cut] = pre_up * sigmoid_gate * (1.0 + pre_gate * (1.0 - sigmoid_gate))
            up_ref[w, :, cut] = pre_gate * sigmoid_gate
        return carry

    lax.fori_loop(0, gate_ref.shape[2] // tile, body, 0)


def slot_factors(rows, gain_row, weights, after):
    pairs = len(weights)
    count, width = rows.shape
    hidden = weights[0][0].shape[1]
    flat = [w for gate_w, up_w, _ in weights for w in (gate_w, up_w)]
    shape = jax.ShapeDtypeStruct((pairs, count, hidden), jnp.float32)
    return pl.pallas_call(
        functools.partial(factors_kernel, pairs),
        in_specs=[in_vmem] * (2 + len(flat)) + [anywhere] * len(after),
        out_specs=[in_vmem] * 2,
        out_shape=[shape] * 2,
        scratch_shapes=[pltpu.VMEM((count, width), jnp.bfloat16)],
        cost_estimate=pl.CostEstimate(
            flops=8 * pairs * count * width * hidden,
            bytes_accessed=4 * pairs * width * hidden,
            transcendentals=pairs * count * hidden,
        ),
        compiler_params=pltpu.CompilerParams(vmem_limit_bytes=8 << 20),
    )(rows, gain_row, *flat, *after)


def share_of(rows_ref, width, experts, flip):
    named = lax.axis_index("expert") ^ flip
    parts = rows_ref[:, width:].astype(jnp.float32)
    lane = lax.broadcasted_iota(jnp.int32, parts.shape, 1)
    wanted = (lax.rem(lane, experts) == named) & (lane < 3 * experts)
    return jnp.sum(jnp.where(wanted, parts, 0.0), axis=1, keepdims=True)


def turning_kernel(experts, start, flip, rows_ref, gain_ref, gate_ref, up_ref, *refs):
    weight_refs, refs = refs[:3], refs[3:]
    base_ref = refs[0] if start else None
    out_ref, gate_turned, up_turned, down_turned, gate_grads, up_grads = refs[-6:]
    width = out_ref.shape[1]
    hidden = gate_ref.shape[2]
    share = share_of(rows_ref, width, experts, flip)

    def grads_of(step, carry):
        cut = tile_cut(step)
        turned = weight_refs[2][cut, :].T
        down_turned[:, cut] = turned
        grad = jnp.dot(rows_ref[:, :width], turned, preferred_element_type=jnp.float32)
        grad = grad * share
        gate_grads[:, cut] = (grad * gate_ref[0, :, cut]).astype(jnp.bfloat16)
        up_grads[:, cut] = (grad * up_ref[0, :, cut]).astype(jnp.bfloat16)
        return carry

    lax.fori_loop(0, hidden // tile, grads_of, 0)

    def pieces_of(step, carry):
        cut = tile_cut(step)
        gate_tile = weight_refs[0][cut, :].T
        up_tile = weight_refs[1][cut, :].T
        gate_turned[:, cut] = gate_tile
        up_turned[:, cut] = up_tile
        total = jnp.dot(gate_grads[...], gate_tile, preferred_element_type=jnp.float32)
        total = total + jnp.dot(up_grads[...], up_tile, preferred_element_type=jnp.float32)
        total = total * gain_ref[:, cut]
        if start:
            total = total + base_ref[:, cut]
        out_ref[:, cut] = total.astype(out_ref.dtype)
        return carry

    lax.fori_loop(0, width // tile, pieces_of, 0)


def turning_pieces(flip, rows, gain_row, factors, weights, experts, kind, base):
    _, count, hidden = factors[0].shape
    width = weights[0].shape[0]
    start = [] if base is None else [base]
    turned = jax.ShapeDtypeStruct((hidden, width), jnp.bfloat16)
    down_turned = jax.ShapeDtypeStruct((width, hidden), jnp.bfloat16)
    return pl.pallas_call(
        functools.partial(turning_kernel, experts, len(start), flip),
        in_specs=[in_vmem] * (7 + len(start)),
        out_specs=[in_vmem] * 4,
        out_shape=[jax.ShapeDtypeStruct((count, width), kind), turned, turned, down_turned],
        scratch_shapes=[pltpu.VMEM((count, hidden), jnp.bfloat16)] * 2,
        cost_estimate=pl.CostEstimate(
            flops=12 * count * width * hidden,
            bytes_accessed=6 * width * hidden,
            transcendentals=0,
        ),
        compiler_params=pltpu.CompilerParams(vmem_limit_bytes=12 << 20),
    )(rows, gain_row, *factors, *weights, *start)


def pieces_kernel(experts, pairs, rows_ref, gain_ref, gate_ref, up_ref, *refs):
    weight_refs = refs[: 3 * pairs]
    out_ref, gate_grads, up_grads = refs[-3:]
    width = out_ref.shape[1]
    hidden = gate_ref.shape[2]
    shares = [share_of(rows_ref, width, experts, w) for w in range(pairs)]

    def grads_of(step, carry):
        cut = tile_cut(step)
        for w in range(pairs):
            grad = jnp.dot(
                rows_ref[:, :width],
                weight_refs[3 * w + 2][:, cut],
                preferred_element_type=jnp.float32,
            )
            grad = grad * shares[w]
            gate_grads[w, :, cut] = (grad * gate_ref[w, :, cut]).astype(jnp.bfloat16)
            up_grads[w, :, cut] = (grad * up_ref[w, :, cut]).astype(jnp.bfloat16)
        return carry

    lax.fori_loop(0, hidden // tile, grads_of, 0)

    def pieces_of(step, carry):
        cut = tile_cut(step)
        total = None
        for w in range(pairs):
            for held, weight_ref in ((gate_grads, weight_refs[3 * w]), (up_grads, weight_refs[3 * w + 1])):
                part = jnp.dot(held[w], weight_ref[:, cut], preferred_element_type=jnp.float32)
                total = part if total is None else total + part
        out_ref[:, cut] = (total * gain_ref[:, cut]).astype(out_ref.dtype)
        return carry

    lax.fori_loop(0, width // tile, pieces_of, 0)


def slot_pieces(rows, gain_row, factors, weights, experts, after):
    pairs, count, hidden = factors[0].shape
    width = weights[0][0].shape[1]
    flat = [w for group in weights for w in group]
    return pl.pallas_call(
        functools.partial(pieces_kernel, experts, pairs),
        in_specs=[in_vmem] * (4 + len(flat)) + [anywhere] * len(after),
        out_specs=in_vmem,
        out_shape=jax.ShapeDtypeStruct((count, width), jnp.bfloat16),
        scratch_shapes=[pltpu.VMEM((pairs, count, hidden), jnp.bfloat16)] * 2,
        cost_estimate=pl.CostEstimate(
            flops=12 * pairs * count * width * hidden,
            bytes_accessed=6 * pairs * width * hidden,
            transcendentals=0,
        ),
        compiler_params=pltpu.CompilerParams(vmem_limit_bytes=8 << 20),
    )(rows, gain_row, *factors, *flat, *after)


def final_kernel(saved_ref, upstream_ref, *refs):
    out_ref = refs[-1]
    value = saved_ref[...].astype(jnp.float32)
    inv_root = lax.rsqrt(jnp.mean(value * value, axis=1, keepdims=True) + epsilon)
    scaled = refs[0][...].astype(jnp.float32)
    for ref in refs[1:-1]:
        scaled = scaled + ref[...].astype(jnp.float32)
    unit = value * inv_root
    mean = jnp.mean(scaled * unit, axis=1, keepdims=True)
    layer_grad = upstream_ref[...].astype(jnp.float32) + inv_root * (scaled - unit * mean)
    out_ref[...] = layer_grad.astype(jnp.bfloat16)


def finish(saved_rows, upstream_rows, pieces):
    return pl.pallas_call(
        final_kernel,
        in_specs=[in_vmem] * (2 + len(pieces)),
        out_specs=in_vmem,
        out_shape=jax.ShapeDtypeStruct(saved_rows.shape, jnp.bfloat16),
        compiler_params=pltpu.CompilerParams(vmem_limit_bytes=8 << 20),
    )(saved_rows, upstream_rows, *pieces)


def joined_kernel(experts, at_ends, some_ref, *refs):
    out_ref = refs[-1]
    me = lax.axis_index("expert")
    is_end = ((me < 2) | (me >= experts - 2)).astype(jnp.int32)
    total = jnp.where(is_end == at_ends, some_ref[...].astype(jnp.float32), 0.0)
    for ref in refs[:-1]:
        total = total + ref[...].astype(jnp.float32)
    out_ref[...] = total.astype(out_ref.dtype)


def joined(experts, at_ends, some, pieces, kind):
    return pl.pallas_call(
        functools.partial(joined_kernel, experts, at_ends),
        in_specs=[in_vmem] * (1 + len(pieces)),
        out_specs=in_vmem,
        out_shape=jax.ShapeDtypeStruct(some.shape, kind),
        compiler_params=pltpu.CompilerParams(vmem_limit_bytes=8 << 20),
    )(some, *pieces)


def line_device(
    saved_input, upstream, norm_gain, gate_weight, up_weight, down_weight, expert_ids, gate_share
):
    own = (gate_weight[0, 0], up_weight[0, 0], down_weight[0, 0])
    saved_rows, upstream_rows = saved_input[0], upstream[0]
    experts = lax.axis_size("expert")
    sections = lax.axis_size("section")

    def hop(by):
        return lambda value: lax.ppermute(value, "expert", [(i, i ^ by) for i in range(experts)])

    def handed(by):
        pairs = [
            (s * experts + i, (s - 1) % sections * experts + (i ^ by))
            for s in range(sections)
            for i in range(experts)
        ]
        return lambda value: lax.ppermute(value, ("section", "expert"), pairs)

    shared = shared_rows(upstream_rows, expert_ids[0].T, gate_share[0].T, experts)
    x_two, x_one = hop(4)(saved_rows), hop(2)(saved_rows)
    gate_other, up_other = hop(1)(own[0]), hop(1)(own[1])
    u_two = hop(4)(shared)
    gain = norm_gain
    ends = (0, 1, experts - 2, experts - 1)

    def second_hop(value):
        pairs = []
        for s in range(sections):
            for i in range(experts):
                target = (s, i ^ 2) if i in ends else ((s - 1) % sections, i ^ 4)
                pairs.append((s * experts + i, target[0] * experts + target[1]))
        return lax.ppermute(value, ("section", "expert"), pairs)

    own_factors = slot_factors(saved_rows, gain, (own,), [])
    later, gate = lax.optimization_barrier((shared, own_factors[0]))
    own_factors = (gate, own_factors[1])
    other = (gate_other, up_other, hop(1)(own[2]))
    u_one = hop(2)(later)
    other_factors = slot_factors(saved_rows, gain, (other,), [gate])
    both = (own, other)
    here, *own_turned = turning_pieces(
        0, shared, gain, own_factors, own, experts, jnp.float32, None
    )
    here, *other_turned = turning_pieces(
        1, shared, gain, other_factors, other, experts, jnp.bfloat16, here
    )
    turned = (own_turned, other_turned)
    x_three = hop(2)(x_two)
    two_factors = slot_factors(x_two, gain, both, [here])
    one_factors = slot_factors(x_one, gain, both, [two_factors[0]])
    three_factors = slot_factors(x_three, gain, both, [one_factors[0]])
    u_two, saved_later, three_gate = lax.optimization_barrier(
        (u_two, saved_rows, three_factors[0])
    )
    three_factors = (three_gate, three_factors[1])
    next_saved = handed(0)(saved_later)
    here_next = handed(0)(here)
    u_three = hop(2)(u_two)
    two = slot_pieces(u_two, gain, two_factors, turned, experts, [here_next])
    two_next = second_hop(two)
    upstream_later, two = lax.optimization_barrier((upstream_rows, two))
    next_upstream = handed(0)(upstream_later)
    one = slot_pieces(u_one, gain, one_factors, turned, experts, [two])
    one_next = handed(2)(one)
    three = slot_pieces(u_three, gain, three_factors, turned, experts, [one, next_saved])
    three = joined(experts, 0, two_next, [three], jnp.bfloat16)
    summed = joined(experts, 1, two_next, [here_next, one_next], jnp.float32)
    three_next = handed(6)(three)
    return finish(next_saved, next_upstream, [summed, three_next])[None]


def solution(mesh):
    placed = (
        P("section", "expert", None),
        P("section", "expert", None),
        P("section", None),
        P("section", "expert", None, None),
        P("section", "expert", None, None),
        P("section", "expert", None, None),
        P("section", "expert", None),
        P("section", "expert", None),
    )
    plan = line_device if mesh.shape["expert"] == 8 else routed_device
    return jax.shard_map(
        plan,
        mesh=mesh,
        in_specs=placed,
        out_specs=P("section", "expert", None),
        check_vma=False,
    )
```

```python
import functools
import jax
import jax.numpy as jnp
from jax import lax
from jax.experimental import pallas as pl
from jax.experimental.pallas import tpu as pltpu
from jax.sharding import PartitionSpec as P

epsilon = 1e-06


def shifted(value, axis, by):
    length = lax.axis_size(axis)
    return lax.ppermute(value, axis, [(i, (i + by) % length) for i in range(length)])


def slot_ranks(flat_ids, experts):
    pairs = flat_ids.shape[0]
    onehot = (flat_ids[:, None] == jnp.arange(experts, dtype=jnp.int32)[None, :]).astype(
        jnp.bfloat16
    )
    row_index = jnp.arange(pairs, dtype=jnp.int32)
    lower = (row_index[None, :] < row_index[:, None]).astype(jnp.bfloat16)
    before = jnp.dot(lower, onehot, preferred_element_type=jnp.float32)
    ranks = jnp.sum(before * onehot.astype(jnp.float32), axis=1)
    return ranks.astype(jnp.int32)


def expert_backward(inputs, grads, gate_w, up_w, down_w):
    pre_gate = jnp.dot(inputs, gate_w, preferred_element_type=jnp.float32)
    pre_up = jnp.dot(inputs, up_w, preferred_element_type=jnp.float32)
    sigmoid_gate = jax.nn.sigmoid(pre_gate)
    hidden_grad = lax.dot_general(
        grads, down_w, (((1,), (1,)), ((), ())), preferred_element_type=jnp.float32
    )
    d_gate = (hidden_grad * pre_up * sigmoid_gate * (1.0 + pre_gate * (1.0 - sigmoid_gate))).astype(
        jnp.bfloat16
    )
    d_up = (hidden_grad * pre_gate * sigmoid_gate).astype(jnp.bfloat16)
    summed = lax.dot_general(
        d_gate, gate_w, (((1,), (1,)), ((), ())), preferred_element_type=jnp.float32
    )
    summed = summed + lax.dot_general(
        d_up, up_w, (((1,), (1,)), ((), ())), preferred_element_type=jnp.float32
    )
    return summed.astype(jnp.bfloat16)


def routed_device(
    saved_input, upstream, norm_gain, gate_weight, up_weight, down_weight, expert_ids, gate_share
):
    saved_rows = saved_input[0]
    upstream_rows = upstream[0]
    gain_row = norm_gain[0]
    gate_w = gate_weight[0, 0]
    up_w = up_weight[0, 0]
    down_w = down_weight[0, 0]
    routed = expert_ids[0]
    shares = gate_share[0]
    tok_rows, top_count = routed.shape
    model_width = saved_rows.shape[1]
    experts = lax.axis_size("expert")
    capacity = max(2, 3 * tok_rows * top_count // (2 * experts))
    inputs_f = saved_rows.astype(jnp.float32)
    inv_root = lax.rsqrt(jnp.mean(inputs_f * inputs_f, axis=1, keepdims=True) + epsilon)
    unit_rows = inputs_f * inv_root
    normed = (unit_rows * gain_row[None, :]).astype(jnp.bfloat16)
    flat_ids = routed.reshape(-1)
    slot_rank = slot_ranks(flat_ids, experts)
    slot_number = (flat_ids * capacity + slot_rank).reshape(tok_rows, top_count)
    slot_index = jnp.arange(experts * capacity, dtype=jnp.int32)
    matches = slot_number[None, :, :] == slot_index[:, None, None]
    select = jnp.any(matches, axis=2).astype(jnp.bfloat16)
    slot_share = jnp.sum(jnp.where(matches, shares[None, :, :], 0.0), axis=(1, 2))
    send_inputs = jnp.dot(select, normed, preferred_element_type=jnp.float32).astype(jnp.bfloat16)
    send_inputs = send_inputs.reshape(experts, capacity, model_width)
    copied_grads = jnp.dot(select, upstream_rows, preferred_element_type=jnp.float32)
    send_grads = (
        (copied_grads * slot_share[:, None])
        .astype(jnp.bfloat16)
        .reshape(experts, capacity, model_width)
    )
    got_inputs, got_grads = (
        lax.all_to_all(send_inputs, "expert", split_axis=0, concat_axis=0, tiled=True),
        lax.all_to_all(send_grads, "expert", split_axis=0, concat_axis=0, tiled=True),
    )
    slot_count = got_inputs.shape[1]
    result_rows = expert_backward(
        got_inputs.reshape(-1, model_width),
        got_grads.reshape(-1, model_width),
        gate_w,
        up_w,
        down_w,
    )
    returned = lax.all_to_all(
        result_rows.reshape(experts, slot_count, model_width),
        "expert",
        split_axis=0,
        concat_axis=0,
        tiled=True,
    )
    normed_grad = lax.dot_general(
        select,
        returned.reshape(experts * capacity, model_width),
        (((0,), (0,)), ((), ())),
        preferred_element_type=jnp.float32,
    )
    scaled = normed_grad * gain_row[None, :]
    layer_grad = upstream_rows.astype(jnp.float32) + inv_root * (
        scaled - unit_rows * jnp.mean(scaled * unit_rows, axis=1, keepdims=True)
    )
    layer_grad = layer_grad.astype(jnp.bfloat16)
    passed = shifted(layer_grad, "section", -1)
    return passed[None]


tile = 256
in_vmem = pl.BlockSpec(memory_space=pltpu.VMEM)
anywhere = pl.BlockSpec(memory_space=pl.ANY)


def tile_cut(step):
    return pl.ds(pl.multiple_of(step * tile, tile), tile)


def shared_kernel(experts, upstream_ref, ids_ref, share_ref, out_ref):
    size, width = upstream_ref.shape
    lanes = out_ref.shape[1] - width
    top = ids_ref.shape[0]
    out_ref[:, :width] = upstream_ref[...]
    both = jnp.concatenate([ids_ref[...].astype(jnp.float32), share_ref[...]], axis=0).T
    lane = lax.broadcasted_iota(jnp.int32, (size, lanes), 1)
    expert = lax.rem(lane, experts).astype(jnp.float32)
    dense = jnp.zeros((size, lanes), jnp.float32)
    for k in range(top):
        hit = expert == both[:, k : k + 1]
        dense = dense + jnp.where(hit, both[:, top + k : top + k + 1], 0.0)
    high = dense.astype(jnp.bfloat16).astype(jnp.float32)
    middle = (dense - high).astype(jnp.bfloat16).astype(jnp.float32)
    low = dense - high - middle
    parts = jnp.where(lane < experts, high, jnp.where(lane < 2 * experts, middle, low))
    out_ref[:, width:] = jnp.where(lane < 3 * experts, parts, 0.0).astype(jnp.bfloat16)


def shared_rows(upstream_rows, routed, shares, experts):
    count, width = upstream_rows.shape
    return pl.pallas_call(
        functools.partial(shared_kernel, experts),
        in_specs=[in_vmem] * 3,
        out_specs=in_vmem,
        out_shape=jax.ShapeDtypeStruct((count, width + 128), jnp.bfloat16),
        compiler_params=pltpu.CompilerParams(vmem_limit_bytes=8 << 20),
    )(upstream_rows, routed, shares)


def factors_kernel(pairs, saved_ref, gain_ref, *refs):
    weight_refs = refs[: 2 * pairs]
    gate_ref, up_ref, rows_ref = refs[-3:]
    value = saved_ref[...].astype(jnp.float32)
    inv_root = lax.rsqrt(jnp.mean(value * value, axis=1, keepdims=True) + epsilon)
    rows_ref[...] = (value * inv_root * gain_ref[...]).astype(jnp.bfloat16)

    def body(step, carry):
        cut = tile_cut(step)
        for w in range(pairs):
            inputs = rows_ref[...]
            pre_gate = jnp.dot(
                inputs, weight_refs[2 * w][:, cut], preferred_element_type=jnp.float32
            )
            pre_up = jnp.dot(
                inputs, weight_refs[2 * w + 1][:, cut], preferred_element_type=jnp.float32
            )
            sigmoid_gate = jax.nn.sigmoid(pre_gate)
            gate_ref[w, :, cut] = pre_up * sigmoid_gate * (1.0 + pre_gate * (1.0 - sigmoid_gate))
            up_ref[w, :, cut] = pre_gate * sigmoid_gate
        return carry

    lax.fori_loop(0, gate_ref.shape[2] // tile, body, 0)


def slot_factors(rows, gain_row, weights, after):
    pairs = len(weights)
    count, width = rows.shape
    hidden = weights[0][0].shape[1]
    flat = [w for gate_w, up_w, _ in weights for w in (gate_w, up_w)]
    shape = jax.ShapeDtypeStruct((pairs, count, hidden), jnp.float32)
    return pl.pallas_call(
        functools.partial(factors_kernel, pairs),
        in_specs=[in_vmem] * (2 + len(flat)) + [anywhere] * len(after),
        out_specs=[in_vmem] * 2,
        out_shape=[shape] * 2,
        scratch_shapes=[pltpu.VMEM((count, width), jnp.bfloat16)],
        cost_estimate=pl.CostEstimate(
            flops=8 * pairs * count * width * hidden,
            bytes_accessed=4 * pairs * width * hidden,
            transcendentals=pairs * count * hidden,
        ),
        compiler_params=pltpu.CompilerParams(vmem_limit_bytes=8 << 20),
    )(rows, gain_row, *flat, *after)


def share_of(rows_ref, width, experts, flip):
    named = lax.axis_index("expert") ^ flip
    parts = rows_ref[:, width:].astype(jnp.float32)
    lane = lax.broadcasted_iota(jnp.int32, parts.shape, 1)
    wanted = (lax.rem(lane, experts) == named) & (lane < 3 * experts)
    return jnp.sum(jnp.where(wanted, parts, 0.0), axis=1, keepdims=True)


def turning_kernel(experts, start, flip, rows_ref, gain_ref, gate_ref, up_ref, *refs):
    weight_refs, refs = refs[:3], refs[3:]
    base_ref = refs[0] if start else None
    out_ref, gate_turned, up_turned, down_turned, gate_grads, up_grads = refs[-6:]
    width = out_ref.shape[1]
    hidden = gate_ref.shape[2]
    share = share_of(rows_ref, width, experts, flip)

    def grads_of(step, carry):
        cut = tile_cut(step)
        turned = weight_refs[2][cut, :].T
        down_turned[:, cut] = turned
        grad = jnp.dot(rows_ref[:, :width], turned, preferred_element_type=jnp.float32)
        grad = grad * share
        gate_grads[:, cut] = (grad * gate_ref[0, :, cut]).astype(jnp.bfloat16)
        up_grads[:, cut] = (grad * up_ref[0, :, cut]).astype(jnp.bfloat16)
        return carry

    lax.fori_loop(0, hidden // tile, grads_of, 0)

    def pieces_of(step, carry):
        cut = tile_cut(step)
        gate_tile = weight_refs[0][cut, :].T
        up_tile = weight_refs[1][cut, :].T
        gate_turned[:, cut] = gate_tile
        up_turned[:, cut] = up_tile
        total = jnp.dot(gate_grads[...], gate_tile, preferred_element_type=jnp.float32)
        total = total + jnp.dot(up_grads[...], up_tile, preferred_element_type=jnp.float32)
        total = total * gain_ref[:, cut]
        if start:
            total = total + base_ref[:, cut]
        out_ref[:, cut] = total.astype(out_ref.dtype)
        return carry

    lax.fori_loop(0, width // tile, pieces_of, 0)


def turning_pieces(flip, rows, gain_row, factors, weights, experts, kind, base):
    _, count, hidden = factors[0].shape
    width = weights[0].shape[0]
    start = [] if base is None else [base]
    turned = jax.ShapeDtypeStruct((hidden, width), jnp.bfloat16)
    down_turned = jax.ShapeDtypeStruct((width, hidden), jnp.bfloat16)
    return pl.pallas_call(
        functools.partial(turning_kernel, experts, len(start), flip),
        in_specs=[in_vmem] * (7 + len(start)),
        out_specs=[in_vmem] * 4,
        out_shape=[jax.ShapeDtypeStruct((count, width), kind), turned, turned, down_turned],
        scratch_shapes=[pltpu.VMEM((count, hidden), jnp.bfloat16)] * 2,
        cost_estimate=pl.CostEstimate(
            flops=12 * count * width * hidden,
            bytes_accessed=6 * width * hidden,
            transcendentals=0,
        ),
        compiler_params=pltpu.CompilerParams(vmem_limit_bytes=12 << 20),
    )(rows, gain_row, *factors, *weights, *start)


def pieces_kernel(experts, pairs, rows_ref, gain_ref, gate_ref, up_ref, *refs):
    weight_refs = refs[: 3 * pairs]
    out_ref, gate_grads, up_grads = refs[-3:]
    width = out_ref.shape[1]
    hidden = gate_ref.shape[2]
    shares = [share_of(rows_ref, width, experts, w) for w in range(pairs)]

    def grads_of(step, carry):
        cut = tile_cut(step)
        for w in range(pairs):
            grad = jnp.dot(
                rows_ref[:, :width],
                weight_refs[3 * w + 2][:, cut],
                preferred_element_type=jnp.float32,
            )
            grad = grad * shares[w]
            gate_grads[w, :, cut] = (grad * gate_ref[w, :, cut]).astype(jnp.bfloat16)
            up_grads[w, :, cut] = (grad * up_ref[w, :, cut]).astype(jnp.bfloat16)
        return carry

    lax.fori_loop(0, hidden // tile, grads_of, 0)

    def pieces_of(step, carry):
        cut = tile_cut(step)
        total = None
        for w in range(pairs):
            for held, weight_ref in ((gate_grads, weight_refs[3 * w]), (up_grads, weight_refs[3 * w + 1])):
                part = jnp.dot(held[w], weight_ref[:, cut], preferred_element_type=jnp.float32)
                total = part if total is None else total + part
        out_ref[:, cut] = (total * gain_ref[:, cut]).astype(out_ref.dtype)
        return carry

    lax.fori_loop(0, width // tile, pieces_of, 0)


def slot_pieces(rows, gain_row, factors, weights, experts, after):
    pairs, count, hidden = factors[0].shape
    width = weights[0][0].shape[1]
    flat = [w for group in weights for w in group]
    return pl.pallas_call(
        functools.partial(pieces_kernel, experts, pairs),
        in_specs=[in_vmem] * (4 + len(flat)) + [anywhere] * len(after),
        out_specs=in_vmem,
        out_shape=jax.ShapeDtypeStruct((count, width), jnp.bfloat16),
        scratch_shapes=[pltpu.VMEM((pairs, count, hidden), jnp.bfloat16)] * 2,
        cost_estimate=pl.CostEstimate(
            flops=12 * pairs * count * width * hidden,
            bytes_accessed=6 * pairs * width * hidden,
            transcendentals=0,
        ),
        compiler_params=pltpu.CompilerParams(vmem_limit_bytes=8 << 20),
    )(rows, gain_row, *factors, *flat, *after)


def final_kernel(saved_ref, upstream_ref, *refs):
    out_ref = refs[-1]
    value = saved_ref[...].astype(jnp.float32)
    inv_root = lax.rsqrt(jnp.mean(value * value, axis=1, keepdims=True) + epsilon)
    scaled = refs[0][...].astype(jnp.float32)
    for ref in refs[1:-1]:
        scaled = scaled + ref[...].astype(jnp.float32)
    unit = value * inv_root
    mean = jnp.mean(scaled * unit, axis=1, keepdims=True)
    layer_grad = upstream_ref[...].astype(jnp.float32) + inv_root * (scaled - unit * mean)
    out_ref[...] = layer_grad.astype(jnp.bfloat16)


def finish(saved_rows, upstream_rows, pieces):
    return pl.pallas_call(
        final_kernel,
        in_specs=[in_vmem] * (2 + len(pieces)),
        out_specs=in_vmem,
        out_shape=jax.ShapeDtypeStruct(saved_rows.shape, jnp.bfloat16),
        compiler_params=pltpu.CompilerParams(vmem_limit_bytes=8 << 20),
    )(saved_rows, upstream_rows, *pieces)


def joined_kernel(experts, at_ends, some_ref, *refs):
    out_ref = refs[-1]
    me = lax.axis_index("expert")
    is_end = ((me < 2) | (me >= experts - 2)).astype(jnp.int32)
    total = jnp.where(is_end == at_ends, some_ref[...].astype(jnp.float32), 0.0)
    for ref in refs[:-1]:
        total = total + ref[...].astype(jnp.float32)
    out_ref[...] = total.astype(out_ref.dtype)


def joined(experts, at_ends, some, pieces, kind):
    return pl.pallas_call(
        functools.partial(joined_kernel, experts, at_ends),
        in_specs=[in_vmem] * (1 + len(pieces)),
        out_specs=in_vmem,
        out_shape=jax.ShapeDtypeStruct(some.shape, kind),
        compiler_params=pltpu.CompilerParams(vmem_limit_bytes=8 << 20),
    )(some, *pieces)


def line_device(
    saved_input, upstream, norm_gain, gate_weight, up_weight, down_weight, expert_ids, gate_share
):
    own = (gate_weight[0, 0], up_weight[0, 0], down_weight[0, 0])
    saved_rows, upstream_rows = saved_input[0], upstream[0]
    experts = lax.axis_size("expert")
    sections = lax.axis_size("section")

    def hop(by):
        return lambda value: lax.ppermute(value, "expert", [(i, i ^ by) for i in range(experts)])

    def handed(by):
        pairs = [
            (s * experts + i, (s - 1) % sections * experts + (i ^ by))
            for s in range(sections)
            for i in range(experts)
        ]
        return lambda value: lax.ppermute(value, ("section", "expert"), pairs)

    shared = shared_rows(upstream_rows, expert_ids[0].T, gate_share[0].T, experts)
    x_two, x_one = hop(4)(saved_rows), hop(2)(saved_rows)
    gate_other, up_other = hop(1)(own[0]), hop(1)(own[1])
    u_two = hop(4)(shared)
    gain = norm_gain
    ends = (0, 1, experts - 2, experts - 1)

    def second_hop(value):
        pairs = []
        for s in range(sections):
            for i in range(experts):
                target = (s, i ^ 2) if i in ends else ((s - 1) % sections, i ^ 4)
                pairs.append((s * experts + i, target[0] * experts + target[1]))
        return lax.ppermute(value, ("section", "expert"), pairs)

    own_factors = slot_factors(saved_rows, gain, (own,), [])
    later, gate = lax.optimization_barrier((shared, own_factors[0]))
    own_factors = (gate, own_factors[1])
    other = (gate_other, up_other, hop(1)(own[2]))
    u_one = hop(2)(later)
    other_factors = slot_factors(saved_rows, gain, (other,), [gate])
    saved_later, upstream_later, gate = lax.optimization_barrier(
        (saved_rows, upstream_rows, other_factors[0])
    )
    other_factors = (gate, other_factors[1])
    next_saved, next_upstream = handed(0)(saved_later), handed(0)(upstream_later)
    both = (own, other)
    here, *own_turned = turning_pieces(
        0, shared, gain, own_factors, own, experts, jnp.float32, None
    )
    here, *other_turned = turning_pieces(
        1, shared, gain, other_factors, other, experts, jnp.bfloat16, here
    )
    turned = (own_turned, other_turned)
    x_three = hop(2)(x_two)
    two_factors = slot_factors(x_two, gain, both, [here])
    one_factors = slot_factors(x_one, gain, both, [two_factors[0]])
    u_two, one_gate = lax.optimization_barrier((u_two, one_factors[0]))
    one_factors = (one_gate, one_factors[1])
    here_next = handed(0)(here)
    u_three = hop(2)(u_two)
    two = slot_pieces(u_two, gain, two_factors, turned, experts, [next_saved, next_upstream])
    two_next = second_hop(two)
    three_factors = slot_factors(x_three, gain, both, [two])
    one = slot_pieces(u_one, gain, one_factors, turned, experts, [three_factors[0]])
    one_next = handed(2)(one)
    three = slot_pieces(u_three, gain, three_factors, turned, experts, [one])
    three = joined(experts, 0, two_next, [three], jnp.bfloat16)
    summed = joined(experts, 1, two_next, [here_next, one_next], jnp.float32)
    three_next = handed(6)(three)
    return finish(next_saved, next_upstream, [summed, three_next])[None]


def solution(mesh):
    placed = (
        P("section", "expert", None),
        P("section", "expert", None),
        P("section", None),
        P("section", "expert", None, None),
        P("section", "expert", None, None),
        P("section", "expert", None, None),
        P("section", "expert", None),
        P("section", "expert", None),
    )
    plan = line_device if mesh.shape["expert"] == 8 else routed_device
    return jax.shard_map(
        plan,
        mesh=mesh,
        in_specs=placed,
        out_specs=P("section", "expert", None),
        check_vma=False,
    )
```

```python
import functools
import jax
import jax.numpy as jnp
from jax import lax
from jax.experimental import pallas as pl
from jax.experimental.pallas import tpu as pltpu
from jax.sharding import PartitionSpec as P

epsilon = 1e-06


def shifted(value, axis, by):
    length = lax.axis_size(axis)
    return lax.ppermute(value, axis, [(i, (i + by) % length) for i in range(length)])


def slot_ranks(flat_ids, experts):
    pairs = flat_ids.shape[0]
    onehot = (flat_ids[:, None] == jnp.arange(experts, dtype=jnp.int32)[None, :]).astype(
        jnp.bfloat16
    )
    row_index = jnp.arange(pairs, dtype=jnp.int32)
    lower = (row_index[None, :] < row_index[:, None]).astype(jnp.bfloat16)
    before = jnp.dot(lower, onehot, preferred_element_type=jnp.float32)
    ranks = jnp.sum(before * onehot.astype(jnp.float32), axis=1)
    return ranks.astype(jnp.int32)


def expert_backward(inputs, grads, gate_w, up_w, down_w):
    pre_gate = jnp.dot(inputs, gate_w, preferred_element_type=jnp.float32)
    pre_up = jnp.dot(inputs, up_w, preferred_element_type=jnp.float32)
    sigmoid_gate = jax.nn.sigmoid(pre_gate)
    hidden_grad = lax.dot_general(
        grads, down_w, (((1,), (1,)), ((), ())), preferred_element_type=jnp.float32
    )
    d_gate = (hidden_grad * pre_up * sigmoid_gate * (1.0 + pre_gate * (1.0 - sigmoid_gate))).astype(
        jnp.bfloat16
    )
    d_up = (hidden_grad * pre_gate * sigmoid_gate).astype(jnp.bfloat16)
    summed = lax.dot_general(
        d_gate, gate_w, (((1,), (1,)), ((), ())), preferred_element_type=jnp.float32
    )
    summed = summed + lax.dot_general(
        d_up, up_w, (((1,), (1,)), ((), ())), preferred_element_type=jnp.float32
    )
    return summed.astype(jnp.bfloat16)


def routed_device(
    saved_input, upstream, norm_gain, gate_weight, up_weight, down_weight, expert_ids, gate_share
):
    saved_rows = saved_input[0]
    upstream_rows = upstream[0]
    gain_row = norm_gain[0]
    gate_w = gate_weight[0, 0]
    up_w = up_weight[0, 0]
    down_w = down_weight[0, 0]
    routed = expert_ids[0]
    shares = gate_share[0]
    tok_rows, top_count = routed.shape
    model_width = saved_rows.shape[1]
    experts = lax.axis_size("expert")
    capacity = max(2, 3 * tok_rows * top_count // (2 * experts))
    inputs_f = saved_rows.astype(jnp.float32)
    inv_root = lax.rsqrt(jnp.mean(inputs_f * inputs_f, axis=1, keepdims=True) + epsilon)
    unit_rows = inputs_f * inv_root
    normed = (unit_rows * gain_row[None, :]).astype(jnp.bfloat16)
    flat_ids = routed.reshape(-1)
    slot_rank = slot_ranks(flat_ids, experts)
    slot_number = (flat_ids * capacity + slot_rank).reshape(tok_rows, top_count)
    slot_index = jnp.arange(experts * capacity, dtype=jnp.int32)
    matches = slot_number[None, :, :] == slot_index[:, None, None]
    select = jnp.any(matches, axis=2).astype(jnp.bfloat16)
    slot_share = jnp.sum(jnp.where(matches, shares[None, :, :], 0.0), axis=(1, 2))
    send_inputs = jnp.dot(select, normed, preferred_element_type=jnp.float32).astype(jnp.bfloat16)
    send_inputs = send_inputs.reshape(experts, capacity, model_width)
    copied_grads = jnp.dot(select, upstream_rows, preferred_element_type=jnp.float32)
    send_grads = (
        (copied_grads * slot_share[:, None])
        .astype(jnp.bfloat16)
        .reshape(experts, capacity, model_width)
    )
    got_inputs, got_grads = (
        lax.all_to_all(send_inputs, "expert", split_axis=0, concat_axis=0, tiled=True),
        lax.all_to_all(send_grads, "expert", split_axis=0, concat_axis=0, tiled=True),
    )
    slot_count = got_inputs.shape[1]
    result_rows = expert_backward(
        got_inputs.reshape(-1, model_width),
        got_grads.reshape(-1, model_width),
        gate_w,
        up_w,
        down_w,
    )
    returned = lax.all_to_all(
        result_rows.reshape(experts, slot_count, model_width),
        "expert",
        split_axis=0,
        concat_axis=0,
        tiled=True,
    )
    normed_grad = lax.dot_general(
        select,
        returned.reshape(experts * capacity, model_width),
        (((0,), (0,)), ((), ())),
        preferred_element_type=jnp.float32,
    )
    scaled = normed_grad * gain_row[None, :]
    layer_grad = upstream_rows.astype(jnp.float32) + inv_root * (
        scaled - unit_rows * jnp.mean(scaled * unit_rows, axis=1, keepdims=True)
    )
    layer_grad = layer_grad.astype(jnp.bfloat16)
    passed = shifted(layer_grad, "section", -1)
    return passed[None]


tile = 256
in_vmem = pl.BlockSpec(memory_space=pltpu.VMEM)
anywhere = pl.BlockSpec(memory_space=pl.ANY)


def tile_cut(step):
    return pl.ds(pl.multiple_of(step * tile, tile), tile)


def shared_kernel(experts, upstream_ref, ids_ref, share_ref, out_ref):
    size, width = upstream_ref.shape
    lanes = out_ref.shape[1] - width
    top = ids_ref.shape[0]
    out_ref[:, :width] = upstream_ref[...]
    both = jnp.concatenate([ids_ref[...].astype(jnp.float32), share_ref[...]], axis=0).T
    lane = lax.broadcasted_iota(jnp.int32, (size, lanes), 1)
    expert = lax.rem(lane, experts).astype(jnp.float32)
    dense = jnp.zeros((size, lanes), jnp.float32)
    for k in range(top):
        hit = expert == both[:, k : k + 1]
        dense = dense + jnp.where(hit, both[:, top + k : top + k + 1], 0.0)
    high = dense.astype(jnp.bfloat16).astype(jnp.float32)
    middle = (dense - high).astype(jnp.bfloat16).astype(jnp.float32)
    low = dense - high - middle
    parts = jnp.where(lane < experts, high, jnp.where(lane < 2 * experts, middle, low))
    out_ref[:, width:] = jnp.where(lane < 3 * experts, parts, 0.0).astype(jnp.bfloat16)


def shared_rows(upstream_rows, routed, shares, experts):
    count, width = upstream_rows.shape
    return pl.pallas_call(
        functools.partial(shared_kernel, experts),
        in_specs=[in_vmem] * 3,
        out_specs=in_vmem,
        out_shape=jax.ShapeDtypeStruct((count, width + 128), jnp.bfloat16),
        compiler_params=pltpu.CompilerParams(vmem_limit_bytes=8 << 20),
    )(upstream_rows, routed, shares)


def factors_kernel(pairs, saved_ref, gain_ref, *refs):
    weight_refs = refs[: 2 * pairs]
    gate_ref, up_ref, rows_ref = refs[-3:]
    value = saved_ref[...].astype(jnp.float32)
    inv_root = lax.rsqrt(jnp.mean(value * value, axis=1, keepdims=True) + epsilon)
    rows_ref[...] = (value * inv_root * gain_ref[...]).astype(jnp.bfloat16)

    def body(step, carry):
        cut = tile_cut(step)
        for w in range(pairs):
            inputs = rows_ref[...]
            pre_gate = jnp.dot(
                inputs, weight_refs[2 * w][:, cut], preferred_element_type=jnp.float32
            )
            pre_up = jnp.dot(
                inputs, weight_refs[2 * w + 1][:, cut], preferred_element_type=jnp.float32
            )
            sigmoid_gate = jax.nn.sigmoid(pre_gate)
            gate_ref[w, :, cut] = pre_up * sigmoid_gate * (1.0 + pre_gate * (1.0 - sigmoid_gate))
            up_ref[w, :, cut] = pre_gate * sigmoid_gate
        return carry

    lax.fori_loop(0, gate_ref.shape[2] // tile, body, 0)


def slot_factors(rows, gain_row, weights, after):
    pairs = len(weights)
    count, width = rows.shape
    hidden = weights[0][0].shape[1]
    flat = [w for gate_w, up_w, _ in weights for w in (gate_w, up_w)]
    shape = jax.ShapeDtypeStruct((pairs, count, hidden), jnp.float32)
    return pl.pallas_call(
        functools.partial(factors_kernel, pairs),
        in_specs=[in_vmem] * (2 + len(flat)) + [anywhere] * len(after),
        out_specs=[in_vmem] * 2,
        out_shape=[shape] * 2,
        scratch_shapes=[pltpu.VMEM((count, width), jnp.bfloat16)],
        cost_estimate=pl.CostEstimate(
            flops=8 * pairs * count * width * hidden,
            bytes_accessed=4 * pairs * width * hidden,
            transcendentals=pairs * count * hidden,
        ),
        compiler_params=pltpu.CompilerParams(vmem_limit_bytes=8 << 20),
    )(rows, gain_row, *flat, *after)


def share_of(rows_ref, width, experts, flip):
    named = lax.axis_index("expert") ^ flip
    parts = rows_ref[:, width:].astype(jnp.float32)
    lane = lax.broadcasted_iota(jnp.int32, parts.shape, 1)
    wanted = (lax.rem(lane, experts) == named) & (lane < 3 * experts)
    return jnp.sum(jnp.where(wanted, parts, 0.0), axis=1, keepdims=True)


def turning_kernel(experts, start, flip, rows_ref, gain_ref, gate_ref, up_ref, *refs):
    weight_refs, refs = refs[:3], refs[3:]
    base_ref = refs[0] if start else None
    out_ref, gate_turned, up_turned, down_turned, gate_grads, up_grads = refs[-6:]
    width = out_ref.shape[1]
    hidden = gate_ref.shape[2]
    share = share_of(rows_ref, width, experts, flip)

    def grads_of(step, carry):
        cut = tile_cut(step)
        turned = weight_refs[2][cut, :].T
        down_turned[:, cut] = turned
        grad = jnp.dot(rows_ref[:, :width], turned, preferred_element_type=jnp.float32)
        grad = grad * share
        gate_grads[:, cut] = (grad * gate_ref[0, :, cut]).astype(jnp.bfloat16)
        up_grads[:, cut] = (grad * up_ref[0, :, cut]).astype(jnp.bfloat16)
        return carry

    lax.fori_loop(0, hidden // tile, grads_of, 0)

    def pieces_of(step, carry):
        cut = tile_cut(step)
        gate_tile = weight_refs[0][cut, :].T
        up_tile = weight_refs[1][cut, :].T
        gate_turned[:, cut] = gate_tile
        up_turned[:, cut] = up_tile
        total = jnp.dot(gate_grads[...], gate_tile, preferred_element_type=jnp.float32)
        total = total + jnp.dot(up_grads[...], up_tile, preferred_element_type=jnp.float32)
        total = total * gain_ref[:, cut]
        if start:
            total = total + base_ref[:, cut]
        out_ref[:, cut] = total.astype(out_ref.dtype)
        return carry

    lax.fori_loop(0, width // tile, pieces_of, 0)


def turning_pieces(flip, rows, gain_row, factors, weights, experts, kind, base):
    _, count, hidden = factors[0].shape
    width = weights[0].shape[0]
    start = [] if base is None else [base]
    turned = jax.ShapeDtypeStruct((hidden, width), jnp.bfloat16)
    down_turned = jax.ShapeDtypeStruct((width, hidden), jnp.bfloat16)
    return pl.pallas_call(
        functools.partial(turning_kernel, experts, len(start), flip),
        in_specs=[in_vmem] * (7 + len(start)),
        out_specs=[in_vmem] * 4,
        out_shape=[jax.ShapeDtypeStruct((count, width), kind), turned, turned, down_turned],
        scratch_shapes=[pltpu.VMEM((count, hidden), jnp.bfloat16)] * 2,
        cost_estimate=pl.CostEstimate(
            flops=12 * count * width * hidden,
            bytes_accessed=6 * width * hidden,
            transcendentals=0,
        ),
        compiler_params=pltpu.CompilerParams(vmem_limit_bytes=12 << 20),
    )(rows, gain_row, *factors, *weights, *start)


def pieces_kernel(experts, pairs, rows_ref, gain_ref, gate_ref, up_ref, *refs):
    weight_refs = refs[: 3 * pairs]
    out_ref, gate_grads, up_grads = refs[-3:]
    width = out_ref.shape[1]
    hidden = gate_ref.shape[2]
    shares = [share_of(rows_ref, width, experts, w) for w in range(pairs)]

    def grads_of(step, carry):
        cut = tile_cut(step)
        for w in range(pairs):
            grad = jnp.dot(
                rows_ref[:, :width],
                weight_refs[3 * w + 2][:, cut],
                preferred_element_type=jnp.float32,
            )
            grad = grad * shares[w]
            gate_grads[w, :, cut] = (grad * gate_ref[w, :, cut]).astype(jnp.bfloat16)
            up_grads[w, :, cut] = (grad * up_ref[w, :, cut]).astype(jnp.bfloat16)
        return carry

    lax.fori_loop(0, hidden // tile, grads_of, 0)

    def pieces_of(step, carry):
        cut = tile_cut(step)
        total = None
        for w in range(pairs):
            for held, weight_ref in ((gate_grads, weight_refs[3 * w]), (up_grads, weight_refs[3 * w + 1])):
                part = jnp.dot(held[w], weight_ref[:, cut], preferred_element_type=jnp.float32)
                total = part if total is None else total + part
        out_ref[:, cut] = (total * gain_ref[:, cut]).astype(out_ref.dtype)
        return carry

    lax.fori_loop(0, width // tile, pieces_of, 0)


def slot_pieces(rows, gain_row, factors, weights, experts, after):
    pairs, count, hidden = factors[0].shape
    width = weights[0][0].shape[1]
    flat = [w for group in weights for w in group]
    return pl.pallas_call(
        functools.partial(pieces_kernel, experts, pairs),
        in_specs=[in_vmem] * (4 + len(flat)) + [anywhere] * len(after),
        out_specs=in_vmem,
        out_shape=jax.ShapeDtypeStruct((count, width), jnp.bfloat16),
        scratch_shapes=[pltpu.VMEM((pairs, count, hidden), jnp.bfloat16)] * 2,
        cost_estimate=pl.CostEstimate(
            flops=12 * pairs * count * width * hidden,
            bytes_accessed=6 * pairs * width * hidden,
            transcendentals=0,
        ),
        compiler_params=pltpu.CompilerParams(vmem_limit_bytes=8 << 20),
    )(rows, gain_row, *factors, *flat, *after)


def final_kernel(saved_ref, upstream_ref, *refs):
    out_ref = refs[-1]
    value = saved_ref[...].astype(jnp.float32)
    inv_root = lax.rsqrt(jnp.mean(value * value, axis=1, keepdims=True) + epsilon)
    scaled = refs[0][...].astype(jnp.float32)
    for ref in refs[1:-1]:
        scaled = scaled + ref[...].astype(jnp.float32)
    unit = value * inv_root
    mean = jnp.mean(scaled * unit, axis=1, keepdims=True)
    layer_grad = upstream_ref[...].astype(jnp.float32) + inv_root * (scaled - unit * mean)
    out_ref[...] = layer_grad.astype(jnp.bfloat16)


def finish(saved_rows, upstream_rows, pieces):
    return pl.pallas_call(
        final_kernel,
        in_specs=[in_vmem] * (2 + len(pieces)),
        out_specs=in_vmem,
        out_shape=jax.ShapeDtypeStruct(saved_rows.shape, jnp.bfloat16),
        compiler_params=pltpu.CompilerParams(vmem_limit_bytes=8 << 20),
    )(saved_rows, upstream_rows, *pieces)


def joined_kernel(experts, at_ends, some_ref, *refs):
    out_ref = refs[-1]
    me = lax.axis_index("expert")
    is_end = ((me < 2) | (me >= experts - 2)).astype(jnp.int32)
    total = jnp.where(is_end == at_ends, some_ref[...].astype(jnp.float32), 0.0)
    for ref in refs[:-1]:
        total = total + ref[...].astype(jnp.float32)
    out_ref[...] = total.astype(out_ref.dtype)


def joined(experts, at_ends, some, pieces, kind):
    return pl.pallas_call(
        functools.partial(joined_kernel, experts, at_ends),
        in_specs=[in_vmem] * (1 + len(pieces)),
        out_specs=in_vmem,
        out_shape=jax.ShapeDtypeStruct(some.shape, kind),
        compiler_params=pltpu.CompilerParams(vmem_limit_bytes=8 << 20),
    )(some, *pieces)


def line_device(
    saved_input, upstream, norm_gain, gate_weight, up_weight, down_weight, expert_ids, gate_share
):
    own = (gate_weight[0, 0], up_weight[0, 0], down_weight[0, 0])
    saved_rows, upstream_rows = saved_input[0], upstream[0]
    experts = lax.axis_size("expert")
    sections = lax.axis_size("section")

    def hop(by):
        return lambda value: lax.ppermute(value, "expert", [(i, i ^ by) for i in range(experts)])

    def handed(by):
        pairs = [
            (s * experts + i, (s - 1) % sections * experts + (i ^ by))
            for s in range(sections)
            for i in range(experts)
        ]
        return lambda value: lax.ppermute(value, ("section", "expert"), pairs)

    shared = shared_rows(upstream_rows, expert_ids[0].T, gate_share[0].T, experts)
    x_two, x_one = hop(4)(saved_rows), hop(2)(saved_rows)
    gate_other, up_other = hop(1)(own[0]), hop(1)(own[1])
    u_two = hop(4)(shared)
    gain = norm_gain
    ends = (0, 1, experts - 2, experts - 1)

    def second_hop(value):
        pairs = []
        for s in range(sections):
            for i in range(experts):
                target = (s, i ^ 2) if i in ends else ((s - 1) % sections, i ^ 4)
                pairs.append((s * experts + i, target[0] * experts + target[1]))
        return lax.ppermute(value, ("section", "expert"), pairs)

    own_factors = slot_factors(saved_rows, gain, (own,), [])
    later, gate = lax.optimization_barrier((shared, own_factors[0]))
    own_factors = (gate, own_factors[1])
    other = (gate_other, up_other, hop(1)(own[2]))
    u_one = hop(2)(later)
    other_factors = slot_factors(saved_rows, gain, (other,), [gate])
    saved_later, upstream_later, gate = lax.optimization_barrier(
        (saved_rows, upstream_rows, other_factors[0])
    )
    other_factors = (gate, other_factors[1])
    next_saved, next_upstream = handed(0)(saved_later), handed(0)(upstream_later)
    both = (own, other)
    here, *own_turned = turning_pieces(
        0, shared, gain, own_factors, own, experts, jnp.float32, None
    )
    here, *other_turned = turning_pieces(
        1, shared, gain, other_factors, other, experts, jnp.bfloat16, here
    )
    turned = (own_turned, other_turned)
    x_three = hop(2)(x_two)
    two_factors = slot_factors(x_two, gain, both, [here])
    one_factors = slot_factors(x_one, gain, both, [two_factors[0]])
    u_two, one_gate = lax.optimization_barrier((u_two, one_factors[0]))
    one_factors = (one_gate, one_factors[1])
    here_next = handed(0)(here)
    u_three = hop(2)(u_two)
    two = slot_pieces(u_two, gain, two_factors, turned, experts, [next_saved, next_upstream])
    two_next = second_hop(two)
    three_factors = slot_factors(x_three, gain, both, [two])
    one = slot_pieces(u_one, gain, one_factors, turned, experts, [three_factors[0]])
    three = slot_pieces(u_three, gain, three_factors, turned, experts, [one])
    three = joined(experts, 0, two_next, [three], jnp.bfloat16)
    three, one = lax.optimization_barrier((three, one))
    three_next = handed(6)(three)
    one_next = handed(2)(one)
    summed = joined(experts, 1, two_next, [here_next, three_next], jnp.float32)
    return finish(next_saved, next_upstream, [summed, one_next])[None]


def solution(mesh):
    placed = (
        P("section", "expert", None),
        P("section", "expert", None),
        P("section", None),
        P("section", "expert", None, None),
        P("section", "expert", None, None),
        P("section", "expert", None, None),
        P("section", "expert", None),
        P("section", "expert", None),
    )
    plan = line_device if mesh.shape["expert"] == 8 else routed_device
    return jax.shard_map(
        plan,
        mesh=mesh,
        in_specs=placed,
        out_specs=P("section", "expert", None),
        check_vma=False,
    )
```

```python
import functools
import jax
import jax.numpy as jnp
from jax import lax
from jax.experimental import pallas as pl
from jax.experimental.pallas import tpu as pltpu
from jax.sharding import PartitionSpec as P

epsilon = 1e-06


def shifted(value, axis, by):
    length = lax.axis_size(axis)
    return lax.ppermute(value, axis, [(i, (i + by) % length) for i in range(length)])


def slot_ranks(flat_ids, experts):
    pairs = flat_ids.shape[0]
    onehot = (flat_ids[:, None] == jnp.arange(experts, dtype=jnp.int32)[None, :]).astype(
        jnp.bfloat16
    )
    row_index = jnp.arange(pairs, dtype=jnp.int32)
    lower = (row_index[None, :] < row_index[:, None]).astype(jnp.bfloat16)
    before = jnp.dot(lower, onehot, preferred_element_type=jnp.float32)
    ranks = jnp.sum(before * onehot.astype(jnp.float32), axis=1)
    return ranks.astype(jnp.int32)


def expert_backward(inputs, grads, gate_w, up_w, down_w):
    pre_gate = jnp.dot(inputs, gate_w, preferred_element_type=jnp.float32)
    pre_up = jnp.dot(inputs, up_w, preferred_element_type=jnp.float32)
    sigmoid_gate = jax.nn.sigmoid(pre_gate)
    hidden_grad = lax.dot_general(
        grads, down_w, (((1,), (1,)), ((), ())), preferred_element_type=jnp.float32
    )
    d_gate = (hidden_grad * pre_up * sigmoid_gate * (1.0 + pre_gate * (1.0 - sigmoid_gate))).astype(
        jnp.bfloat16
    )
    d_up = (hidden_grad * pre_gate * sigmoid_gate).astype(jnp.bfloat16)
    summed = lax.dot_general(
        d_gate, gate_w, (((1,), (1,)), ((), ())), preferred_element_type=jnp.float32
    )
    summed = summed + lax.dot_general(
        d_up, up_w, (((1,), (1,)), ((), ())), preferred_element_type=jnp.float32
    )
    return summed.astype(jnp.bfloat16)


def routed_device(
    saved_input, upstream, norm_gain, gate_weight, up_weight, down_weight, expert_ids, gate_share
):
    saved_rows = saved_input[0]
    upstream_rows = upstream[0]
    gain_row = norm_gain[0]
    gate_w = gate_weight[0, 0]
    up_w = up_weight[0, 0]
    down_w = down_weight[0, 0]
    routed = expert_ids[0]
    shares = gate_share[0]
    tok_rows, top_count = routed.shape
    model_width = saved_rows.shape[1]
    experts = lax.axis_size("expert")
    capacity = max(2, 3 * tok_rows * top_count // (2 * experts))
    inputs_f = saved_rows.astype(jnp.float32)
    inv_root = lax.rsqrt(jnp.mean(inputs_f * inputs_f, axis=1, keepdims=True) + epsilon)
    unit_rows = inputs_f * inv_root
    normed = (unit_rows * gain_row[None, :]).astype(jnp.bfloat16)
    flat_ids = routed.reshape(-1)
    slot_rank = slot_ranks(flat_ids, experts)
    slot_number = (flat_ids * capacity + slot_rank).reshape(tok_rows, top_count)
    slot_index = jnp.arange(experts * capacity, dtype=jnp.int32)
    matches = slot_number[None, :, :] == slot_index[:, None, None]
    select = jnp.any(matches, axis=2).astype(jnp.bfloat16)
    slot_share = jnp.sum(jnp.where(matches, shares[None, :, :], 0.0), axis=(1, 2))
    send_inputs = jnp.dot(select, normed, preferred_element_type=jnp.float32).astype(jnp.bfloat16)
    send_inputs = send_inputs.reshape(experts, capacity, model_width)
    copied_grads = jnp.dot(select, upstream_rows, preferred_element_type=jnp.float32)
    send_grads = (
        (copied_grads * slot_share[:, None])
        .astype(jnp.bfloat16)
        .reshape(experts, capacity, model_width)
    )
    got_inputs, got_grads = (
        lax.all_to_all(send_inputs, "expert", split_axis=0, concat_axis=0, tiled=True),
        lax.all_to_all(send_grads, "expert", split_axis=0, concat_axis=0, tiled=True),
    )
    slot_count = got_inputs.shape[1]
    result_rows = expert_backward(
        got_inputs.reshape(-1, model_width),
        got_grads.reshape(-1, model_width),
        gate_w,
        up_w,
        down_w,
    )
    returned = lax.all_to_all(
        result_rows.reshape(experts, slot_count, model_width),
        "expert",
        split_axis=0,
        concat_axis=0,
        tiled=True,
    )
    normed_grad = lax.dot_general(
        select,
        returned.reshape(experts * capacity, model_width),
        (((0,), (0,)), ((), ())),
        preferred_element_type=jnp.float32,
    )
    scaled = normed_grad * gain_row[None, :]
    layer_grad = upstream_rows.astype(jnp.float32) + inv_root * (
        scaled - unit_rows * jnp.mean(scaled * unit_rows, axis=1, keepdims=True)
    )
    layer_grad = layer_grad.astype(jnp.bfloat16)
    passed = shifted(layer_grad, "section", -1)
    return passed[None]


tile = 256
in_vmem = pl.BlockSpec(memory_space=pltpu.VMEM)
anywhere = pl.BlockSpec(memory_space=pl.ANY)


def tile_cut(step):
    return pl.ds(pl.multiple_of(step * tile, tile), tile)


def shared_kernel(experts, upstream_ref, ids_ref, share_ref, out_ref):
    size, width = upstream_ref.shape
    lanes = out_ref.shape[1] - width
    top = ids_ref.shape[0]
    out_ref[:, :width] = upstream_ref[...]
    both = jnp.concatenate([ids_ref[...].astype(jnp.float32), share_ref[...]], axis=0).T
    lane = lax.broadcasted_iota(jnp.int32, (size, lanes), 1)
    expert = lax.rem(lane, experts).astype(jnp.float32)
    dense = jnp.zeros((size, lanes), jnp.float32)
    for k in range(top):
        hit = expert == both[:, k : k + 1]
        dense = dense + jnp.where(hit, both[:, top + k : top + k + 1], 0.0)
    high = dense.astype(jnp.bfloat16).astype(jnp.float32)
    middle = (dense - high).astype(jnp.bfloat16).astype(jnp.float32)
    low = dense - high - middle
    parts = jnp.where(lane < experts, high, jnp.where(lane < 2 * experts, middle, low))
    out_ref[:, width:] = jnp.where(lane < 3 * experts, parts, 0.0).astype(jnp.bfloat16)


def shared_rows(upstream_rows, routed, shares, experts):
    count, width = upstream_rows.shape
    return pl.pallas_call(
        functools.partial(shared_kernel, experts),
        in_specs=[in_vmem] * 3,
        out_specs=in_vmem,
        out_shape=jax.ShapeDtypeStruct((count, width + 128), jnp.bfloat16),
        compiler_params=pltpu.CompilerParams(vmem_limit_bytes=8 << 20),
    )(upstream_rows, routed, shares)


def factors_kernel(pairs, saved_ref, gain_ref, *refs):
    weight_refs = refs[: 2 * pairs]
    gate_ref, up_ref, rows_ref = refs[-3:]
    value = saved_ref[...].astype(jnp.float32)
    inv_root = lax.rsqrt(jnp.mean(value * value, axis=1, keepdims=True) + epsilon)
    rows_ref[...] = (value * inv_root * gain_ref[...]).astype(jnp.bfloat16)

    def body(step, carry):
        cut = tile_cut(step)
        for w in range(pairs):
            inputs = rows_ref[...]
            pre_gate = jnp.dot(
                inputs, weight_refs[2 * w][:, cut], preferred_element_type=jnp.float32
            )
            pre_up = jnp.dot(
                inputs, weight_refs[2 * w + 1][:, cut], preferred_element_type=jnp.float32
            )
            sigmoid_gate = jax.nn.sigmoid(pre_gate)
            gate_ref[w, :, cut] = pre_up * sigmoid_gate * (1.0 + pre_gate * (1.0 - sigmoid_gate))
            up_ref[w, :, cut] = pre_gate * sigmoid_gate
        return carry

    lax.fori_loop(0, gate_ref.shape[2] // tile, body, 0)


def slot_factors(rows, gain_row, weights, after):
    pairs = len(weights)
    count, width = rows.shape
    hidden = weights[0][0].shape[1]
    flat = [w for gate_w, up_w, _ in weights for w in (gate_w, up_w)]
    shape = jax.ShapeDtypeStruct((pairs, count, hidden), jnp.float32)
    return pl.pallas_call(
        functools.partial(factors_kernel, pairs),
        in_specs=[in_vmem] * (2 + len(flat)) + [anywhere] * len(after),
        out_specs=[in_vmem] * 2,
        out_shape=[shape] * 2,
        scratch_shapes=[pltpu.VMEM((count, width), jnp.bfloat16)],
        cost_estimate=pl.CostEstimate(
            flops=8 * pairs * count * width * hidden,
            bytes_accessed=4 * pairs * width * hidden,
            transcendentals=pairs * count * hidden,
        ),
        compiler_params=pltpu.CompilerParams(vmem_limit_bytes=8 << 20),
    )(rows, gain_row, *flat, *after)


def share_of(rows_ref, width, experts, flip):
    named = lax.axis_index("expert") ^ flip
    parts = rows_ref[:, width:].astype(jnp.float32)
    lane = lax.broadcasted_iota(jnp.int32, parts.shape, 1)
    wanted = (lax.rem(lane, experts) == named) & (lane < 3 * experts)
    return jnp.sum(jnp.where(wanted, parts, 0.0), axis=1, keepdims=True)


def turning_kernel(experts, start, flip, rows_ref, gain_ref, gate_ref, up_ref, *refs):
    weight_refs, refs = refs[:3], refs[3:]
    base_ref = refs[0] if start else None
    out_ref, gate_turned, up_turned, down_turned, gate_grads, up_grads = refs[-6:]
    width = out_ref.shape[1]
    hidden = gate_ref.shape[2]
    share = share_of(rows_ref, width, experts, flip)

    def grads_of(step, carry):
        cut = tile_cut(step)
        turned = weight_refs[2][cut, :].T
        down_turned[:, cut] = turned
        grad = jnp.dot(rows_ref[:, :width], turned, preferred_element_type=jnp.float32)
        grad = grad * share
        gate_grads[:, cut] = (grad * gate_ref[0, :, cut]).astype(jnp.bfloat16)
        up_grads[:, cut] = (grad * up_ref[0, :, cut]).astype(jnp.bfloat16)
        return carry

    lax.fori_loop(0, hidden // tile, grads_of, 0)

    def pieces_of(step, carry):
        cut = tile_cut(step)
        gate_tile = weight_refs[0][cut, :].T
        up_tile = weight_refs[1][cut, :].T
        gate_turned[:, cut] = gate_tile
        up_turned[:, cut] = up_tile
        total = jnp.dot(gate_grads[...], gate_tile, preferred_element_type=jnp.float32)
        total = total + jnp.dot(up_grads[...], up_tile, preferred_element_type=jnp.float32)
        total = total * gain_ref[:, cut]
        if start:
            total = total + base_ref[:, cut]
        out_ref[:, cut] = total.astype(out_ref.dtype)
        return carry

    lax.fori_loop(0, width // tile, pieces_of, 0)


def turning_pieces(flip, rows, gain_row, factors, weights, experts, kind, base):
    _, count, hidden = factors[0].shape
    width = weights[0].shape[0]
    start = [] if base is None else [base]
    turned = jax.ShapeDtypeStruct((hidden, width), jnp.bfloat16)
    down_turned = jax.ShapeDtypeStruct((width, hidden), jnp.bfloat16)
    return pl.pallas_call(
        functools.partial(turning_kernel, experts, len(start), flip),
        in_specs=[in_vmem] * (7 + len(start)),
        out_specs=[in_vmem] * 4,
        out_shape=[jax.ShapeDtypeStruct((count, width), kind), turned, turned, down_turned],
        scratch_shapes=[pltpu.VMEM((count, hidden), jnp.bfloat16)] * 2,
        cost_estimate=pl.CostEstimate(
            flops=12 * count * width * hidden,
            bytes_accessed=6 * width * hidden,
            transcendentals=0,
        ),
        compiler_params=pltpu.CompilerParams(vmem_limit_bytes=12 << 20),
    )(rows, gain_row, *factors, *weights, *start)


def pieces_kernel(experts, pairs, rows_ref, gain_ref, gate_ref, up_ref, *refs):
    weight_refs = refs[: 3 * pairs]
    out_ref, gate_grads, up_grads = refs[-3:]
    width = out_ref.shape[1]
    hidden = gate_ref.shape[2]
    shares = [share_of(rows_ref, width, experts, w) for w in range(pairs)]

    def grads_of(step, carry):
        cut = tile_cut(step)
        for w in range(pairs):
            grad = jnp.dot(
                rows_ref[:, :width],
                weight_refs[3 * w + 2][:, cut],
                preferred_element_type=jnp.float32,
            )
            grad = grad * shares[w]
            gate_grads[w, :, cut] = (grad * gate_ref[w, :, cut]).astype(jnp.bfloat16)
            up_grads[w, :, cut] = (grad * up_ref[w, :, cut]).astype(jnp.bfloat16)
        return carry

    lax.fori_loop(0, hidden // tile, grads_of, 0)

    def pieces_of(step, carry):
        cut = tile_cut(step)
        total = None
        for w in range(pairs):
            for held, weight_ref in ((gate_grads, weight_refs[3 * w]), (up_grads, weight_refs[3 * w + 1])):
                part = jnp.dot(held[w], weight_ref[:, cut], preferred_element_type=jnp.float32)
                total = part if total is None else total + part
        out_ref[:, cut] = (total * gain_ref[:, cut]).astype(out_ref.dtype)
        return carry

    lax.fori_loop(0, width // tile, pieces_of, 0)


def slot_pieces(rows, gain_row, factors, weights, experts, after):
    pairs, count, hidden = factors[0].shape
    width = weights[0][0].shape[1]
    flat = [w for group in weights for w in group]
    return pl.pallas_call(
        functools.partial(pieces_kernel, experts, pairs),
        in_specs=[in_vmem] * (4 + len(flat)) + [anywhere] * len(after),
        out_specs=in_vmem,
        out_shape=jax.ShapeDtypeStruct((count, width), jnp.bfloat16),
        scratch_shapes=[pltpu.VMEM((pairs, count, hidden), jnp.bfloat16)] * 2,
        cost_estimate=pl.CostEstimate(
            flops=12 * pairs * count * width * hidden,
            bytes_accessed=6 * pairs * width * hidden,
            transcendentals=0,
        ),
        compiler_params=pltpu.CompilerParams(vmem_limit_bytes=8 << 20),
    )(rows, gain_row, *factors, *flat, *after)


def final_kernel(saved_ref, upstream_ref, *refs):
    out_ref = refs[-1]
    value = saved_ref[...].astype(jnp.float32)
    inv_root = lax.rsqrt(jnp.mean(value * value, axis=1, keepdims=True) + epsilon)
    scaled = refs[0][...].astype(jnp.float32)
    for ref in refs[1:-1]:
        scaled = scaled + ref[...].astype(jnp.float32)
    unit = value * inv_root
    mean = jnp.mean(scaled * unit, axis=1, keepdims=True)
    layer_grad = upstream_ref[...].astype(jnp.float32) + inv_root * (scaled - unit * mean)
    out_ref[...] = layer_grad.astype(jnp.bfloat16)


def finish(saved_rows, upstream_rows, pieces):
    return pl.pallas_call(
        final_kernel,
        in_specs=[in_vmem] * (2 + len(pieces)),
        out_specs=in_vmem,
        out_shape=jax.ShapeDtypeStruct(saved_rows.shape, jnp.bfloat16),
        compiler_params=pltpu.CompilerParams(vmem_limit_bytes=8 << 20),
    )(saved_rows, upstream_rows, *pieces)


def joined_kernel(experts, at_ends, some_ref, *refs):
    out_ref = refs[-1]
    me = lax.axis_index("expert")
    is_end = ((me < 2) | (me >= experts - 2)).astype(jnp.int32)
    total = jnp.where(is_end == at_ends, some_ref[...].astype(jnp.float32), 0.0)
    for ref in refs[:-1]:
        total = total + ref[...].astype(jnp.float32)
    out_ref[...] = total.astype(out_ref.dtype)


def joined(experts, at_ends, some, pieces, kind):
    return pl.pallas_call(
        functools.partial(joined_kernel, experts, at_ends),
        in_specs=[in_vmem] * (1 + len(pieces)),
        out_specs=in_vmem,
        out_shape=jax.ShapeDtypeStruct(some.shape, kind),
        compiler_params=pltpu.CompilerParams(vmem_limit_bytes=8 << 20),
    )(some, *pieces)


def line_device(
    saved_input, upstream, norm_gain, gate_weight, up_weight, down_weight, expert_ids, gate_share
):
    own = (gate_weight[0, 0], up_weight[0, 0], down_weight[0, 0])
    saved_rows, upstream_rows = saved_input[0], upstream[0]
    experts = lax.axis_size("expert")
    sections = lax.axis_size("section")

    def hop(by):
        return lambda value: lax.ppermute(value, "expert", [(i, i ^ by) for i in range(experts)])

    def handed(by):
        pairs = [
            (s * experts + i, (s - 1) % sections * experts + (i ^ by))
            for s in range(sections)
            for i in range(experts)
        ]
        return lambda value: lax.ppermute(value, ("section", "expert"), pairs)

    shared = shared_rows(upstream_rows, expert_ids[0].T, gate_share[0].T, experts)
    x_two, x_one = hop(4)(saved_rows), hop(2)(saved_rows)
    gate_other, up_other = hop(1)(own[0]), hop(1)(own[1])
    u_two = hop(4)(shared)
    gain = norm_gain
    ends = (0, 1, experts - 2, experts - 1)

    def second_hop(value):
        pairs = []
        for s in range(sections):
            for i in range(experts):
                target = (s, i ^ 2) if i in ends else ((s - 1) % sections, i ^ 4)
                pairs.append((s * experts + i, target[0] * experts + target[1]))
        return lax.ppermute(value, ("section", "expert"), pairs)

    own_factors = slot_factors(saved_rows, gain, (own,), [])
    later, gate = lax.optimization_barrier((shared, own_factors[0]))
    own_factors = (gate, own_factors[1])
    other = (gate_other, up_other, hop(1)(own[2]))
    u_one = hop(2)(later)
    other_factors = slot_factors(saved_rows, gain, (other,), [gate])
    saved_later, upstream_later, gate = lax.optimization_barrier(
        (saved_rows, upstream_rows, other_factors[0])
    )
    other_factors = (gate, other_factors[1])
    next_saved, next_upstream = handed(0)(saved_later), handed(0)(upstream_later)
    both = (own, other)
    here, *own_turned = turning_pieces(
        0, shared, gain, own_factors, own, experts, jnp.float32, None
    )
    here, *other_turned = turning_pieces(
        1, shared, gain, other_factors, other, experts, jnp.bfloat16, here
    )
    turned = (own_turned, other_turned)
    x_three = hop(2)(x_two)
    two_factors = slot_factors(x_two, gain, both, [here])
    one_factors = slot_factors(x_one, gain, both, [two_factors[0]])
    u_two, one_gate = lax.optimization_barrier((u_two, one_factors[0]))
    one_factors = (one_gate, one_factors[1])
    u_three = hop(2)(u_two)
    two = slot_pieces(u_two, gain, two_factors, turned, experts, [next_saved, next_upstream])
    two_next = second_hop(two)
    three_factors = slot_factors(x_three, gain, both, [two])
    here_later, three_gate = lax.optimization_barrier((here, three_factors[0]))
    three_factors = (three_gate, three_factors[1])
    here_next = handed(0)(here_later)
    one = slot_pieces(u_one, gain, one_factors, turned, experts, [three_factors[0]])
    one_next = handed(2)(one)
    three = slot_pieces(u_three, gain, three_factors, turned, experts, [one, here_next])
    three = joined(experts, 0, two_next, [three], jnp.bfloat16)
    summed = joined(experts, 1, two_next, [here_next, one_next], jnp.float32)
    three_next = handed(6)(three)
    return finish(next_saved, next_upstream, [summed, three_next])[None]


def solution(mesh):
    placed = (
        P("section", "expert", None),
        P("section", "expert", None),
        P("section", None),
        P("section", "expert", None, None),
        P("section", "expert", None, None),
        P("section", "expert", None, None),
        P("section", "expert", None),
        P("section", "expert", None),
    )
    plan = line_device if mesh.shape["expert"] == 8 else routed_device
    return jax.shard_map(
        plan,
        mesh=mesh,
        in_specs=placed,
        out_specs=P("section", "expert", None),
        check_vma=False,
    )
```

```python
import functools
import jax
import jax.numpy as jnp
from jax import lax
from jax.experimental import pallas as pl
from jax.experimental.pallas import tpu as pltpu
from jax.sharding import PartitionSpec as P

epsilon = 1e-06


def shifted(value, axis, by):
    length = lax.axis_size(axis)
    return lax.ppermute(value, axis, [(i, (i + by) % length) for i in range(length)])


def slot_ranks(flat_ids, experts):
    pairs = flat_ids.shape[0]
    onehot = (flat_ids[:, None] == jnp.arange(experts, dtype=jnp.int32)[None, :]).astype(
        jnp.bfloat16
    )
    row_index = jnp.arange(pairs, dtype=jnp.int32)
    lower = (row_index[None, :] < row_index[:, None]).astype(jnp.bfloat16)
    before = jnp.dot(lower, onehot, preferred_element_type=jnp.float32)
    ranks = jnp.sum(before * onehot.astype(jnp.float32), axis=1)
    return ranks.astype(jnp.int32)


def expert_backward(inputs, grads, gate_w, up_w, down_w):
    pre_gate = jnp.dot(inputs, gate_w, preferred_element_type=jnp.float32)
    pre_up = jnp.dot(inputs, up_w, preferred_element_type=jnp.float32)
    sigmoid_gate = jax.nn.sigmoid(pre_gate)
    hidden_grad = lax.dot_general(
        grads, down_w, (((1,), (1,)), ((), ())), preferred_element_type=jnp.float32
    )
    d_gate = (hidden_grad * pre_up * sigmoid_gate * (1.0 + pre_gate * (1.0 - sigmoid_gate))).astype(
        jnp.bfloat16
    )
    d_up = (hidden_grad * pre_gate * sigmoid_gate).astype(jnp.bfloat16)
    summed = lax.dot_general(
        d_gate, gate_w, (((1,), (1,)), ((), ())), preferred_element_type=jnp.float32
    )
    summed = summed + lax.dot_general(
        d_up, up_w, (((1,), (1,)), ((), ())), preferred_element_type=jnp.float32
    )
    return summed.astype(jnp.bfloat16)


def routed_device(
    saved_input, upstream, norm_gain, gate_weight, up_weight, down_weight, expert_ids, gate_share
):
    saved_rows = saved_input[0]
    upstream_rows = upstream[0]
    gain_row = norm_gain[0]
    gate_w = gate_weight[0, 0]
    up_w = up_weight[0, 0]
    down_w = down_weight[0, 0]
    routed = expert_ids[0]
    shares = gate_share[0]
    tok_rows, top_count = routed.shape
    model_width = saved_rows.shape[1]
    experts = lax.axis_size("expert")
    capacity = max(2, 3 * tok_rows * top_count // (2 * experts))
    inputs_f = saved_rows.astype(jnp.float32)
    inv_root = lax.rsqrt(jnp.mean(inputs_f * inputs_f, axis=1, keepdims=True) + epsilon)
    unit_rows = inputs_f * inv_root
    normed = (unit_rows * gain_row[None, :]).astype(jnp.bfloat16)
    flat_ids = routed.reshape(-1)
    slot_rank = slot_ranks(flat_ids, experts)
    slot_number = (flat_ids * capacity + slot_rank).reshape(tok_rows, top_count)
    slot_index = jnp.arange(experts * capacity, dtype=jnp.int32)
    matches = slot_number[None, :, :] == slot_index[:, None, None]
    select = jnp.any(matches, axis=2).astype(jnp.bfloat16)
    slot_share = jnp.sum(jnp.where(matches, shares[None, :, :], 0.0), axis=(1, 2))
    send_inputs = jnp.dot(select, normed, preferred_element_type=jnp.float32).astype(jnp.bfloat16)
    send_inputs = send_inputs.reshape(experts, capacity, model_width)
    copied_grads = jnp.dot(select, upstream_rows, preferred_element_type=jnp.float32)
    send_grads = (
        (copied_grads * slot_share[:, None])
        .astype(jnp.bfloat16)
        .reshape(experts, capacity, model_width)
    )
    got_inputs, got_grads = (
        lax.all_to_all(send_inputs, "expert", split_axis=0, concat_axis=0, tiled=True),
        lax.all_to_all(send_grads, "expert", split_axis=0, concat_axis=0, tiled=True),
    )
    slot_count = got_inputs.shape[1]
    result_rows = expert_backward(
        got_inputs.reshape(-1, model_width),
        got_grads.reshape(-1, model_width),
        gate_w,
        up_w,
        down_w,
    )
    returned = lax.all_to_all(
        result_rows.reshape(experts, slot_count, model_width),
        "expert",
        split_axis=0,
        concat_axis=0,
        tiled=True,
    )
    normed_grad = lax.dot_general(
        select,
        returned.reshape(experts * capacity, model_width),
        (((0,), (0,)), ((), ())),
        preferred_element_type=jnp.float32,
    )
    scaled = normed_grad * gain_row[None, :]
    layer_grad = upstream_rows.astype(jnp.float32) + inv_root * (
        scaled - unit_rows * jnp.mean(scaled * unit_rows, axis=1, keepdims=True)
    )
    layer_grad = layer_grad.astype(jnp.bfloat16)
    passed = shifted(layer_grad, "section", -1)
    return passed[None]


tile = 256
in_vmem = pl.BlockSpec(memory_space=pltpu.VMEM)
anywhere = pl.BlockSpec(memory_space=pl.ANY)


def tile_cut(step):
    return pl.ds(pl.multiple_of(step * tile, tile), tile)


def shared_kernel(experts, upstream_ref, ids_ref, share_ref, out_ref):
    size, width = upstream_ref.shape
    lanes = out_ref.shape[1] - width
    top = ids_ref.shape[0]
    out_ref[:, :width] = upstream_ref[...]
    both = jnp.concatenate([ids_ref[...].astype(jnp.float32), share_ref[...]], axis=0).T
    lane = lax.broadcasted_iota(jnp.int32, (size, lanes), 1)
    expert = lax.rem(lane, experts).astype(jnp.float32)
    dense = jnp.zeros((size, lanes), jnp.float32)
    for k in range(top):
        hit = expert == both[:, k : k + 1]
        dense = dense + jnp.where(hit, both[:, top + k : top + k + 1], 0.0)
    high = dense.astype(jnp.bfloat16).astype(jnp.float32)
    middle = (dense - high).astype(jnp.bfloat16).astype(jnp.float32)
    low = dense - high - middle
    parts = jnp.where(lane < experts, high, jnp.where(lane < 2 * experts, middle, low))
    out_ref[:, width:] = jnp.where(lane < 3 * experts, parts, 0.0).astype(jnp.bfloat16)


def shared_rows(upstream_rows, routed, shares, experts):
    count, width = upstream_rows.shape
    return pl.pallas_call(
        functools.partial(shared_kernel, experts),
        in_specs=[in_vmem] * 3,
        out_specs=in_vmem,
        out_shape=jax.ShapeDtypeStruct((count, width + 128), jnp.bfloat16),
        compiler_params=pltpu.CompilerParams(vmem_limit_bytes=8 << 20),
    )(upstream_rows, routed, shares)


def factors_kernel(pairs, saved_ref, gain_ref, *refs):
    weight_refs = refs[: 2 * pairs]
    gate_ref, up_ref, rows_ref = refs[-3:]
    value = saved_ref[...].astype(jnp.float32)
    inv_root = lax.rsqrt(jnp.mean(value * value, axis=1, keepdims=True) + epsilon)
    rows_ref[...] = (value * inv_root * gain_ref[...]).astype(jnp.bfloat16)

    def body(step, carry):
        cut = tile_cut(step)
        for w in range(pairs):
            inputs = rows_ref[...]
            pre_gate = jnp.dot(
                inputs, weight_refs[2 * w][:, cut], preferred_element_type=jnp.float32
            )
            pre_up = jnp.dot(
                inputs, weight_refs[2 * w + 1][:, cut], preferred_element_type=jnp.float32
            )
            sigmoid_gate = jax.nn.sigmoid(pre_gate)
            gate_ref[w, :, cut] = pre_up * sigmoid_gate * (1.0 + pre_gate * (1.0 - sigmoid_gate))
            up_ref[w, :, cut] = pre_gate * sigmoid_gate
        return carry

    lax.fori_loop(0, gate_ref.shape[2] // tile, body, 0)


def slot_factors(rows, gain_row, weights, after):
    pairs = len(weights)
    count, width = rows.shape
    hidden = weights[0][0].shape[1]
    flat = [w for gate_w, up_w, _ in weights for w in (gate_w, up_w)]
    shape = jax.ShapeDtypeStruct((pairs, count, hidden), jnp.float32)
    return pl.pallas_call(
        functools.partial(factors_kernel, pairs),
        in_specs=[in_vmem] * (2 + len(flat)) + [anywhere] * len(after),
        out_specs=[in_vmem] * 2,
        out_shape=[shape] * 2,
        scratch_shapes=[pltpu.VMEM((count, width), jnp.bfloat16)],
        cost_estimate=pl.CostEstimate(
            flops=8 * pairs * count * width * hidden,
            bytes_accessed=4 * pairs * width * hidden,
            transcendentals=pairs * count * hidden,
        ),
        compiler_params=pltpu.CompilerParams(vmem_limit_bytes=8 << 20),
    )(rows, gain_row, *flat, *after)


def share_of(rows_ref, width, experts, flip):
    named = lax.axis_index("expert") ^ flip
    parts = rows_ref[:, width:].astype(jnp.float32)
    lane = lax.broadcasted_iota(jnp.int32, parts.shape, 1)
    wanted = (lax.rem(lane, experts) == named) & (lane < 3 * experts)
    return jnp.sum(jnp.where(wanted, parts, 0.0), axis=1, keepdims=True)


def turning_kernel(experts, start, flip, rows_ref, gain_ref, gate_ref, up_ref, *refs):
    weight_refs, refs = refs[:3], refs[3:]
    base_ref = refs[0] if start else None
    out_ref, gate_turned, up_turned, down_turned, gate_grads, up_grads = refs[-6:]
    width = out_ref.shape[1]
    hidden = gate_ref.shape[2]
    share = share_of(rows_ref, width, experts, flip)

    def grads_of(step, carry):
        cut = tile_cut(step)
        turned = weight_refs[2][cut, :].T
        down_turned[:, cut] = turned
        grad = jnp.dot(rows_ref[:, :width], turned, preferred_element_type=jnp.float32)
        grad = grad * share
        gate_grads[:, cut] = (grad * gate_ref[0, :, cut]).astype(jnp.bfloat16)
        up_grads[:, cut] = (grad * up_ref[0, :, cut]).astype(jnp.bfloat16)
        return carry

    lax.fori_loop(0, hidden // tile, grads_of, 0)

    def pieces_of(step, carry):
        cut = tile_cut(step)
        gate_tile = weight_refs[0][cut, :].T
        up_tile = weight_refs[1][cut, :].T
        gate_turned[:, cut] = gate_tile
        up_turned[:, cut] = up_tile
        total = jnp.dot(gate_grads[...], gate_tile, preferred_element_type=jnp.float32)
        total = total + jnp.dot(up_grads[...], up_tile, preferred_element_type=jnp.float32)
        total = total * gain_ref[:, cut]
        if start:
            total = total + base_ref[:, cut]
        out_ref[:, cut] = total.astype(out_ref.dtype)
        return carry

    lax.fori_loop(0, width // tile, pieces_of, 0)


def turning_pieces(flip, rows, gain_row, factors, weights, experts, kind, base):
    _, count, hidden = factors[0].shape
    width = weights[0].shape[0]
    start = [] if base is None else [base]
    turned = jax.ShapeDtypeStruct((hidden, width), jnp.bfloat16)
    down_turned = jax.ShapeDtypeStruct((width, hidden), jnp.bfloat16)
    return pl.pallas_call(
        functools.partial(turning_kernel, experts, len(start), flip),
        in_specs=[in_vmem] * (7 + len(start)),
        out_specs=[in_vmem] * 4,
        out_shape=[jax.ShapeDtypeStruct((count, width), kind), turned, turned, down_turned],
        scratch_shapes=[pltpu.VMEM((count, hidden), jnp.bfloat16)] * 2,
        cost_estimate=pl.CostEstimate(
            flops=12 * count * width * hidden,
            bytes_accessed=6 * width * hidden,
            transcendentals=0,
        ),
        compiler_params=pltpu.CompilerParams(vmem_limit_bytes=12 << 20),
    )(rows, gain_row, *factors, *weights, *start)


def pieces_kernel(experts, pairs, rows_ref, gain_ref, gate_ref, up_ref, *refs):
    weight_refs = refs[: 3 * pairs]
    out_ref, gate_grads, up_grads = refs[-3:]
    width = out_ref.shape[1]
    hidden = gate_ref.shape[2]
    shares = [share_of(rows_ref, width, experts, w) for w in range(pairs)]

    def grads_of(step, carry):
        cut = tile_cut(step)
        for w in range(pairs):
            grad = jnp.dot(
                rows_ref[:, :width],
                weight_refs[3 * w + 2][:, cut],
                preferred_element_type=jnp.float32,
            )
            grad = grad * shares[w]
            gate_grads[w, :, cut] = (grad * gate_ref[w, :, cut]).astype(jnp.bfloat16)
            up_grads[w, :, cut] = (grad * up_ref[w, :, cut]).astype(jnp.bfloat16)
        return carry

    lax.fori_loop(0, hidden // tile, grads_of, 0)

    def pieces_of(step, carry):
        cut = tile_cut(step)
        total = None
        for w in range(pairs):
            for held, weight_ref in ((gate_grads, weight_refs[3 * w]), (up_grads, weight_refs[3 * w + 1])):
                part = jnp.dot(held[w], weight_ref[:, cut], preferred_element_type=jnp.float32)
                total = part if total is None else total + part
        out_ref[:, cut] = (total * gain_ref[:, cut]).astype(out_ref.dtype)
        return carry

    lax.fori_loop(0, width // tile, pieces_of, 0)


def slot_pieces(rows, gain_row, factors, weights, experts, after):
    pairs, count, hidden = factors[0].shape
    width = weights[0][0].shape[1]
    flat = [w for group in weights for w in group]
    return pl.pallas_call(
        functools.partial(pieces_kernel, experts, pairs),
        in_specs=[in_vmem] * (4 + len(flat)) + [anywhere] * len(after),
        out_specs=in_vmem,
        out_shape=jax.ShapeDtypeStruct((count, width), jnp.bfloat16),
        scratch_shapes=[pltpu.VMEM((pairs, count, hidden), jnp.bfloat16)] * 2,
        cost_estimate=pl.CostEstimate(
            flops=12 * pairs * count * width * hidden,
            bytes_accessed=6 * pairs * width * hidden,
            transcendentals=0,
        ),
        compiler_params=pltpu.CompilerParams(vmem_limit_bytes=8 << 20),
    )(rows, gain_row, *factors, *flat, *after)


def final_kernel(saved_ref, upstream_ref, *refs):
    out_ref = refs[-1]
    value = saved_ref[...].astype(jnp.float32)
    inv_root = lax.rsqrt(jnp.mean(value * value, axis=1, keepdims=True) + epsilon)
    scaled = refs[0][...].astype(jnp.float32)
    for ref in refs[1:-1]:
        scaled = scaled + ref[...].astype(jnp.float32)
    unit = value * inv_root
    mean = jnp.mean(scaled * unit, axis=1, keepdims=True)
    layer_grad = upstream_ref[...].astype(jnp.float32) + inv_root * (scaled - unit * mean)
    out_ref[...] = layer_grad.astype(jnp.bfloat16)


def finish(saved_rows, upstream_rows, pieces):
    return pl.pallas_call(
        final_kernel,
        in_specs=[in_vmem] * (2 + len(pieces)),
        out_specs=in_vmem,
        out_shape=jax.ShapeDtypeStruct(saved_rows.shape, jnp.bfloat16),
        compiler_params=pltpu.CompilerParams(vmem_limit_bytes=8 << 20),
    )(saved_rows, upstream_rows, *pieces)


def joined_kernel(experts, at_ends, some_ref, *refs):
    out_ref = refs[-1]
    me = lax.axis_index("expert")
    is_end = ((me < 2) | (me >= experts - 2)).astype(jnp.int32)
    total = jnp.where(is_end == at_ends, some_ref[...].astype(jnp.float32), 0.0)
    for ref in refs[:-1]:
        total = total + ref[...].astype(jnp.float32)
    out_ref[...] = total.astype(out_ref.dtype)


def joined(experts, at_ends, some, pieces, kind):
    return pl.pallas_call(
        functools.partial(joined_kernel, experts, at_ends),
        in_specs=[in_vmem] * (1 + len(pieces)),
        out_specs=in_vmem,
        out_shape=jax.ShapeDtypeStruct(some.shape, kind),
        compiler_params=pltpu.CompilerParams(vmem_limit_bytes=8 << 20),
    )(some, *pieces)


def line_device(
    saved_input, upstream, norm_gain, gate_weight, up_weight, down_weight, expert_ids, gate_share
):
    own = (gate_weight[0, 0], up_weight[0, 0], down_weight[0, 0])
    saved_rows, upstream_rows = saved_input[0], upstream[0]
    experts = lax.axis_size("expert")
    sections = lax.axis_size("section")

    def hop(by):
        return lambda value: lax.ppermute(value, "expert", [(i, i ^ by) for i in range(experts)])

    def handed(by):
        pairs = [
            (s * experts + i, (s - 1) % sections * experts + (i ^ by))
            for s in range(sections)
            for i in range(experts)
        ]
        return lambda value: lax.ppermute(value, ("section", "expert"), pairs)

    shared = shared_rows(upstream_rows, expert_ids[0].T, gate_share[0].T, experts)
    x_two, x_one = hop(4)(saved_rows), hop(2)(saved_rows)
    gate_other, up_other = hop(1)(own[0]), hop(1)(own[1])
    u_two = hop(4)(shared)
    gain = norm_gain
    ends = (0, 1, experts - 2, experts - 1)

    def second_hop(value):
        pairs = []
        for s in range(sections):
            for i in range(experts):
                target = (s, i ^ 2) if i in ends else ((s - 1) % sections, i ^ 4)
                pairs.append((s * experts + i, target[0] * experts + target[1]))
        return lax.ppermute(value, ("section", "expert"), pairs)

    own_factors = slot_factors(saved_rows, gain, (own,), [])
    later, gate = lax.optimization_barrier((shared, own_factors[0]))
    own_factors = (gate, own_factors[1])
    other = (gate_other, up_other, hop(1)(own[2]))
    u_one = hop(2)(later)
    other_factors = slot_factors(saved_rows, gain, (other,), [gate])
    saved_later, upstream_later, gate = lax.optimization_barrier(
        (saved_rows, upstream_rows, other_factors[0])
    )
    other_factors = (gate, other_factors[1])
    next_saved, next_upstream = handed(0)(saved_later), handed(0)(upstream_later)
    both = (own, other)
    here, *own_turned = turning_pieces(
        0, shared, gain, own_factors, own, experts, jnp.float32, None
    )
    here, *other_turned = turning_pieces(
        1, shared, gain, other_factors, other, experts, jnp.bfloat16, here
    )
    turned = (own_turned, other_turned)
    x_three = hop(2)(x_two)
    two_factors = slot_factors(x_two, gain, both, [here])
    one_factors = slot_factors(x_one, gain, both, [two_factors[0]])
    three_factors = slot_factors(x_three, gain, both, [one_factors[0]])
    u_two, three_gate = lax.optimization_barrier((u_two, three_factors[0]))
    three_factors = (three_gate, three_factors[1])
    here_next = handed(0)(here)
    u_three = hop(2)(u_two)
    two = slot_pieces(u_two, gain, two_factors, turned, experts, [next_saved, next_upstream])
    two_next = second_hop(two)
    one = slot_pieces(u_one, gain, one_factors, turned, experts, [two])
    one_next = handed(2)(one)
    three = slot_pieces(u_three, gain, three_factors, turned, experts, [one])
    three = joined(experts, 0, two_next, [three], jnp.bfloat16)
    summed = joined(experts, 1, two_next, [here_next, one_next], jnp.float32)
    three_next = handed(6)(three)
    return finish(next_saved, next_upstream, [summed, three_next])[None]


def solution(mesh):
    placed = (
        P("section", "expert", None),
        P("section", "expert", None),
        P("section", None),
        P("section", "expert", None, None),
        P("section", "expert", None, None),
        P("section", "expert", None, None),
        P("section", "expert", None),
        P("section", "expert", None),
    )
    plan = line_device if mesh.shape["expert"] == 8 else routed_device
    return jax.shard_map(
        plan,
        mesh=mesh,
        in_specs=placed,
        out_specs=P("section", "expert", None),
        check_vma=False,
    )
```
